32 devices in a mesh: cells: 8 (over z, y), states: 4 (over x, core).
Axes of the slice: x: 2, y: 2, z: 4, core: 2. Of those that a mesh axis runs over, the one named last changes fastest.
Arguments:
- filter_input: bfloat16 [5096, 512], P('cells', 'states'), may hold values from -4 to 4, as said below
- cell_table: bfloat16 [8, 343, 343], replicated, may hold values from -0.5 to 3.5, as said below
- cell_type: int32 [16], P('cells'), may hold values from 0 to 7
- atom_center: int32 [32], P('cells'), may hold values from 0 to 1, as said below
- proj_values: bfloat16 [32, 3, 16, 343], P('cells'), may hold values from -0.3125 to 0.3125
- coupling: float32 [16, 16], replicated, may hold values from -1.5 to 1.5
- occupation: float32 [512], P('states'), may hold values from 0.25 to 4
Outputs:
- filtered: float32 [5096, 512], P('cells', 'states')
- density: float32 [5096], P('cells')
The draws below stay inside these ranges and needn't reach their ends.
Inputs may be any that keep to these rules, and one draw needn't show every extreme that they name: `filter_input`: rows that stand for the same node on two blocks hold the same values. `cell_table`: each of the 8 matrices is symmetric. `atom_center`: in each block of 4 atoms of one owner, at least one atom sits on cell 0 and at least one on cell 1.
All inputs are finite; a program needn't handle non-finite values.
Results may differ from the reference program's by a relative error of at most 0.0027.
Values may be sent and summed in bfloat16 or wider, within the bound.
No kernel may reach another device: no remote copies, remote signals or barrier semaphores. Data moves between devices by JAX's collectives and lax.ppermute only.
A program may use at most 64 MiB of HBM per device.

```python
import math
import jax
import jax.numpy as jnp
from jax import lax

CELL_DEV = 2
STATE_DEV = 128
NTYPE = 8
ATOM_DEV = 4
PROJECTORS = 16
STEPS = 3
FACE = 49
CELL_NODES = 343
STRIDE = 294
NODE_DEV = 637
CELLS = 16
NODES = 5096
STATES = 512
ATOMS = 32
N_CELLS = 8
N_STATES = 4


def draw_filter_input(key, part):
    total_rows = N_CELLS * CELL_DEV * STRIDE
    values = jnp.clip(jax.random.normal(key, (total_rows, STATES), jnp.float32), -4.0, 4.0)
    blocks = values.reshape(N_CELLS, CELL_DEV * STRIDE, STATES)
    following = jnp.roll(blocks, -1, axis=0)[:, :FACE]
    return jnp.concatenate([blocks, following], axis=1).reshape(NODES, STATES).astype(jnp.bfloat16)


def draw_cell_table(key, part):
    first, second = jax.random.split(key)
    shape = (NTYPE, CELL_NODES, CELL_NODES)
    noise = jnp.clip(jax.random.normal(first, shape, jnp.float32), -5.0, 5.0)
    symmetric = (noise + jnp.swapaxes(noise, 1, 2)) * (0.5 / math.sqrt(CELL_NODES))
    diagonal = jax.random.uniform(second, (NTYPE, CELL_NODES), jnp.float32, 1.0, 3.0)
    eye = jnp.eye(CELL_NODES, dtype=jnp.float32)
    table = symmetric * (1.0 - eye)[None] + diagonal[:, :, None] * eye[None]
    return table.astype(jnp.bfloat16)


def draw_atom_center(key, part):
    first, second = jax.random.split(jax.random.fold_in(key, 17))
    base = jax.random.randint(first, (N_CELLS, ATOM_DEV), 0, CELL_DEV, dtype=jnp.int32)
    slot_keys = jax.random.split(second, N_CELLS)
    slots = jax.vmap(lambda k: jax.random.permutation(k, ATOM_DEV))(slot_keys).astype(jnp.int32)
    centers = jnp.where(slots == 0, 0, jnp.where(slots == 1, CELL_DEV - 1, base))
    return centers.reshape(ATOMS).astype(jnp.int32)


def with_ends(entries, stream_key, least, top_value):
    longest = entries.shape.index(max(entries.shape))
    spots = []
    for shift in (0, 1):
        where = [jax.random.randint(jax.random.fold_in(stream_key, axis), (), 0, length) for axis, length in enumerate(entries.shape)]
        where[longest] = (where[longest] + shift) % entries.shape[longest]
        spots.append(tuple(where))
    return entries.at[spots[0]].set(least).at[spots[1]].set(top_value)


def steps_of(rng, extent, pieces, smallest, largest):
    loudness = 1.0
    for dim, blocks in pieces:
        draws = jax.random.uniform(jax.random.fold_in(jax.random.fold_in(rng, 6), dim), (blocks,), jnp.float32, smallest / len(pieces), largest / len(pieces))
        loudness = loudness * jnp.repeat(jnp.exp(draws), extent[dim] // blocks).reshape((-1,) + (1,) * (len(extent) - 1 - dim))
    return loudness


def gaussian(stream_key, extent, scale, most, cuts=(), held_as=jnp.bfloat16):
    entries = scale * jax.random.normal(stream_key, extent, jnp.float32)
    if cuts:
        entries = entries * steps_of(stream_key, extent, cuts, -0.22, 0.18)
    return jnp.clip(entries, -most, most).astype(held_as)


def setup_inputs(seed: int = 0) -> dict:
    key_of = jax.random.split(jax.random.key(seed), 8)
    filter_input = draw_filter_input(jax.random.fold_in(key_of[7], 71), 0)
    cell_table = draw_cell_table(jax.random.fold_in(key_of[7], 71), 0)
    cell_type = with_ends(jax.random.randint(key_of[2], (CELLS,), 0, NTYPE), jax.random.fold_in(key_of[2], 1), 0, NTYPE - 1).astype(jnp.int32)
    atom_center = draw_atom_center(jax.random.fold_in(key_of[7], 71), 0)
    proj_values = gaussian(key_of[4], (ATOMS, 3, PROJECTORS, CELL_NODES), CELL_NODES ** -0.5, 0.3125, ((0, 8),))
    coupling = gaussian(key_of[5], (PROJECTORS, PROJECTORS), PROJECTORS ** -0.5, 1.5, (), jnp.float32)
    occupation = jnp.clip(jnp.exp(math.log(4.0) - 2.7725887 * jax.random.uniform(key_of[6], (STATES,), jnp.float32) ** steps_of(key_of[6], (STATES,), ((0, 4),), -0.2, 0.2)), 0.25, 4.0)
    return {"filter_input": filter_input, "cell_table": cell_table, "cell_type": cell_type, "atom_center": atom_center, "proj_values": proj_values, "coupling": coupling, "occupation": occupation}


lower_edge = 4.0
upper_edge = 12.0
ground_edge = -2.0


def split_cells(node_block):
    tile_count = (node_block.shape[0] - FACE) // STRIDE
    columns = node_block.shape[1]
    head_rows = node_block[: tile_count * STRIDE].reshape(tile_count, STRIDE, columns)
    padded = jnp.pad(node_block, ((0, STRIDE - FACE), (0, 0)))
    face_rows = padded[STRIDE: STRIDE + tile_count * STRIDE].reshape(tile_count, STRIDE, columns)[:, :FACE]
    return jnp.concatenate([head_rows, face_rows], axis=1)


def join_cells(cell_tiles):
    tile_count = cell_tiles.shape[0]
    columns = cell_tiles.shape[2]
    head_rows = cell_tiles[:, :STRIDE].reshape(tile_count * STRIDE, columns)
    tail_rows = jnp.pad(cell_tiles[:, STRIDE:], ((0, 0), (0, STRIDE - FACE), (0, 0))).reshape(tile_count * STRIDE, columns)
    return jnp.pad(head_rows, ((0, FACE), (0, 0))) + jnp.pad(tail_rows, ((STRIDE, 0), (0, 0)))[: tile_count * STRIDE + FACE]


def apply_cycle(current, cell_table, cell_type, atom_center, proj_values, coupling):
    rounded = current.astype(jnp.bfloat16)
    closed = jnp.concatenate([rounded, rounded[:FACE]], axis=0)
    tiles = split_cells(closed).reshape(N_CELLS, CELL_DEV, CELL_NODES, -1)
    types = cell_type.reshape(N_CELLS, CELL_DEV)

    def cell_block(inputs_pair):
        tile_block, type_block = inputs_pair
        matrices = jnp.take(cell_table, type_block, axis=0).astype(jnp.float32)
        return jnp.einsum("cij,cjs->cis", matrices, tile_block.astype(jnp.float32), precision=lax.Precision.HIGHEST)

    cell_terms = lax.map(cell_block, (tiles, types))
    extended = jnp.concatenate([jnp.roll(tiles, 1, axis=0)[:, -1:], tiles, jnp.roll(tiles, -1, axis=0)[:, :1]], axis=1)
    centers = atom_center.reshape(N_CELLS, ATOM_DEV)
    values = proj_values.reshape(N_CELLS, ATOM_DEV, 3, PROJECTORS, CELL_NODES)

    def atom_block(inputs_triple):
        ext_block, center_block, value_block = inputs_triple
        picks = center_block[:, None] + jnp.arange(3, dtype=jnp.int32)[None, :]
        onehot = (picks[:, :, None] == jnp.arange(CELL_DEV + 2, dtype=jnp.int32)[None, None, :]).astype(jnp.float32)
        beta_cells = jnp.einsum("ajk,ajpr->kapr", onehot, value_block.astype(jnp.float32), precision=lax.Precision.HIGHEST)
        beta_cells = beta_cells.reshape(CELL_DEV + 2, ATOM_DEV * PROJECTORS, CELL_NODES)
        coeffs = jnp.einsum("kqr,krs->qs", beta_cells, ext_block.astype(jnp.float32), precision=lax.Precision.HIGHEST)
        weighted = jnp.einsum("pq,aqs->aps", coupling, coeffs.reshape(ATOM_DEV, PROJECTORS, -1), precision=lax.Precision.HIGHEST)
        weighted = weighted.astype(jnp.bfloat16).astype(jnp.float32).reshape(ATOM_DEV * PROJECTORS, -1)
        return jnp.einsum("kqr,qs->krs", beta_cells, weighted, precision=lax.Precision.HIGHEST)

    spread = lax.map(atom_block, (extended, centers, values))
    total = cell_terms + spread[:, 1:-1]
    total = total.at[:, 0].add(jnp.roll(spread[:, -1], 1, axis=0))
    total = total.at[:, -1].add(jnp.roll(spread[:, 0], -1, axis=0))
    opened = join_cells(total.reshape(CELLS, CELL_NODES, -1))
    return opened[:-FACE] + jnp.pad(opened[-FACE:], ((0, CELLS * STRIDE - FACE), (0, 0)))


def filter_block(columns, cell_table, cell_type, atom_center, proj_values, coupling):
    half_width = (upper_edge - lower_edge) / 2.0
    centre = (upper_edge + lower_edge) / 2.0
    scale_now = half_width / (ground_edge - centre)
    twice_inverse = 2.0 / scale_now
    previous = columns.astype(jnp.float32)
    current = (apply_cycle(previous, cell_table, cell_type, atom_center, proj_values, coupling) - centre * previous) * (scale_now / half_width)
    for repeat in range(STEPS - 1):
        scale_next = 1.0 / (twice_inverse - scale_now)
        image = apply_cycle(current, cell_table, cell_type, atom_center, proj_values, coupling)
        upcoming = (image - centre * current) * (2.0 * scale_next / half_width) - (scale_now * scale_next) * previous
        previous, current = current, upcoming
        scale_now = scale_next
    return current


def lay_out(node_rows):
    blocks = node_rows.reshape((N_CELLS, CELL_DEV * STRIDE) + node_rows.shape[1:])
    following = jnp.roll(blocks, -1, axis=0)[:, :FACE]
    return jnp.concatenate([blocks, following], axis=1).reshape((NODES,) + node_rows.shape[1:])


def reference(filter_input, cell_table, cell_type, atom_center, proj_values, coupling, occupation):
    owned = filter_input.reshape(N_CELLS, NODE_DEV, STATES)[:, : CELL_DEV * STRIDE]
    owned = owned.reshape(CELLS * STRIDE, N_STATES, STATE_DEV)
    by_block = jnp.transpose(owned, (1, 0, 2))
    weights = occupation.reshape(N_STATES, STATE_DEV)

    def one_block(inputs_pair):
        columns, occ_block = inputs_pair
        result = filter_block(columns, cell_table, cell_type, atom_center, proj_values, coupling)
        return result, jnp.sum(result * result * occ_block[None, :], axis=1)

    results, partial_density = lax.map(one_block, (by_block, weights))
    filtered_rows = jnp.transpose(results, (1, 0, 2)).reshape(CELLS * STRIDE, STATES)
    density_rows = jnp.sum(partial_density, axis=0) / STATES
    return lay_out(filtered_rows), lay_out(density_rows)
```

```python
import functools

import jax
import jax.numpy as jnp
from jax import lax
from jax.experimental import pallas as pl
from jax.experimental.pallas import tpu as pltpu
from jax.sharding import PartitionSpec as P

STEPS = 3
LANES = 128
ROWS16 = 16

lower_edge = 4.0
upper_edge = 12.0
ground_edge = -2.0

F32 = jnp.float32
BF16 = jnp.bfloat16


def up16(n):
    return -(-n // ROWS16) * ROWS16


def down16(n):
    return n // ROWS16 * ROWS16


class Sizes:
    def __init__(self, node_rows, cells, cell_nodes, atoms, projectors):
        self.rows = node_rows
        self.nodes = cell_nodes
        self.stride = (node_rows - cell_nodes) // (cells - 1)
        self.face = cell_nodes - self.stride
        self.last = node_rows - cell_nodes
        self.end = node_rows - self.face
        self.atoms = atoms
        self.proj = projectors
        self.coef = atoms * projectors
        self.chunks = -(-cell_nodes // LANES)
        self.tail = cell_nodes - (self.chunks - 1) * LANES
        self.shift = self.stride - (self.chunks - 1) * LANES
        self.m_face = self.chunks * self.coef
        self.m_coef = self.m_face + self.coef
        self.m_rows = self.m_coef + self.coef
        self.right_lo, self.right_hi = down16(self.last), up16(self.end)
        self.left_lo, self.left_hi = down16(self.face), up16(cell_nodes)
        self.halo = max(self.right_hi - self.right_lo, self.left_hi - self.left_lo)
        self.first = self.m_rows + self.halo
        self.pad_face = up16(self.face)
        self.l_face = 2 * self.coef
        self.l_term = self.l_face + self.pad_face
        self.later = self.l_term + self.pad_face


def dot(a, b):
    return jnp.dot(a, b, preferred_element_type=F32)


def exact_dot(a, b):
    return jnp.dot(a, b, preferred_element_type=F32, precision=lax.Precision.HIGHEST)


def pack_kernel(z, center, x0, proj, right, left, own0, own1, xs):
    xs[...] = x0[...].astype(F32)
    right[...] = jnp.zeros_like(right)
    left[...] = jnp.zeros_like(left)
    for a in range(z.atoms):
        low = center[a] == 0
        before, here, after = proj[a, 0], proj[a, 1], proj[a, 2]
        none = jnp.zeros_like(before)
        at = slice(a * z.proj, (a + 1) * z.proj)
        on0 = jnp.where(low, here, before)
        on1 = jnp.where(low, after, here)
        own0[at, :] = on0
        own1[at, :] = on1
        reach_left = jnp.where(low, before, none)
        reach_right = jnp.where(low, none, after)
        for k in range(z.chunks):
            width = LANES if k < z.chunks - 1 else z.tail
            cols = slice(k * LANES, k * LANES + width)
            rows = slice(k * z.coef + a * z.proj, k * z.coef + (a + 1) * z.proj)
            right[rows, :width] = reach_right[:, cols]
            left[rows, :width] = reach_left[:, cols]
        rows = slice(z.m_face + a * z.proj, z.m_face + (a + 1) * z.proj)
        right[rows, : z.tail] = on1[:, (z.chunks - 1) * LANES :]
        left[rows, :] = on0[:, :LANES]
    coeffs = dot(own0[...], x0[: z.nodes, :]) + dot(own1[...], xs[z.last :, :].astype(BF16))
    sent = coeffs.astype(BF16)
    right[z.m_coef : z.m_rows, :] = sent
    left[z.m_coef : z.m_rows, :] = sent
    n = z.right_hi - z.right_lo
    right[z.m_rows : z.m_rows + n, :] = x0[z.right_lo : z.right_hi, :]
    n = z.left_hi - z.left_lo
    left[z.m_rows : z.m_rows + n, :] = x0[z.left_lo : z.left_hi, :]


def local_terms(z, cell0, cell1, spread0, spread1, x_ref, weighted, out):
    c = z.coef
    before, own, after = (weighted[i * c : (i + 1) * c] for i in range(3))
    w0 = jnp.concatenate([own, before], axis=0)
    w1 = jnp.concatenate([own, after], axis=0)
    out[: z.nodes, :] = dot(cell0[...], x_ref[: z.nodes, :].astype(BF16)) + dot(spread0[...], w0)
    term1 = dot(cell1[...], x_ref[z.last :, :].astype(BF16)) + dot(spread1[...], w1)
    out[z.last : z.nodes, :] += term1[: z.nodes - z.last]
    out[z.nodes :, :] = term1[z.nodes - z.last :]


def face_scale(z):
    row = lax.broadcasted_iota(jnp.int32, (z.rows, 1), 0)
    return jnp.where((row < z.face) | (row >= z.end), 0.5, 1.0).astype(F32)


def part_coeffs(z, rows0, rows1, face0, face1, part, pad):
    c = z.coef
    pad[0] = jnp.zeros(pad.shape[1:], F32)
    pad[1] = jnp.zeros(pad.shape[1:], F32)
    pad[0, z.shift : z.shift + z.face, :] = part[: z.face, :]
    pad[1, : z.face, :] = part[z.end :, :]
    s0 = dot(rows0[...], part[: z.nodes, :].astype(BF16)) + dot(face0[...], pad[0].astype(BF16))
    s1 = dot(rows1[...], part[z.last :, :].astype(BF16)) + dot(face1[...], pad[1].astype(BF16))
    return s0[c:], s0[:c] + s1[:c], s1[c:]


def fill_messages(z, coeffs, part, right, left, far_right, far_left):
    before, own, after = (s.astype(BF16) for s in coeffs)
    right[: z.coef, :] = own
    left[: z.coef, :] = own
    right[z.coef : 2 * z.coef, :] = after
    left[z.coef : 2 * z.coef, :] = before
    far_right[...] = after
    far_left[...] = before
    right[z.l_face :, :] = jnp.zeros((z.later - z.l_face, right.shape[1]), BF16)
    left[z.l_face :, :] = jnp.zeros((z.later - z.l_face, left.shape[1]), BF16)
    right[z.l_face : z.l_face + z.face, :] = part[z.end :, :].astype(BF16)
    left[z.l_face : z.l_face + z.face, :] = part[: z.face, :].astype(BF16)


def whole_coeffs(z, own_ref, from_left, from_right, far_left, far_right, mix):
    c = z.coef
    l0, l1 = from_left[:c, :].astype(F32), from_left[c : 2 * c, :].astype(F32)
    r0, r1 = from_right[:c, :].astype(F32), from_right[c : 2 * c, :].astype(F32)
    before = own_ref[:c, :] + l0 + far_left[...].astype(F32)
    own = own_ref[c : 2 * c, :] + l1 + r1
    after = own_ref[2 * c :, :] + r0 + far_right[...].astype(F32)
    return exact_dot(mix[...], jnp.concatenate([before, own, after], axis=0)).astype(BF16)


def whole_field(z, part, from_left, from_right, out):
    out[...] = part[...]
    out[: z.face, :] += from_left[z.l_face : z.l_face + z.face, :].astype(F32)
    out[z.end :, :] += from_right[z.l_face : z.l_face + z.face, :].astype(F32)


def first_kernel(
    z, gain,
    x0, own0, own1, mine_right, mine_left, from_left, from_right, cell0, cell1, mix,
    part, coeffs, right, left, far_right, far_left,
    rows0, rows1, spread0, spread1, face0, face1,
    xs, ext, terms, pad,
):
    c, k_last = z.coef, (z.chunks - 1) * LANES
    xs[...] = x0[...].astype(F32)
    rows0[:c, :] = own0[...]
    rows1[:c, :] = own1[...]
    for k in range(z.chunks):
        width = LANES if k < z.chunks - 1 else z.tail
        cols = slice(k * LANES, k * LANES + width)
        rows0[c:, cols] = from_left[k * c : (k + 1) * c, :width]
        rows1[c:, cols] = from_right[k * c : (k + 1) * c, :width]
    spread0[...] = rows0[...].T
    spread1[...] = rows1[...].T
    face0[:c, :] = mine_left[(z.chunks - 1) * c : z.chunks * c, :]
    face0[c:, :] = from_left[z.m_face : z.m_coef, :]
    face1[:c, :] = mine_right[:c, :]
    face1[c:, :] = from_right[z.m_face : z.m_coef, :]
    ext[...] = jnp.zeros_like(ext)
    halo = from_left[z.m_rows :, :].astype(F32)
    skip = z.last - z.right_lo
    ext[0, : z.stride, :] = halo[skip : skip + z.stride]
    ext[0, z.stride : z.nodes, :] = xs[: z.face, :]
    halo = from_right[z.m_rows :, :].astype(F32)
    skip = z.face - z.left_lo
    ext[1, : z.face, :] = xs[z.end :, :]
    ext[1, z.face : z.nodes, :] = halo[skip : skip + z.stride]
    s0 = dot(rows0[...], x0[: z.nodes, :])
    s1 = dot(rows1[...], xs[z.last :, :].astype(BF16))
    own = s0[:c] + s1[:c]
    for k in range(z.chunks):
        cols = slice(k * LANES, (k + 1) * LANES)
        own += dot(mine_left[k * c : (k + 1) * c, :], ext[0, cols, :].astype(BF16))
        own += dot(mine_right[k * c : (k + 1) * c, :], ext[1, cols, :].astype(BF16))
    before = s0[c:] + from_left[z.m_coef : z.m_rows, :].astype(F32)
    after = s1[c:] + from_right[z.m_coef : z.m_rows, :].astype(F32)
    weighted = exact_dot(mix[...], jnp.concatenate([before, own, after], axis=0)).astype(BF16)
    local_terms(z, cell0, cell1, spread0, spread1, xs, weighted, terms)
    centre = (upper_edge + lower_edge) / 2.0
    part[...] = (terms[...] - centre * (face_scale(z) * xs[...])) * gain
    s = part_coeffs(z, rows0, rows1, face0, face1, part, pad)
    for i in range(3):
        coeffs[i * c : (i + 1) * c, :] = s[i]
    fill_messages(z, s, part, right, left, far_right, far_left)
    right[z.l_term : z.l_term + z.face, : z.tail] = (
        cell1[...].astype(F32)[z.stride :, k_last:].astype(BF16)
    )
    left[z.l_term : z.l_term + z.face, :] = cell0[...].astype(F32)[: z.face, :LANES].astype(BF16)


def second_kernel(
    z, gain, back,
    x0, own_part, own_coeffs, from_left, from_right, from_far_left, from_far_right,
    cell0, cell1, mix, rows0, rows1, spread0, spread1, face0, face1,
    part, coeffs, whole, right, left, far_right, far_left,
    terms, pad,
):
    c = z.coef
    weighted = whole_coeffs(
        z, own_coeffs, from_left, from_right, from_far_left, from_far_right, mix
    )
    whole_field(z, own_part, from_left, from_right, whole)
    local_terms(z, cell0, cell1, spread0, spread1, whole, weighted, terms)
    centre = (upper_edge + lower_edge) / 2.0
    scale = face_scale(z)
    part[...] = (terms[...] - centre * (scale * whole[...])) * gain - back * (
        scale * x0[...].astype(F32)
    )
    s = part_coeffs(z, rows0, rows1, face0, face1, part, pad)
    for i in range(3):
        coeffs[i * c : (i + 1) * c, :] = s[i]
    fill_messages(z, s, part, right, left, far_right, far_left)
    last = dot(cell1[...], part[z.last :, :].astype(BF16))
    first = dot(cell0[...], part[: z.nodes, :].astype(BF16))
    right[z.l_term : z.l_term + z.face, :] = last[z.stride :].astype(BF16)
    left[z.l_term : z.l_term + z.face, :] = first[: z.face].astype(BF16)


def third_kernel(
    z, gain, back, share,
    previous, own_part, own_coeffs, from_left, from_right, from_far_left, from_far_right,
    block_left, block_right, cell0, cell1, mix, spread0, spread1, face0, face1, occupation,
    out, density,
    whole, terms, pad,
):
    c = z.coef
    weighted = whole_coeffs(
        z, own_coeffs, from_left, from_right, from_far_left, from_far_right, mix
    )
    whole_field(z, own_part, from_left, from_right, whole)
    local_terms(z, cell0, cell1, spread0, spread1, whole, weighted, terms)
    before, own, after = (weighted[i * c : (i + 1) * c] for i in range(3))
    pad[...] = jnp.zeros_like(pad)
    pad[0, z.shift : z.shift + z.face, :] = own_part[: z.face, :]
    pad[1, : z.face, :] = own_part[z.end :, :]
    faces = slice(z.l_term, z.l_term + z.face)
    term = from_left[faces, :].astype(F32)
    term += dot(block_left[z.l_term :, :], pad[0].astype(BF16))[: z.face]
    term += dot(face0[...].T, jnp.concatenate([own, before], axis=0))[
        z.shift : z.shift + z.face
    ]
    terms[: z.face, :] += term
    term = from_right[faces, :].astype(F32)
    term += dot(block_right[z.l_term :, :], pad[1].astype(BF16))[: z.face]
    term += dot(face1[...].T, jnp.concatenate([own, after], axis=0))[: z.face]
    terms[z.end :, :] += term
    centre = (upper_edge + lower_edge) / 2.0
    result = (terms[...] - centre * whole[...]) * gain - back * previous[...]
    out[...] = result
    density[...] = lax.dot_general(
        occupation[...] * share,
        result * result,
        (((1,), (1,)), ((), ())),
        preferred_element_type=F32,
        precision=lax.Precision.HIGHEST,
    )


def call(kernel, outs, scratch, *args, scalars=0):
    vmem = pl.BlockSpec(memory_space=pltpu.VMEM)
    smem = pl.BlockSpec(memory_space=pltpu.SMEM)
    return pl.pallas_call(
        kernel,
        out_shape=[jax.ShapeDtypeStruct(s, t) for s, t in outs],
        in_specs=[smem] * scalars + [vmem] * (len(args) - scalars),
        out_specs=[vmem] * len(outs),
        scratch_shapes=[pltpu.VMEM(s, t) for s, t in scratch],
        compiler_params=pltpu.CompilerParams(vmem_limit_bytes=32 * 1024 * 1024),
    )(*args)


def body(filter_input, cell_table, cell_type, atom_center, proj_values, coupling, occupation):
    cells = cell_type.shape[0]
    atoms, projectors = proj_values.shape[0], proj_values.shape[2]
    rows, states = filter_input.shape
    z = Sizes(rows, cells, cell_table.shape[1], atoms, projectors)
    c, n = z.coef, z.nodes
    devices = lax.axis_size("cells")
    states_all = states * lax.axis_size("states")

    def shifted(array, by):
        return lax.ppermute(array, "cells", [(i, (i + by) % devices) for i in range(devices)])

    half_width = (upper_edge - lower_edge) / 2.0
    centre = (upper_edge + lower_edge) / 2.0
    scale = half_width / (ground_edge - centre)
    twice_inverse = 2.0 / scale
    gains, backs = [scale / half_width], [0.0]
    for _ in range(STEPS - 1):
        scale_next = 1.0 / (twice_inverse - scale)
        gains.append(2.0 * scale_next / half_width)
        backs.append(scale * scale_next)
        scale = scale_next

    right, left, own0, own1 = call(
        functools.partial(pack_kernel, z),
        [((z.first, states), BF16)] * 2 + [((c, n), BF16)] * 2,
        [((rows, states), F32)],
        atom_center, filter_input, proj_values,
        scalars=1,
    )
    from_left, from_right = shifted(right, 1), shifted(left, -1)

    onehot = (cell_type[:, None] == jnp.arange(cell_table.shape[0])[None, :]).astype(BF16)
    matrices = jnp.einsum("ct,tij->cij", onehot, cell_table, preferred_element_type=F32)
    matrices = matrices.astype(BF16)
    cell0, cell1 = matrices[0], matrices[-1]
    group = jnp.arange(3 * c) // projectors
    mix = jnp.where(
        group[:, None] == group[None, :], jnp.tile(coupling, (3 * atoms, 3 * atoms)), 0.0
    )

    block, field = (rows, states), ((rows, states), F32)
    messages = [((z.later, states), BF16)] * 2 + [((c, states), BF16)] * 2
    pad = ((2, LANES, states), F32)
    part, coeffs, right, left, far_right, far_left, rows0, rows1, spread0, spread1, face0, face1 = (
        call(
            functools.partial(first_kernel, z, gains[0]),
            [field, ((3 * c, states), F32)]
            + messages
            + [((2 * c, n), BF16)] * 2
            + [((n, 2 * c), BF16)] * 2
            + [((2 * c, LANES), BF16)] * 2,
            [field, ((2, z.chunks * LANES, states), F32), field, pad],
            filter_input, own0, own1, right, left, from_left, from_right, cell0, cell1, mix,
        )
    )
    block_left, block_right = shifted(right, 1), shifted(left, -1)
    from_far_left, from_far_right = shifted(far_right, 2), shifted(far_left, -2)
    part, coeffs, whole, right, left, far_right, far_left = call(
        functools.partial(second_kernel, z, gains[1], backs[1]),
        [field, ((3 * c, states), F32), field] + messages,
        [field, pad],
        filter_input, part, coeffs, block_left, block_right, from_far_left, from_far_right,
        cell0, cell1, mix, rows0, rows1, spread0, spread1, face0, face1,
    )
    from_left, from_right = shifted(right, 1), shifted(left, -1)
    from_far_left, from_far_right = shifted(far_right, 2), shifted(far_left, -2)
    filtered, density = call(
        functools.partial(third_kernel, z, gains[2], backs[2], 1.0 / states_all),
        [field, ((1, rows), F32)],
        [field, field, pad],
        whole, part, coeffs, from_left, from_right, from_far_left, from_far_right,
        block_left, block_right, cell0, cell1, mix, spread0, spread1, face0, face1,
        occupation[None, :],
    )
    return filtered, lax.psum(density[0], "states")


def solution(mesh):
    in_specs = (
        P("cells", "states"),
        P(),
        P("cells"),
        P("cells"),
        P("cells", None, None, None),
        P(),
        P("states"),
    )
    out_specs = (P("cells", "states"), P("cells"))
    return jax.shard_map(body, mesh=mesh, in_specs=in_specs, out_specs=out_specs, check_vma=False)
```

```python
import functools

import jax
import jax.numpy as jnp
from jax import lax
from jax.experimental import pallas as pl
from jax.experimental.pallas import tpu as pltpu
from jax.sharding import PartitionSpec as P

STEPS = 3
LANES = 128
ROWS16 = 16

lower_edge = 4.0
upper_edge = 12.0
ground_edge = -2.0

F32 = jnp.float32
BF16 = jnp.bfloat16


def up16(n):
    return -(-n // ROWS16) * ROWS16


def down16(n):
    return n // ROWS16 * ROWS16


class Sizes:
    def __init__(self, node_rows, cells, cell_nodes, atoms, projectors):
        self.rows = node_rows
        self.nodes = cell_nodes
        self.stride = (node_rows - cell_nodes) // (cells - 1)
        self.face = cell_nodes - self.stride
        self.last = node_rows - cell_nodes
        self.end = node_rows - self.face
        self.atoms = atoms
        self.proj = projectors
        self.coef = atoms * projectors
        self.chunks = -(-cell_nodes // LANES)
        self.tail = cell_nodes - (self.chunks - 1) * LANES
        self.shift = self.stride - (self.chunks - 1) * LANES
        self.m_face = self.chunks * self.coef
        self.m_coef = self.m_face + self.coef
        self.m_rows = self.m_coef + self.coef
        self.right_lo, self.right_hi = down16(self.last), up16(self.end)
        self.left_lo, self.left_hi = down16(self.face), up16(cell_nodes)
        self.halo = max(self.right_hi - self.right_lo, self.left_hi - self.left_lo)
        self.first = self.m_rows + self.halo
        self.pad_face = up16(self.face)
        self.span = up16(self.shift + self.face)
        self.l_face = 2 * self.coef
        self.l_term = self.l_face + self.span
        self.later = self.l_term + self.pad_face


def dot(a, b):
    return jnp.dot(a, b, preferred_element_type=F32)


def exact_dot(a, b):
    return jnp.dot(a, b, preferred_element_type=F32, precision=lax.Precision.HIGHEST)


def halves(v):
    high = v.astype(BF16)
    return high, (v - high.astype(F32)).astype(BF16)


def pack_kernel(
    z, center_hbm, x0_hbm, proj_hbm, x0, right, left, own0, own1, coeffs, center, proj, xs, sems
):
    copies = [
        pltpu.make_async_copy(x0_hbm, x0, sems.at[0]),
        pltpu.make_async_copy(center_hbm, center, sems.at[1]),
        pltpu.make_async_copy(proj_hbm, proj, sems.at[2]),
    ]
    for copy in copies:
        copy.start()
    right[...] = jnp.zeros_like(right)
    left[...] = jnp.zeros_like(left)
    copies[0].wait()
    xs[...] = x0[...].astype(F32)
    n = z.right_hi - z.right_lo
    right[z.m_rows : z.m_rows + n, :] = x0[z.right_lo : z.right_hi, :]
    n = z.left_hi - z.left_lo
    left[z.m_rows : z.m_rows + n, :] = x0[z.left_lo : z.left_hi, :]
    copies[1].wait()
    copies[2].wait()
    for a in range(z.atoms):
        low = center[a] == 0
        before, here, after = proj[a, 0], proj[a, 1], proj[a, 2]
        none = jnp.zeros_like(before)
        at = slice(a * z.proj, (a + 1) * z.proj)
        on0 = jnp.where(low, here, before)
        on1 = jnp.where(low, after, here)
        own0[at, :] = on0
        own1[at, :] = on1
        reach_left = jnp.where(low, before, none)
        reach_right = jnp.where(low, none, after)
        for k in range(z.chunks):
            width = LANES if k < z.chunks - 1 else z.tail
            cols = slice(k * LANES, k * LANES + width)
            rows = slice(k * z.coef + a * z.proj, k * z.coef + (a + 1) * z.proj)
            right[rows, :width] = reach_right[:, cols]
            left[rows, :width] = reach_left[:, cols]
        rows = slice(z.m_face + a * z.proj, z.m_face + (a + 1) * z.proj)
        right[rows, : z.tail] = on1[:, (z.chunks - 1) * LANES :]
        left[rows, :] = on0[:, :LANES]
    s = dot(own0[...], x0[: z.nodes, :]) + dot(own1[...], xs[z.last :, :].astype(BF16))
    coeffs[...] = s
    sent = s.astype(BF16)
    right[z.m_coef : z.m_rows, :] = sent
    left[z.m_coef : z.m_rows, :] = sent


def add_cells(z, term0, term1, out):
    out[: z.nodes, :] += term0
    out[z.last :, :] += term1


def face_scale(z):
    row = lax.broadcasted_iota(jnp.int32, (z.rows, 1), 0)
    return jnp.where((row < z.face) | (row >= z.end), 0.5, 1.0).astype(F32)


CENTRE = (upper_edge + lower_edge) / 2.0


def twice(a, b):
    return jnp.concatenate([a, b, a, b], axis=0).astype(BF16)


def send_part(z, rows0, rows1, face0, face1, part, coeffs, right, left, far_right, far_left):
    c = z.coef
    right[z.l_face :, :] = jnp.zeros((z.later - z.l_face, right.shape[1]), BF16)
    left[z.l_face :, :] = jnp.zeros((z.later - z.l_face, left.shape[1]), BF16)
    right[z.l_face : z.l_face + z.face, :] = part[z.end :, :].astype(BF16)
    at = z.l_face + z.shift
    left[at : at + z.face, :] = part[: z.face, :].astype(BF16)
    last = right[z.l_face : z.l_term, :]
    first = left[z.l_face : z.l_term, :]
    s0 = dot(rows0[...], part[: z.nodes, :].astype(BF16)) + dot(face0[:, : z.span], first)
    s1 = dot(rows1[...], part[z.last :, :].astype(BF16)) + dot(face1[:, : z.span], last)
    before, own, after = s0[c:], s0[:c] + s1[:c], s1[c:]
    coeffs[:c, :] = before
    coeffs[c : 2 * c, :] = own
    coeffs[2 * c :, :] = after
    before, own, after = before.astype(BF16), own.astype(BF16), after.astype(BF16)
    right[:c, :] = own
    left[:c, :] = own
    right[c : 2 * c, :] = after
    left[c : 2 * c, :] = before
    far_right[...] = after
    far_left[...] = before


def whole_coeffs(z, own_ref, from_left, from_right, far_left, far_right):
    c = z.coef
    l0, l1 = from_left[:c, :].astype(F32), from_left[c : 2 * c, :].astype(F32)
    r0, r1 = from_right[:c, :].astype(F32), from_right[c : 2 * c, :].astype(F32)
    before = own_ref[:c, :] + l0 + far_left[...].astype(F32)
    own = own_ref[c : 2 * c, :] + l1 + r1
    after = own_ref[2 * c :, :] + r0 + far_right[...].astype(F32)
    return before, own, after


def face_rows(z, from_left, from_right):
    at = z.l_face + z.shift
    return (
        from_left[z.l_face : z.l_face + z.face, :].astype(F32),
        from_right[at : at + z.face, :].astype(F32),
    )


def neighbour_terms(z, s, from_left, from_right, cell0, cell1, spread0, spread1):
    before, own, after = s
    first = from_left[z.l_face : z.l_term, :]
    last = from_right[z.l_face : z.l_term, :]
    k_last = (z.chunks - 1) * LANES
    term0 = dot(spread0[...], twice(own, before)) + dot(cell0[:, : z.span], first)
    term1 = dot(spread1[...], twice(own, after)) + dot(cell1[:, k_last:], last[: z.tail])
    return term0, term1


def beside_first(
    z, coupling, x0, cell0, cell1, base, mix_high, mix_low, end_rows, xs
):
    xs[...] = x0[...].astype(F32)
    base[...] = (-CENTRE) * (face_scale(z) * xs[...])
    add_cells(
        z, dot(cell0[...], x0[: z.nodes, :]), dot(cell1[...], xs[z.last :, :].astype(BF16)), base
    )
    size = 2 * z.coef
    row = lax.broadcasted_iota(jnp.int32, (size, z.proj), 0)
    col = lax.broadcasted_iota(jnp.int32, (size, z.proj), 1)
    pick = jnp.where(lax.rem(row, z.proj) == col, 1.0, 0.0).astype(F32)
    wide = exact_dot(pick, coupling[...])
    wide = lax.dot_general(
        wide, pick, (((1,), (1,)), ((), ())),
        preferred_element_type=F32, precision=lax.Precision.HIGHEST,
    )
    row = lax.broadcasted_iota(jnp.int32, (size, size), 0)
    col = lax.broadcasted_iota(jnp.int32, (size, size), 1)
    mix = jnp.where(lax.div(row, z.proj) == lax.div(col, z.proj), wide, 0.0)
    mix_high[...], mix_low[...] = halves(mix)
    end_rows[...] = jnp.zeros_like(end_rows)
    end_rows[: z.face, :] = cell1[...].astype(F32)[z.stride :].astype(BF16)


def mixed(a, mix_high, mix_low):
    high, low = halves(dot(a, mix_high[...]) + dot(a, mix_low[...]))
    return jnp.concatenate([high, low], axis=1)


def first_kernel(
    z, gain,
    base, x0, own0, own1, own_coeffs, mine_right, mine_left, from_left, from_right,
    cell0, mix_high, mix_low, end_rows,
    part, coeffs, right, left, far_right, far_left,
    rows0, rows1, spread0, spread1, face0, face1,
    xs, ext, terms,
):
    c, k_last = z.coef, (z.chunks - 1) * LANES
    xs[...] = x0[...].astype(F32)
    rows0[:c, :] = own0[...]
    rows1[:c, :] = own1[...]
    for k in range(z.chunks):
        width = LANES if k < z.chunks - 1 else z.tail
        cols = slice(k * LANES, k * LANES + width)
        rows0[c:, cols] = from_left[k * c : (k + 1) * c, :width]
        rows1[c:, cols] = from_right[k * c : (k + 1) * c, :width]
    spread0[...] = mixed(rows0[...].T, mix_high, mix_low)
    spread1[...] = mixed(rows1[...].T, mix_high, mix_low)
    face0[:c, :] = mine_left[(z.chunks - 1) * c : z.chunks * c, :]
    face0[c:, :] = from_left[z.m_face : z.m_coef, :]
    face1[:c, :] = mine_right[:c, :]
    face1[c:, :] = from_right[z.m_face : z.m_coef, :]
    ext[...] = jnp.zeros_like(ext)
    halo = from_left[z.m_rows :, :].astype(F32)
    skip = z.last - z.right_lo
    ext[0, : z.stride, :] = halo[skip : skip + z.stride]
    ext[0, z.stride : z.nodes, :] = xs[: z.face, :]
    halo = from_right[z.m_rows :, :].astype(F32)
    skip = z.face - z.left_lo
    ext[1, : z.face, :] = xs[z.end :, :]
    ext[1, z.face : z.nodes, :] = halo[skip : skip + z.stride]
    own = own_coeffs[...]
    for k in range(z.chunks):
        cols = slice(k * LANES, (k + 1) * LANES)
        own += dot(mine_left[k * c : (k + 1) * c, :], ext[0, cols, :].astype(BF16))
        own += dot(mine_right[k * c : (k + 1) * c, :], ext[1, cols, :].astype(BF16))
    before = dot(rows0[c:, :], x0[: z.nodes, :])
    before += from_left[z.m_coef : z.m_rows, :].astype(F32)
    after = dot(rows1[c:, :], xs[z.last :, :].astype(BF16))
    after += from_right[z.m_coef : z.m_rows, :].astype(F32)
    terms[...] = base[...]
    add_cells(
        z, dot(spread0[...], twice(own, before)), dot(spread1[...], twice(own, after)), terms
    )
    part[...] = terms[...] * gain
    send_part(z, rows0, rows1, face0, face1, part, coeffs, right, left, far_right, far_left)
    right[z.l_term :, : z.tail] = end_rows[:, k_last:]
    left[z.l_term :, :] = cell0[: z.pad_face, :LANES]


def beside_second(z, gain, back, part, x0, cell0, cell1, mix_high, mix_low, face0, face1,
                  base, edge0, edge1):
    scale = face_scale(z)
    base[...] = scale * ((-CENTRE * gain) * part[...] - back * x0[...].astype(F32))
    add_cells(
        z,
        gain * dot(cell0[...], part[: z.nodes, :].astype(BF16)),
        gain * dot(cell1[...], part[z.last :, :].astype(BF16)),
        base,
    )
    edge0[...] = mixed(face0[...].T, mix_high, mix_low)
    edge1[...] = mixed(face1[...].T, mix_high, mix_low)


def second_kernel(
    z, gain,
    base, own_coeffs, from_left, from_right, from_far_left, from_far_right,
    cell0, cell1, end_rows, rows0, rows1, spread0, spread1, face0, face1,
    part, coeffs, right, left, far_right, far_left,
):
    s = whole_coeffs(z, own_coeffs, from_left, from_right, from_far_left, from_far_right)
    term0, term1 = neighbour_terms(
        z, s, from_left, from_right, cell0, cell1, spread0, spread1
    )
    part[...] = base[...]
    add_cells(z, gain * term0, gain * term1, part)
    first, last = face_rows(z, from_left, from_right)
    part[: z.face, :] -= (0.5 * CENTRE * gain) * first
    part[z.end :, :] -= (0.5 * CENTRE * gain) * last
    send_part(z, rows0, rows1, face0, face1, part, coeffs, right, left, far_right, far_left)
    right[z.l_term :, :] = dot(end_rows[...], part[z.last :, :].astype(BF16)).astype(BF16)
    left[z.l_term :, :] = dot(
        cell0[: z.pad_face, :], part[: z.nodes, :].astype(BF16)
    ).astype(BF16)


def beside_third(z, gain, back, part, earlier, from_left, from_right, mine_right, mine_left,
                 cell0, cell1, base):
    base[...] = (-CENTRE * gain) * part[...] - back * earlier[...]
    add_cells(
        z,
        gain * dot(cell0[...], part[: z.nodes, :].astype(BF16)),
        gain * dot(cell1[...], part[z.last :, :].astype(BF16)),
        base,
    )
    first, last = face_rows(z, from_left, from_right)
    faces = slice(z.l_face, z.l_term)
    term = dot(from_left[z.l_term :, : z.span], mine_left[faces, :])[: z.face]
    base[: z.face, :] += gain * term - back * first
    term = dot(from_right[z.l_term :, : z.span], mine_right[faces, :])[: z.face]
    base[z.end :, :] += gain * term - back * last


def third_kernel(
    z, gain, share,
    base, own_coeffs, from_left, from_right, from_far_left, from_far_right,
    cell0, cell1, spread0, spread1, edge0, edge1, occupation,
    out, density,
):
    s = whole_coeffs(z, own_coeffs, from_left, from_right, from_far_left, from_far_right)
    before, own, after = s
    term0, term1 = neighbour_terms(
        z, s, from_left, from_right, cell0, cell1, spread0, spread1
    )
    out[...] = base[...]
    add_cells(z, gain * term0, gain * term1, out)
    first, last = face_rows(z, from_left, from_right)
    faces = slice(z.l_term, z.l_term + z.face)
    at = slice(z.shift, z.shift + z.face)
    term = from_left[faces, :].astype(F32) + dot(edge0[...], twice(own, before))[at]
    out[: z.face, :] += gain * (term - CENTRE * first)
    term = from_right[faces, :].astype(F32) + dot(edge1[...], twice(own, after))[: z.face]
    out[z.end :, :] += gain * (term - CENTRE * last)
    result = out[...]
    density[...] = lax.dot_general(
        occupation[...] * share,
        result * result,
        (((1,), (1,)), ((), ())),
        preferred_element_type=F32,
        precision=lax.Precision.HIGHEST,
    )


def call(kernel, outs, scratch, *args, hbm=0):
    vmem = pl.BlockSpec(memory_space=pltpu.VMEM)
    far = pl.BlockSpec(memory_space=pltpu.HBM)
    return pl.pallas_call(
        kernel,
        out_shape=[jax.ShapeDtypeStruct(s, t) for s, t in outs],
        in_specs=[far] * hbm + [vmem] * (len(args) - hbm),
        out_specs=[vmem] * len(outs),
        scratch_shapes=scratch,
        compiler_params=pltpu.CompilerParams(vmem_limit_bytes=32 * 1024 * 1024),
    )(*args)


def body(filter_input, cell_table, cell_type, atom_center, proj_values, coupling, occupation):
    cells = cell_type.shape[0]
    atoms, projectors = proj_values.shape[0], proj_values.shape[2]
    rows, states = filter_input.shape
    z = Sizes(rows, cells, cell_table.shape[1], atoms, projectors)
    c, n = z.coef, z.nodes
    devices, groups = lax.axis_size("cells"), lax.axis_size("states")

    def shifted(array, by):
        return lax.ppermute(array, "cells", [(i, (i + by) % devices) for i in range(devices)])

    half_width = (upper_edge - lower_edge) / 2.0
    scale = half_width / (ground_edge - CENTRE)
    twice_inverse = 2.0 / scale
    gains, backs = [scale / half_width], [0.0]
    for _ in range(STEPS - 1):
        scale_next = 1.0 / (twice_inverse - scale)
        gains.append(2.0 * scale_next / half_width)
        backs.append(scale * scale_next)
        scale = scale_next

    field, share = ((rows, states), F32), ((c, states), F32)
    scratch = pltpu.VMEM(*field)
    x0, right, left, own0, own1, own_share = call(
        functools.partial(pack_kernel, z),
        [((rows, states), BF16)]
        + [((z.first, states), BF16)] * 2
        + [((c, n), BF16)] * 2
        + [share],
        [
            pltpu.SMEM(atom_center.shape, jnp.int32),
            pltpu.VMEM(proj_values.shape, BF16),
            scratch,
            pltpu.SemaphoreType.DMA((3,)),
        ],
        atom_center, filter_input, proj_values,
        hbm=3,
    )
    from_left, from_right = shifted(right, 1), shifted(left, -1)

    onehot = (cell_type[:, None] == jnp.arange(cell_table.shape[0])[None, :]).astype(BF16)
    matrices = jnp.einsum("ct,tij->cij", onehot, cell_table, preferred_element_type=F32)
    matrices = matrices.astype(BF16)
    cell0, cell1 = matrices[0], matrices[-1]
    base, mix_high, mix_low, end_rows = call(
        functools.partial(beside_first, z),
        [field] + [((2 * c, 2 * c), BF16)] * 2 + [((z.pad_face, n), BF16)],
        [scratch],
        coupling, x0, cell0, cell1,
    )

    coeffs = ((3 * c, states), F32)
    messages = [((z.later, states), BF16)] * 2 + [((c, states), BF16)] * 2
    part1, own_coeffs, right, left, far_right, far_left, rows0, rows1, spread0, spread1, face0, face1 = (
        call(
            functools.partial(first_kernel, z, gains[0]),
            [field, coeffs]
            + messages
            + [((2 * c, n), BF16)] * 2
            + [((n, 4 * c), BF16)] * 2
            + [((2 * c, LANES), BF16)] * 2,
            [scratch, pltpu.VMEM((2, z.chunks * LANES, states), F32), scratch],
            base, x0, own0, own1, own_share, right, left, from_left, from_right,
            cell0, mix_high, mix_low, end_rows,
        )
    )
    second_left, second_right = shifted(right, 1), shifted(left, -1)
    from_far_left, from_far_right = shifted(far_right, 2), shifted(far_left, -2)
    base, edge0, edge1 = call(
        functools.partial(beside_second, z, gains[1], backs[1]),
        [field] + [((LANES, 4 * c), BF16)] * 2,
        [],
        part1, x0, cell0, cell1, mix_high, mix_low, face0, face1,
    )
    part2, own_coeffs, right, left, far_right, far_left = call(
        functools.partial(second_kernel, z, gains[1]),
        [field, coeffs] + messages,
        [],
        base, own_coeffs, second_left, second_right, from_far_left, from_far_right,
        cell0, cell1, end_rows, rows0, rows1, spread0, spread1, face0, face1,
    )
    from_left, from_right = shifted(right, 1), shifted(left, -1)
    from_far_left, from_far_right = shifted(far_right, 2), shifted(far_left, -2)
    (base,) = call(
        functools.partial(beside_third, z, gains[2], backs[2]),
        [field],
        [],
        part2, part1, second_left, second_right, right, left, cell0, cell1,
    )
    filtered, density = call(
        functools.partial(third_kernel, z, gains[2], 1.0 / (states * groups)),
        [field, ((1, rows), F32)],
        [],
        base, own_coeffs, from_left, from_right, from_far_left, from_far_right,
        cell0, cell1, spread0, spread1, edge0, edge1, occupation[None, :],
    )
    return filtered, total(density, groups)[0]


def total(density, groups):
    if groups & (groups - 1):
        return lax.psum(density, "states")
    step = 1
    while step < groups:
        density += lax.ppermute(density, "states", [(i, i ^ step) for i in range(groups)])
        step *= 2
    return density


def solution(mesh):
    in_specs = (
        P("cells", "states"),
        P(),
        P("cells"),
        P("cells"),
        P("cells", None, None, None),
        P(),
        P("states"),
    )
    out_specs = (P("cells", "states"), P("cells"))
    return jax.shard_map(body, mesh=mesh, in_specs=in_specs, out_specs=out_specs, check_vma=False)
```

```python
import functools

import jax
import jax.numpy as jnp
from jax import lax
from jax.experimental import pallas as pl
from jax.experimental.pallas import tpu as pltpu
from jax.sharding import PartitionSpec as P

STEPS = 3
LANES = 128
ROWS16 = 16

lower_edge = 4.0
upper_edge = 12.0
ground_edge = -2.0

F32 = jnp.float32
BF16 = jnp.bfloat16


def up16(n):
    return -(-n // ROWS16) * ROWS16


def down16(n):
    return n // ROWS16 * ROWS16


class Sizes:
    def __init__(self, node_rows, cells, cell_nodes, atoms, projectors):
        self.rows = node_rows
        self.nodes = cell_nodes
        self.stride = (node_rows - cell_nodes) // (cells - 1)
        self.face = cell_nodes - self.stride
        self.last = node_rows - cell_nodes
        self.end = node_rows - self.face
        self.atoms = atoms
        self.proj = projectors
        self.coef = atoms * projectors
        self.chunks = -(-cell_nodes // LANES)
        self.tail = cell_nodes - (self.chunks - 1) * LANES
        self.shift = self.stride - (self.chunks - 1) * LANES
        self.m_face = self.chunks * self.coef
        self.m_coef = self.m_face + self.coef
        self.m_rows = self.m_coef + self.coef
        self.right_lo, self.right_hi = down16(self.last), up16(self.end)
        self.left_lo, self.left_hi = down16(self.face), up16(cell_nodes)
        self.halo = max(self.right_hi - self.right_lo, self.left_hi - self.left_lo)
        self.first = self.m_rows + self.halo
        self.pad_face = up16(self.face)
        self.span = up16(self.shift + self.face)
        self.l_face = 2 * self.coef
        self.l_term = self.l_face + self.span
        self.later = self.l_term + self.pad_face


def dot(a, b):
    return jnp.dot(a, b, preferred_element_type=F32)


def exact_dot(a, b):
    return jnp.dot(a, b, preferred_element_type=F32, precision=lax.Precision.HIGHEST)


def halves(v):
    high = v.astype(BF16)
    return high, (v - high.astype(F32)).astype(BF16)


def is_even():
    return lax.rem(lax.axis_index("cells"), 2) == 0


def put(near, over, at, to_right, to_left):
    even = is_even()
    near[at] = jnp.where(even, to_right, to_left)
    over[at] = jnp.where(even, to_left, to_right)


def take(near, over, at):
    even = is_even()
    a, b = near[at], over[at]
    return jnp.where(even, b, a), jnp.where(even, a, b)


def pack_kernel(
    z, center_hbm, x0_hbm, proj_hbm, x0, near, over, own0, own1, coeffs, center, proj, xs, sems
):
    copies = [
        pltpu.make_async_copy(x0_hbm, x0, sems.at[0]),
        pltpu.make_async_copy(center_hbm, center, sems.at[1]),
        pltpu.make_async_copy(proj_hbm, proj, sems.at[2]),
    ]
    for copy in copies:
        copy.start()
    near[: z.m_coef, :] = jnp.zeros((z.m_coef, near.shape[1]), BF16)
    over[: z.m_coef, :] = jnp.zeros((z.m_coef, near.shape[1]), BF16)
    copies[0].wait()
    xs[...] = x0[...].astype(F32)
    put(
        near, over, (slice(z.m_rows, z.first), slice(None)),
        x0[z.right_lo : z.right_lo + z.halo, :], x0[z.left_lo : z.left_lo + z.halo, :],
    )
    copies[1].wait()
    copies[2].wait()
    for a in range(z.atoms):
        low = center[a] == 0
        before, here, after = proj[a, 0], proj[a, 1], proj[a, 2]
        none = jnp.zeros_like(before)
        at = slice(a * z.proj, (a + 1) * z.proj)
        on0 = jnp.where(low, here, before)
        on1 = jnp.where(low, after, here)
        own0[at, :] = on0
        own1[at, :] = on1
        reach_left = jnp.where(low, before, none)
        reach_right = jnp.where(low, none, after)
        for k in range(z.chunks):
            width = LANES if k < z.chunks - 1 else z.tail
            cols = slice(k * LANES, k * LANES + width)
            rows = slice(k * z.coef + a * z.proj, k * z.coef + (a + 1) * z.proj)
            put(
                near, over, (rows, slice(0, width)), reach_right[:, cols], reach_left[:, cols]
            )
        rows = slice(z.m_face + a * z.proj, z.m_face + (a + 1) * z.proj)
        wide = jnp.zeros((z.proj, LANES - z.tail), BF16)
        end = jnp.concatenate([on1[:, (z.chunks - 1) * LANES :], wide], axis=1)
        put(near, over, (rows, slice(None)), end, on0[:, :LANES])
    s = dot(own0[...], x0[: z.nodes, :]) + dot(own1[...], xs[z.last :, :].astype(BF16))
    coeffs[...] = s
    sent = s.astype(BF16)
    near[z.m_coef : z.m_rows, :] = sent
    over[z.m_coef : z.m_rows, :] = sent


def add_cells(z, term0, term1, out):
    out[: z.nodes, :] += term0
    out[z.last :, :] += term1


def face_scale(z):
    row = lax.broadcasted_iota(jnp.int32, (z.rows, 1), 0)
    return jnp.where((row < z.face) | (row >= z.end), 0.5, 1.0).astype(F32)


CENTRE = (upper_edge + lower_edge) / 2.0


def twice(a, b):
    return jnp.concatenate([a, b, a, b], axis=0).astype(BF16)


def send_part(
    z, rows0, rows1, face0, face1, end0, end1, part, coeffs, near, over, far, farther, first, last
):
    c = z.coef
    last[...] = jnp.zeros_like(last)
    first[...] = jnp.zeros_like(first)
    last[: z.face, :] = part[z.end :, :]
    first[z.shift : z.shift + z.face, :] = part[: z.face, :]
    last_rows, first_rows = last[...].astype(BF16), first[...].astype(BF16)
    put(near, over, (slice(z.l_face, z.l_term), slice(None)), last_rows, first_rows)
    on0, on1 = part[: z.nodes, :].astype(BF16), part[z.last :, :].astype(BF16)
    s0 = dot(rows0[...], on0) + dot(face0[:, : z.span], first_rows)
    s1 = dot(rows1[...], on1) + dot(face1[:, : z.span], last_rows)
    before, own, after = s0[c:], s0[:c] + s1[:c], s1[c:]
    coeffs[:c, :] = before
    coeffs[c : 2 * c, :] = own
    coeffs[2 * c :, :] = after
    before, own, after = before.astype(BF16), own.astype(BF16), after.astype(BF16)
    near[:c, :] = own
    over[:c, :] = own
    put(near, over, (slice(c, 2 * c), slice(None)), after, before)
    even = is_even()
    far[...] = jnp.where(even, before, after)
    farther[...] = jnp.where(even, after, before)
    if end0 is None:
        return
    put(
        near, over, (slice(z.l_term, z.later), slice(None)),
        dot(end1[...], on1).astype(BF16), dot(end0[: z.pad_face, :], on0).astype(BF16),
    )


def whole_coeffs(z, own_ref, near, over, far, farther):
    c = z.coef
    left, right = (v.astype(F32) for v in take(near, over, (slice(0, 2 * c), slice(None))))
    even = is_even()
    a, b = far[...], farther[...]
    far_left, far_right = jnp.where(even, b, a), jnp.where(even, a, b)
    before = own_ref[:c, :] + left[:c] + far_left.astype(F32)
    own = own_ref[c : 2 * c, :] + left[c:] + right[c:]
    after = own_ref[2 * c :, :] + right[:c] + far_right.astype(F32)
    return before, own, after


def face_rows(z, near, over):
    first, last = take(near, over, (slice(z.l_face, z.l_term), slice(None)))
    return (
        first.astype(F32)[: z.face],
        last.astype(F32)[z.shift : z.shift + z.face],
    )


def neighbour_terms(z, s, near, over, cell0, cell1, spread0, spread1):
    before, own, after = s
    first, last = take(near, over, (slice(z.l_face, z.l_term), slice(None)))
    k_last = (z.chunks - 1) * LANES
    term0 = dot(spread0[...], twice(own, before)) + dot(cell0[:, : z.span], first)
    term1 = dot(spread1[...], twice(own, after)) + dot(cell1[:, k_last:], last[: z.tail])
    return term0, term1


def beside_first(
    z, coupling, x0, cell0, cell1, base, mix_high, mix_low, end_rows, xs
):
    xs[...] = x0[...].astype(F32)
    base[...] = (-CENTRE) * (face_scale(z) * xs[...])
    add_cells(
        z, dot(cell0[...], x0[: z.nodes, :]), dot(cell1[...], xs[z.last :, :].astype(BF16)), base
    )
    size = 2 * z.coef
    row = lax.broadcasted_iota(jnp.int32, (size, z.proj), 0)
    col = lax.broadcasted_iota(jnp.int32, (size, z.proj), 1)
    pick = jnp.where(lax.rem(row, z.proj) == col, 1.0, 0.0).astype(F32)
    wide = exact_dot(pick, coupling[...])
    wide = lax.dot_general(
        wide, pick, (((1,), (1,)), ((), ())),
        preferred_element_type=F32, precision=lax.Precision.HIGHEST,
    )
    row = lax.broadcasted_iota(jnp.int32, (size, size), 0)
    col = lax.broadcasted_iota(jnp.int32, (size, size), 1)
    mix = jnp.where(lax.div(row, z.proj) == lax.div(col, z.proj), wide, 0.0)
    mix_high[...], mix_low[...] = halves(mix)
    end_rows[...] = jnp.zeros_like(end_rows)
    end_rows[: z.face, :] = cell1[...].astype(F32)[z.stride :].astype(BF16)


def mixed(a, mix_high, mix_low):
    high, low = halves(dot(a, mix_high[...]) + dot(a, mix_low[...]))
    return jnp.concatenate([high, low], axis=1)


def first_kernel(
    z, gain,
    base, x0, own0, own1, own_coeffs, mine_near, mine_over, from_near, from_over,
    cell0, mix_high, mix_low, end_rows,
    part, coeffs, near, over, far, farther,
    rows0, rows1, spread0, spread1, face0, face1,
    xs, ext, terms, first, last,
):
    c, k_last = z.coef, (z.chunks - 1) * LANES
    xs[...] = x0[...].astype(F32)
    rows0[:c, :] = own0[...]
    rows1[:c, :] = own1[...]
    for k in range(z.chunks):
        width = LANES if k < z.chunks - 1 else z.tail
        cols = slice(k * LANES, k * LANES + width)
        rows0[c:, cols], rows1[c:, cols] = take(
            from_near, from_over, (slice(k * c, (k + 1) * c), slice(0, width))
        )
    spread0[...] = mixed(rows0[...].T, mix_high, mix_low)
    spread1[...] = mixed(rows1[...].T, mix_high, mix_low)
    chunks = [
        take(mine_near, mine_over, (slice(k * c, (k + 1) * c), slice(None)))
        for k in range(z.chunks)
    ]
    face0[:c, :] = chunks[-1][0]
    face1[:c, :] = chunks[0][1]
    face0[c:, :], face1[c:, :] = take(
        from_near, from_over, (slice(z.m_face, z.m_coef), slice(None))
    )
    ext[...] = jnp.zeros_like(ext)
    halo = take(from_near, from_over, (slice(z.m_rows, z.first), slice(None)))
    skip = z.last - z.right_lo
    ext[0, : z.stride, :] = halo[0].astype(F32)[skip : skip + z.stride]
    ext[0, z.stride : z.nodes, :] = xs[: z.face, :]
    skip = z.face - z.left_lo
    ext[1, : z.face, :] = xs[z.end :, :]
    ext[1, z.face : z.nodes, :] = halo[1].astype(F32)[skip : skip + z.stride]
    own = own_coeffs[...]
    for k in range(z.chunks):
        cols = slice(k * LANES, (k + 1) * LANES)
        own += dot(chunks[k][0], ext[0, cols, :].astype(BF16))
        own += dot(chunks[k][1], ext[1, cols, :].astype(BF16))
    before, after = take(from_near, from_over, (slice(z.m_coef, z.m_rows), slice(None)))
    before = before.astype(F32) + dot(rows0[c:, :], x0[: z.nodes, :])
    after = after.astype(F32) + dot(rows1[c:, :], xs[z.last :, :].astype(BF16))
    terms[...] = base[...]
    add_cells(
        z, dot(spread0[...], twice(own, before)), dot(spread1[...], twice(own, after)), terms
    )
    part[...] = terms[...] * gain
    send_part(
        z, rows0, rows1, face0, face1, None, None,
        part, coeffs, near, over, far, farther, first, last,
    )
    wide = jnp.zeros((z.pad_face, LANES - z.tail), BF16)
    put(
        near, over, (slice(z.l_term, z.later), slice(None)),
        jnp.concatenate([end_rows[:, k_last:], wide], axis=1), cell0[: z.pad_face, :LANES],
    )


def beside_second(z, gain, back, part, x0, cell0, cell1, mix_high, mix_low, face0, face1,
                  base, edge0, edge1):
    scale = face_scale(z)
    base[...] = scale * ((-CENTRE * gain) * part[...] - back * x0[...].astype(F32))
    add_cells(
        z,
        gain * dot(cell0[...], part[: z.nodes, :].astype(BF16)),
        gain * dot(cell1[...], part[z.last :, :].astype(BF16)),
        base,
    )
    edge0[...] = mixed(face0[...].T, mix_high, mix_low)
    edge1[...] = mixed(face1[...].T, mix_high, mix_low)


def second_kernel(
    z, gain,
    base, own_coeffs, from_near, from_over, from_far, from_farther,
    cell0, cell1, end_rows, rows0, rows1, spread0, spread1, face0, face1,
    part, coeffs, near, over, far, farther,
    first_rows, last_rows,
):
    s = whole_coeffs(z, own_coeffs, from_near, from_over, from_far, from_farther)
    term0, term1 = neighbour_terms(z, s, from_near, from_over, cell0, cell1, spread0, spread1)
    part[...] = base[...]
    add_cells(z, gain * term0, gain * term1, part)
    first, last = face_rows(z, from_near, from_over)
    part[: z.face, :] -= (0.5 * CENTRE * gain) * first
    part[z.end :, :] -= (0.5 * CENTRE * gain) * last
    send_part(
        z, rows0, rows1, face0, face1, cell0, end_rows,
        part, coeffs, near, over, far, farther, first_rows, last_rows,
    )


def beside_third(z, gain, back, part, earlier, from_near, from_over, mine_near, mine_over,
                 cell0, cell1, base):
    base[...] = (-CENTRE * gain) * part[...] - back * earlier[...]
    add_cells(
        z,
        gain * dot(cell0[...], part[: z.nodes, :].astype(BF16)),
        gain * dot(cell1[...], part[z.last :, :].astype(BF16)),
        base,
    )
    first, last = face_rows(z, from_near, from_over)
    blocks = take(from_near, from_over, (slice(z.l_term, z.later), slice(0, z.span)))
    mine = take(mine_near, mine_over, (slice(z.l_face, z.l_term), slice(None)))
    base[: z.face, :] += gain * dot(blocks[0], mine[0])[: z.face] - back * first
    base[z.end :, :] += gain * dot(blocks[1], mine[1])[: z.face] - back * last


def third_kernel(
    z, gain, share,
    base, own_coeffs, from_near, from_over, from_far, from_farther,
    cell0, cell1, spread0, spread1, edge0, edge1, occupation,
    out, density,
):
    s = whole_coeffs(z, own_coeffs, from_near, from_over, from_far, from_farther)
    before, own, after = s
    term0, term1 = neighbour_terms(z, s, from_near, from_over, cell0, cell1, spread0, spread1)
    out[...] = base[...]
    add_cells(z, gain * term0, gain * term1, out)
    first, last = face_rows(z, from_near, from_over)
    terms = take(from_near, from_over, (slice(z.l_term, z.later), slice(None)))
    left, right = (v.astype(F32)[: z.face] for v in terms)
    left += dot(edge0[...], twice(own, before))[z.shift : z.shift + z.face]
    right += dot(edge1[...], twice(own, after))[: z.face]
    out[: z.face, :] += gain * (left - CENTRE * first)
    out[z.end :, :] += gain * (right - CENTRE * last)
    result = out[...]
    density[...] = lax.dot_general(
        occupation[...] * share,
        result * result,
        (((1,), (1,)), ((), ())),
        preferred_element_type=F32,
        precision=lax.Precision.HIGHEST,
    )


def call(kernel, outs, scratch, *args, hbm=0, megabytes=32):
    vmem = pl.BlockSpec(memory_space=pltpu.VMEM)
    far = pl.BlockSpec(memory_space=pltpu.HBM)
    return pl.pallas_call(
        kernel,
        out_shape=[jax.ShapeDtypeStruct(s, t) for s, t in outs],
        in_specs=[far] * hbm + [vmem] * (len(args) - hbm),
        out_specs=[vmem] * len(outs),
        scratch_shapes=scratch,
        compiler_params=pltpu.CompilerParams(vmem_limit_bytes=megabytes * 1024 * 1024),
    )(*args)


def body(filter_input, cell_table, cell_type, atom_center, proj_values, coupling, occupation):
    cells = cell_type.shape[0]
    atoms, projectors = proj_values.shape[0], proj_values.shape[2]
    rows, states = filter_input.shape
    z = Sizes(rows, cells, cell_table.shape[1], atoms, projectors)
    c, n = z.coef, z.nodes
    devices, groups = lax.axis_size("cells"), lax.axis_size("states")

    def exchanged(array, even_by):
        pairs = [
            (i, (i + (even_by if i % 2 == 0 else -even_by)) % devices) for i in range(devices)
        ]
        return lax.ppermute(array, "cells", pairs)

    def exchange_all(near, over, far, farther):
        far = exchanged(far, -2)
        near = exchanged(near, 1)
        farther = exchanged(farther, 2)
        over = exchanged(over, -1)
        return near, over, far, farther

    half_width = (upper_edge - lower_edge) / 2.0
    scale = half_width / (ground_edge - CENTRE)
    twice_inverse = 2.0 / scale
    gains, backs = [scale / half_width], [0.0]
    for _ in range(STEPS - 1):
        scale_next = 1.0 / (twice_inverse - scale)
        gains.append(2.0 * scale_next / half_width)
        backs.append(scale * scale_next)
        scale = scale_next

    field, share = ((rows, states), F32), ((c, states), F32)
    scratch = pltpu.VMEM(*field)
    x0, near, over, own0, own1, own_share = call(
        functools.partial(pack_kernel, z),
        [((rows, states), BF16)]
        + [((z.first, states), BF16)] * 2
        + [((c, n), BF16)] * 2
        + [share],
        [
            pltpu.SMEM(atom_center.shape, jnp.int32),
            pltpu.VMEM(proj_values.shape, BF16),
            scratch,
            pltpu.SemaphoreType.DMA((3,)),
        ],
        atom_center, filter_input, proj_values,
        hbm=3,
        megabytes=56,
    )
    from_over, from_near = exchanged(over, -1), exchanged(near, 1)

    onehot = (cell_type[:, None] == jnp.arange(cell_table.shape[0])[None, :]).astype(BF16)
    matrices = jnp.einsum("ct,tij->cij", onehot, cell_table, preferred_element_type=F32)
    matrices = matrices.astype(BF16)
    cell0, cell1 = matrices[0], matrices[-1]
    base, mix_high, mix_low, end_rows = call(
        functools.partial(beside_first, z),
        [field] + [((2 * c, 2 * c), BF16)] * 2 + [((z.pad_face, n), BF16)],
        [scratch],
        coupling, x0, cell0, cell1,
    )

    coeffs = ((3 * c, states), F32)
    messages = [((z.later, states), BF16)] * 2 + [((c, states), BF16)] * 2
    faces = [pltpu.VMEM((z.span, states), F32)] * 2
    part1, own_coeffs, near, over, far, farther, rows0, rows1, spread0, spread1, face0, face1 = (
        call(
            functools.partial(first_kernel, z, gains[0]),
            [field, coeffs]
            + messages
            + [((2 * c, n), BF16)] * 2
            + [((n, 4 * c), BF16)] * 2
            + [((2 * c, LANES), BF16)] * 2,
            [scratch, pltpu.VMEM((2, z.chunks * LANES, states), F32), scratch] + faces,
            base, x0, own0, own1, own_share, near, over, from_near, from_over,
            cell0, mix_high, mix_low, end_rows,
        )
    )
    second = exchange_all(near, over, far, farther)
    base, edge0, edge1 = call(
        functools.partial(beside_second, z, gains[1], backs[1]),
        [field] + [((LANES, 4 * c), BF16)] * 2,
        [],
        part1, x0, cell0, cell1, mix_high, mix_low, face0, face1,
    )
    part2, own_coeffs, near, over, far, farther = call(
        functools.partial(second_kernel, z, gains[1]),
        [field, coeffs] + messages,
        faces,
        base, own_coeffs, *second,
        cell0, cell1, end_rows, rows0, rows1, spread0, spread1, face0, face1,
    )
    third = exchange_all(near, over, far, farther)
    (base,) = call(
        functools.partial(beside_third, z, gains[2], backs[2]),
        [field],
        [],
        part2, part1, second[0], second[1], near, over, cell0, cell1,
    )
    filtered, density = call(
        functools.partial(third_kernel, z, gains[2], 1.0 / (states * groups)),
        [field, ((1, rows), F32)],
        [],
        base, own_coeffs, *third,
        cell0, cell1, spread0, spread1, edge0, edge1, occupation[None, :],
    )
    return filtered, total(density, groups)[0]


def total(density, groups):
    if groups & (groups - 1):
        return lax.psum(density, "states")
    step = 1
    while step < groups:
        density += lax.ppermute(density, "states", [(i, i ^ step) for i in range(groups)])
        step *= 2
    return density


def solution(mesh):
    in_specs = (
        P("cells", "states"),
        P(),
        P("cells"),
        P("cells"),
        P("cells", None, None, None),
        P(),
        P("states"),
    )
    out_specs = (P("cells", "states"), P("cells"))
    return jax.shard_map(body, mesh=mesh, in_specs=in_specs, out_specs=out_specs, check_vma=False)
```

```python
import functools

import jax
import jax.numpy as jnp
from jax import lax
from jax.experimental import pallas as pl
from jax.experimental.pallas import tpu as pltpu
from jax.sharding import PartitionSpec as P

STEPS = 3
LANES = 128
ROWS16 = 16

lower_edge = 4.0
upper_edge = 12.0
ground_edge = -2.0

F32 = jnp.float32
BF16 = jnp.bfloat16


def up16(n):
    return -(-n // ROWS16) * ROWS16


def down16(n):
    return n // ROWS16 * ROWS16


class Sizes:
    def __init__(self, node_rows, cells, cell_nodes, atoms, projectors):
        self.rows = node_rows
        self.nodes = cell_nodes
        self.stride = (node_rows - cell_nodes) // (cells - 1)
        self.face = cell_nodes - self.stride
        self.last = node_rows - cell_nodes
        self.end = node_rows - self.face
        self.atoms = atoms
        self.proj = projectors
        self.coef = atoms * projectors
        self.chunks = -(-cell_nodes // LANES)
        self.tail = cell_nodes - (self.chunks - 1) * LANES
        self.shift = self.stride - (self.chunks - 1) * LANES
        self.m_face = self.chunks * self.coef
        self.m_coef = self.m_face + self.coef
        self.m_rows = self.m_coef + self.coef
        self.right_lo, self.right_hi = down16(self.last), up16(self.end)
        self.left_lo, self.left_hi = down16(self.face), up16(cell_nodes)
        self.halo = max(self.right_hi - self.right_lo, self.left_hi - self.left_lo)
        self.first = self.m_rows + self.halo
        self.pad_face = up16(self.face)
        self.span = up16(self.shift + self.face)
        self.l_face = 2 * self.coef
        self.l_term = self.l_face + self.span
        self.later = self.l_term + self.pad_face


def dot(a, b):
    return jnp.dot(a, b, preferred_element_type=F32)


def exact_dot(a, b):
    return jnp.dot(a, b, preferred_element_type=F32, precision=lax.Precision.HIGHEST)


def halves(v):
    high = v.astype(BF16)
    return high, (v - high.astype(F32)).astype(BF16)


def is_even():
    return lax.rem(lax.axis_index("cells"), 2) == 0


def put(near, over, at, to_right, to_left):
    even = is_even()
    near[at] = jnp.where(even, to_right, to_left)
    over[at] = jnp.where(even, to_left, to_right)


def take(near, over, at):
    even = is_even()
    a, b = near[at], over[at]
    return jnp.where(even, b, a), jnp.where(even, a, b)


def pack_kernel(
    z, center_hbm, x0_hbm, proj_hbm, x0, near, over, own0, own1, coeffs, center, proj, xs, sems
):
    copies = [
        pltpu.make_async_copy(x0_hbm, x0, sems.at[0]),
        pltpu.make_async_copy(center_hbm, center, sems.at[1]),
        pltpu.make_async_copy(proj_hbm, proj, sems.at[2]),
    ]
    for copy in copies:
        copy.start()
    near[: z.m_coef, :] = jnp.zeros((z.m_coef, near.shape[1]), BF16)
    over[: z.m_coef, :] = jnp.zeros((z.m_coef, near.shape[1]), BF16)
    copies[0].wait()
    xs[...] = x0[...].astype(F32)
    put(
        near, over, (slice(z.m_rows, z.first), slice(None)),
        x0[z.right_lo : z.right_lo + z.halo, :], x0[z.left_lo : z.left_lo + z.halo, :],
    )
    copies[1].wait()
    copies[2].wait()
    for a in range(z.atoms):
        low = center[a] == 0
        before, here, after = proj[a, 0], proj[a, 1], proj[a, 2]
        none = jnp.zeros_like(before)
        at = slice(a * z.proj, (a + 1) * z.proj)
        on0 = jnp.where(low, here, before)
        on1 = jnp.where(low, after, here)
        own0[at, :] = on0
        own1[at, :] = on1
        reach_left = jnp.where(low, before, none)
        reach_right = jnp.where(low, none, after)
        for k in range(z.chunks):
            width = LANES if k < z.chunks - 1 else z.tail
            cols = slice(k * LANES, k * LANES + width)
            rows = slice(k * z.coef + a * z.proj, k * z.coef + (a + 1) * z.proj)
            put(
                near, over, (rows, slice(0, width)), reach_right[:, cols], reach_left[:, cols]
            )
        rows = slice(z.m_face + a * z.proj, z.m_face + (a + 1) * z.proj)
        wide = jnp.zeros((z.proj, LANES - z.tail), BF16)
        end = jnp.concatenate([on1[:, (z.chunks - 1) * LANES :], wide], axis=1)
        put(near, over, (rows, slice(None)), end, on0[:, :LANES])
    s = dot(own0[...], x0[: z.nodes, :]) + dot(own1[...], xs[z.last :, :].astype(BF16))
    coeffs[...] = s
    sent = s.astype(BF16)
    near[z.m_coef : z.m_rows, :] = sent
    over[z.m_coef : z.m_rows, :] = sent


def add_cells(z, term0, term1, out):
    out[: z.nodes, :] += term0
    out[z.last :, :] += term1


def face_scale(z):
    row = lax.broadcasted_iota(jnp.int32, (z.rows, 1), 0)
    return jnp.where((row < z.face) | (row >= z.end), 0.5, 1.0).astype(F32)


CENTRE = (upper_edge + lower_edge) / 2.0

FIRST_ORDER = (7, 8)
ORDER = (3, 2, 5, 4)


def twice(a, b):
    return jnp.concatenate([a, b, a, b], axis=0).astype(BF16)


def send_part(
    z, rows0, rows1, face0, face1, end0, end1, part, coeffs, near, over, far, farther, first, last
):
    c = z.coef
    last[...] = jnp.zeros_like(last)
    first[...] = jnp.zeros_like(first)
    last[: z.face, :] = part[z.end :, :]
    first[z.shift : z.shift + z.face, :] = part[: z.face, :]
    last_rows, first_rows = last[...].astype(BF16), first[...].astype(BF16)
    put(near, over, (slice(z.l_face, z.l_term), slice(None)), last_rows, first_rows)
    on0, on1 = part[: z.nodes, :].astype(BF16), part[z.last :, :].astype(BF16)
    s0 = dot(rows0[...], on0) + dot(face0[:, : z.span], first_rows)
    s1 = dot(rows1[...], on1) + dot(face1[:, : z.span], last_rows)
    before, own, after = s0[c:], s0[:c] + s1[:c], s1[c:]
    coeffs[:c, :] = before
    coeffs[c : 2 * c, :] = own
    coeffs[2 * c :, :] = after
    before, own, after = before.astype(BF16), own.astype(BF16), after.astype(BF16)
    near[:c, :] = own
    over[:c, :] = own
    put(near, over, (slice(c, 2 * c), slice(None)), after, before)
    even = is_even()
    far[...] = jnp.where(even, before, after)
    farther[...] = jnp.where(even, after, before)
    if end0 is None:
        return
    put(
        near, over, (slice(z.l_term, z.later), slice(None)),
        dot(end1[...], on1).astype(BF16), dot(end0[: z.pad_face, :], on0).astype(BF16),
    )


def whole_coeffs(z, own_ref, near, over, far, farther):
    c = z.coef
    left, right = (v.astype(F32) for v in take(near, over, (slice(0, 2 * c), slice(None))))
    even = is_even()
    a, b = far[...], farther[...]
    far_left, far_right = jnp.where(even, b, a), jnp.where(even, a, b)
    before = own_ref[:c, :] + left[:c] + far_left.astype(F32)
    own = own_ref[c : 2 * c, :] + left[c:] + right[c:]
    after = own_ref[2 * c :, :] + right[:c] + far_right.astype(F32)
    return before, own, after


def face_rows(z, near, over):
    first, last = take(near, over, (slice(z.l_face, z.l_term), slice(None)))
    return (
        first.astype(F32)[: z.face],
        last.astype(F32)[z.shift : z.shift + z.face],
    )


def neighbour_terms(z, s, near, over, cell0, cell1, spread0, spread1):
    before, own, after = s
    first, last = take(near, over, (slice(z.l_face, z.l_term), slice(None)))
    k_last = (z.chunks - 1) * LANES
    term0 = dot(spread0[...], twice(own, before)) + dot(cell0[:, : z.span], first)
    term1 = dot(spread1[...], twice(own, after)) + dot(cell1[:, k_last:], last[: z.tail])
    return term0, term1


def beside_first(
    z, coupling, x0, cell0, cell1, base, mix_high, mix_low, end_rows, xs
):
    xs[...] = x0[...].astype(F32)
    base[...] = (-CENTRE) * (face_scale(z) * xs[...])
    add_cells(
        z, dot(cell0[...], x0[: z.nodes, :]), dot(cell1[...], xs[z.last :, :].astype(BF16)), base
    )
    size = 2 * z.coef
    row = lax.broadcasted_iota(jnp.int32, (size, z.proj), 0)
    col = lax.broadcasted_iota(jnp.int32, (size, z.proj), 1)
    pick = jnp.where(lax.rem(row, z.proj) == col, 1.0, 0.0).astype(F32)
    wide = exact_dot(pick, coupling[...])
    wide = lax.dot_general(
        wide, pick, (((1,), (1,)), ((), ())),
        preferred_element_type=F32, precision=lax.Precision.HIGHEST,
    )
    row = lax.broadcasted_iota(jnp.int32, (size, size), 0)
    col = lax.broadcasted_iota(jnp.int32, (size, size), 1)
    mix = jnp.where(lax.div(row, z.proj) == lax.div(col, z.proj), wide, 0.0)
    mix_high[...], mix_low[...] = halves(mix)
    end_rows[...] = jnp.zeros_like(end_rows)
    end_rows[: z.face, :] = cell1[...].astype(F32)[z.stride :].astype(BF16)


def mixed(a, mix_high, mix_low):
    high, low = halves(dot(a, mix_high[...]) + dot(a, mix_low[...]))
    return jnp.concatenate([high, low], axis=1)


def first_kernel(
    z, gain,
    base, x0, own0, own1, own_coeffs, mine_near, mine_over, from_near, from_over,
    cell0, mix_high, mix_low, end_rows,
    part, coeffs, near, over, far, farther,
    rows0, rows1, spread0, spread1, face0, face1,
    xs, ext, terms, first, last,
):
    c, k_last = z.coef, (z.chunks - 1) * LANES
    xs[...] = x0[...].astype(F32)
    rows0[:c, :] = own0[...]
    rows1[:c, :] = own1[...]
    for k in range(z.chunks):
        width = LANES if k < z.chunks - 1 else z.tail
        cols = slice(k * LANES, k * LANES + width)
        rows0[c:, cols], rows1[c:, cols] = take(
            from_near, from_over, (slice(k * c, (k + 1) * c), slice(0, width))
        )
    spread0[...] = mixed(rows0[...].T, mix_high, mix_low)
    spread1[...] = mixed(rows1[...].T, mix_high, mix_low)
    chunks = [
        take(mine_near, mine_over, (slice(k * c, (k + 1) * c), slice(None)))
        for k in range(z.chunks)
    ]
    face0[:c, :] = chunks[-1][0]
    face1[:c, :] = chunks[0][1]
    face0[c:, :], face1[c:, :] = take(
        from_near, from_over, (slice(z.m_face, z.m_coef), slice(None))
    )
    ext[...] = jnp.zeros_like(ext)
    halo = take(from_near, from_over, (slice(z.m_rows, z.first), slice(None)))
    skip = z.last - z.right_lo
    ext[0, : z.stride, :] = halo[0].astype(F32)[skip : skip + z.stride]
    ext[0, z.stride : z.nodes, :] = xs[: z.face, :]
    skip = z.face - z.left_lo
    ext[1, : z.face, :] = xs[z.end :, :]
    ext[1, z.face : z.nodes, :] = halo[1].astype(F32)[skip : skip + z.stride]
    own = own_coeffs[...]
    for k in range(z.chunks):
        cols = slice(k * LANES, (k + 1) * LANES)
        own += dot(chunks[k][0], ext[0, cols, :].astype(BF16))
        own += dot(chunks[k][1], ext[1, cols, :].astype(BF16))
    before, after = take(from_near, from_over, (slice(z.m_coef, z.m_rows), slice(None)))
    before = before.astype(F32) + dot(rows0[c:, :], x0[: z.nodes, :])
    after = after.astype(F32) + dot(rows1[c:, :], xs[z.last :, :].astype(BF16))
    terms[...] = base[...]
    add_cells(
        z, dot(spread0[...], twice(own, before)), dot(spread1[...], twice(own, after)), terms
    )
    part[...] = terms[...] * gain
    send_part(
        z, rows0, rows1, face0, face1, None, None,
        part, coeffs, near, over, far, farther, first, last,
    )
    wide = jnp.zeros((z.pad_face, LANES - z.tail), BF16)
    put(
        near, over, (slice(z.l_term, z.later), slice(None)),
        jnp.concatenate([end_rows[:, k_last:], wide], axis=1), cell0[: z.pad_face, :LANES],
    )


def beside_second(z, gain, back, part, x0, cell0, cell1, mix_high, mix_low, face0, face1,
                  base, edge0, edge1):
    scale = face_scale(z)
    base[...] = scale * ((-CENTRE * gain) * part[...] - back * x0[...].astype(F32))
    add_cells(
        z,
        gain * dot(cell0[...], part[: z.nodes, :].astype(BF16)),
        gain * dot(cell1[...], part[z.last :, :].astype(BF16)),
        base,
    )
    edge0[...] = mixed(face0[...].T, mix_high, mix_low)
    edge1[...] = mixed(face1[...].T, mix_high, mix_low)


def second_kernel(
    z, gain,
    base, own_coeffs, from_near, from_over, from_far, from_farther,
    cell0, cell1, end_rows, rows0, rows1, spread0, spread1, face0, face1,
    part, coeffs, near, over, far, farther,
    first_rows, last_rows,
):
    s = whole_coeffs(z, own_coeffs, from_near, from_over, from_far, from_farther)
    term0, term1 = neighbour_terms(z, s, from_near, from_over, cell0, cell1, spread0, spread1)
    part[...] = base[...]
    add_cells(z, gain * term0, gain * term1, part)
    first, last = face_rows(z, from_near, from_over)
    part[: z.face, :] -= (0.5 * CENTRE * gain) * first
    part[z.end :, :] -= (0.5 * CENTRE * gain) * last
    send_part(
        z, rows0, rows1, face0, face1, cell0, end_rows,
        part, coeffs, near, over, far, farther, first_rows, last_rows,
    )


def beside_third(z, gain, back, part, earlier, from_near, from_over, mine_near, mine_over,
                 cell0, cell1, base):
    base[...] = (-CENTRE * gain) * part[...] - back * earlier[...]
    add_cells(
        z,
        gain * dot(cell0[...], part[: z.nodes, :].astype(BF16)),
        gain * dot(cell1[...], part[z.last :, :].astype(BF16)),
        base,
    )
    first, last = face_rows(z, from_near, from_over)
    blocks = take(from_near, from_over, (slice(z.l_term, z.later), slice(0, z.span)))
    mine = take(mine_near, mine_over, (slice(z.l_face, z.l_term), slice(None)))
    base[: z.face, :] += gain * dot(blocks[0], mine[0])[: z.face] - back * first
    base[z.end :, :] += gain * dot(blocks[1], mine[1])[: z.face] - back * last


def third_kernel(
    z, gain, share,
    base, own_coeffs, from_near, from_over, from_far, from_farther,
    cell0, cell1, spread0, spread1, edge0, edge1, occupation,
    out, density,
):
    s = whole_coeffs(z, own_coeffs, from_near, from_over, from_far, from_farther)
    before, own, after = s
    term0, term1 = neighbour_terms(z, s, from_near, from_over, cell0, cell1, spread0, spread1)
    out[...] = base[...]
    add_cells(z, gain * term0, gain * term1, out)
    first, last = face_rows(z, from_near, from_over)
    terms = take(from_near, from_over, (slice(z.l_term, z.later), slice(None)))
    left, right = (v.astype(F32)[: z.face] for v in terms)
    left += dot(edge0[...], twice(own, before))[z.shift : z.shift + z.face]
    right += dot(edge1[...], twice(own, after))[: z.face]
    out[: z.face, :] += gain * (left - CENTRE * first)
    out[z.end :, :] += gain * (right - CENTRE * last)
    result = out[...]
    density[...] = lax.dot_general(
        occupation[...] * share,
        result * result,
        (((1,), (1,)), ((), ())),
        preferred_element_type=F32,
        precision=lax.Precision.HIGHEST,
    )


def call(kernel, outs, scratch, *args, hbm=0, megabytes=32, order=()):
    vmem = pl.BlockSpec(memory_space=pltpu.VMEM)
    far = pl.BlockSpec(memory_space=pltpu.HBM)
    inputs = len(args)
    order = list(order) + [i for i in range(inputs) if i not in order]
    where = [order.index(i) for i in range(inputs)]

    def ordered(*refs):
        kernel(*(refs[i] for i in where), *refs[inputs:])

    return pl.pallas_call(
        ordered,
        out_shape=[pltpu.VMEM(s, t) for s, t in outs],
        in_specs=[far] * hbm + [vmem] * (inputs - hbm),
        out_specs=[vmem] * len(outs),
        scratch_shapes=scratch,
        compiler_params=pltpu.CompilerParams(vmem_limit_bytes=megabytes * 1024 * 1024),
    )(*(args[i] for i in order))


def body(filter_input, cell_table, cell_type, atom_center, proj_values, coupling, occupation):
    cells = cell_type.shape[0]
    atoms, projectors = proj_values.shape[0], proj_values.shape[2]
    rows, states = filter_input.shape
    z = Sizes(rows, cells, cell_table.shape[1], atoms, projectors)
    c, n = z.coef, z.nodes
    devices, groups = lax.axis_size("cells"), lax.axis_size("states")

    def exchanged(array, even_by):
        pairs = [
            (i, (i + (even_by if i % 2 == 0 else -even_by)) % devices) for i in range(devices)
        ]
        return lax.ppermute(array, "cells", pairs)

    def exchange_all(near, over, far, farther):
        far = exchanged(far, -2)
        near = exchanged(near, 1)
        farther = exchanged(farther, 2)
        over = exchanged(over, -1)
        return near, over, far, farther

    half_width = (upper_edge - lower_edge) / 2.0
    scale = half_width / (ground_edge - CENTRE)
    twice_inverse = 2.0 / scale
    gains, backs = [scale / half_width], [0.0]
    for _ in range(STEPS - 1):
        scale_next = 1.0 / (twice_inverse - scale)
        gains.append(2.0 * scale_next / half_width)
        backs.append(scale * scale_next)
        scale = scale_next

    field, share = ((rows, states), F32), ((c, states), F32)
    scratch = pltpu.VMEM(*field)
    x0, near, over, own0, own1, own_share = call(
        functools.partial(pack_kernel, z),
        [((rows, states), BF16)]
        + [((z.first, states), BF16)] * 2
        + [((c, n), BF16)] * 2
        + [share],
        [
            pltpu.SMEM(atom_center.shape, jnp.int32),
            pltpu.VMEM(proj_values.shape, BF16),
            scratch,
            pltpu.SemaphoreType.DMA((3,)),
        ],
        atom_center, filter_input, proj_values,
        hbm=3,
        megabytes=56,
    )
    from_over, from_near = exchanged(over, -1), exchanged(near, 1)

    onehot = (cell_type[:, None] == jnp.arange(cell_table.shape[0])[None, :]).astype(BF16)
    matrices = jnp.einsum("ct,tij->cij", onehot, cell_table, preferred_element_type=F32)
    matrices = matrices.astype(BF16)
    cell0, cell1 = matrices[0], matrices[-1]
    base, mix_high, mix_low, end_rows = call(
        functools.partial(beside_first, z),
        [field] + [((2 * c, 2 * c), BF16)] * 2 + [((z.pad_face, n), BF16)],
        [scratch],
        coupling, x0, cell0, cell1,
    )

    coeffs = ((3 * c, states), F32)
    messages = [((z.later, states), BF16)] * 2 + [((c, states), BF16)] * 2
    faces = [pltpu.VMEM((z.span, states), F32)] * 2
    part1, own_coeffs, near, over, far, farther, rows0, rows1, spread0, spread1, face0, face1 = (
        call(
            functools.partial(first_kernel, z, gains[0]),
            [field, coeffs]
            + messages
            + [((2 * c, n), BF16)] * 2
            + [((n, 4 * c), BF16)] * 2
            + [((2 * c, LANES), BF16)] * 2,
            [scratch, pltpu.VMEM((2, z.chunks * LANES, states), F32), scratch] + faces,
            base, x0, own0, own1, own_share, near, over, from_near, from_over,
            cell0, mix_high, mix_low, end_rows,
            order=FIRST_ORDER,
        )
    )
    second = exchange_all(near, over, far, farther)
    base, edge0, edge1 = call(
        functools.partial(beside_second, z, gains[1], backs[1]),
        [field] + [((LANES, 4 * c), BF16)] * 2,
        [],
        part1, x0, cell0, cell1, mix_high, mix_low, face0, face1,
    )
    part2, own_coeffs, near, over, far, farther = call(
        functools.partial(second_kernel, z, gains[1]),
        [field, coeffs] + messages,
        faces,
        base, own_coeffs, *second,
        cell0, cell1, end_rows, rows0, rows1, spread0, spread1, face0, face1,
        order=ORDER,
    )
    third = exchange_all(near, over, far, farther)
    (base,) = call(
        functools.partial(beside_third, z, gains[2], backs[2]),
        [field],
        [],
        part2, part1, second[0], second[1], near, over, cell0, cell1,
    )
    filtered, density = call(
        functools.partial(third_kernel, z, gains[2], 1.0 / (states * groups)),
        [field, ((1, rows), F32)],
        [],
        base, own_coeffs, *third,
        cell0, cell1, spread0, spread1, edge0, edge1, occupation[None, :],
        order=ORDER,
    )
    return filtered, total(density, groups)[0]


def total(density, groups):
    if groups & (groups - 1):
        return lax.psum(density, "states")
    step = 1
    while step < groups:
        density += lax.ppermute(density, "states", [(i, i ^ step) for i in range(groups)])
        step *= 2
    return density


def solution(mesh):
    in_specs = (
        P("cells", "states"),
        P(),
        P("cells"),
        P("cells"),
        P("cells", None, None, None),
        P(),
        P("states"),
    )
    out_specs = (P("cells", "states"), P("cells"))
    return jax.shard_map(body, mesh=mesh, in_specs=in_specs, out_specs=out_specs, check_vma=False)
```

```python
import functools

import jax
import jax.numpy as jnp
from jax import lax
from jax.experimental import pallas as pl
from jax.experimental.pallas import tpu as pltpu
from jax.sharding import PartitionSpec as P

STEPS = 3
LANES = 128
ROWS16 = 16

lower_edge = 4.0
upper_edge = 12.0
ground_edge = -2.0

F32 = jnp.float32
BF16 = jnp.bfloat16


def up16(n):
    return -(-n // ROWS16) * ROWS16


def down16(n):
    return n // ROWS16 * ROWS16


class Sizes:
    def __init__(self, node_rows, cells, cell_nodes, atoms, projectors):
        self.rows = node_rows
        self.nodes = cell_nodes
        self.stride = (node_rows - cell_nodes) // (cells - 1)
        self.face = cell_nodes - self.stride
        self.last = node_rows - cell_nodes
        self.end = node_rows - self.face
        self.atoms = atoms
        self.proj = projectors
        self.coef = atoms * projectors
        self.chunks = -(-cell_nodes // LANES)
        self.tail = cell_nodes - (self.chunks - 1) * LANES
        self.shift = self.stride - (self.chunks - 1) * LANES
        self.m_coef = self.chunks * self.coef
        self.m_rows = self.m_coef + self.coef
        self.right_lo, self.right_hi = down16(self.last), up16(self.end)
        self.left_lo, self.left_hi = down16(self.face), up16(cell_nodes)
        self.halo = max(self.right_hi - self.right_lo, self.left_hi - self.left_lo)
        self.first = self.m_rows + self.halo
        self.pad_face = up16(self.face)
        self.span = up16(self.shift + self.face)
        self.l_face = 2 * self.coef
        self.l_term = self.l_face + self.span
        self.later = self.l_term + self.pad_face


def dot(a, b):
    return jnp.dot(a, b, preferred_element_type=F32)


def exact_dot(a, b):
    return jnp.dot(a, b, preferred_element_type=F32, precision=lax.Precision.HIGHEST)


def halves(v):
    high = v.astype(BF16)
    return high, (v - high.astype(F32)).astype(BF16)


def is_even():
    return lax.rem(lax.axis_index("cells"), 2) == 0


def put(near, over, at, to_right, to_left):
    even = is_even()
    near[at] = jnp.where(even, to_right, to_left)
    over[at] = jnp.where(even, to_left, to_right)


def take(near, over, at):
    even = is_even()
    a, b = near[at], over[at]
    return jnp.where(even, b, a), jnp.where(even, a, b)


def pack_kernel(
    z, center_hbm, x0_hbm, proj_hbm, x0, near, over, own0, own1, coeffs, center, proj, xs, sems
):
    copies = [
        pltpu.make_async_copy(x0_hbm, x0, sems.at[0]),
        pltpu.make_async_copy(center_hbm, center, sems.at[1]),
        pltpu.make_async_copy(proj_hbm, proj, sems.at[2]),
    ]
    for copy in copies:
        copy.start()
    copies[0].wait()
    xs[...] = x0[...].astype(F32)
    put(
        near, over, (slice(z.m_rows, z.first), slice(None)),
        x0[z.right_lo : z.right_lo + z.halo, :], x0[z.left_lo : z.left_lo + z.halo, :],
    )
    copies[1].wait()
    copies[2].wait()
    on0, on1, reach_left, reach_right = [], [], [], []
    for a in range(z.atoms):
        low = center[a] == 0
        before, here, after = proj[a, 0], proj[a, 1], proj[a, 2]
        none = jnp.zeros_like(before)
        on0.append(jnp.where(low, here, before))
        on1.append(jnp.where(low, after, here))
        reach_left.append(jnp.where(low, before, none))
        reach_right.append(jnp.where(low, none, after))
    on0, on1, reach_left, reach_right = (
        jnp.concatenate(v, axis=0) for v in (on0, on1, reach_left, reach_right)
    )
    k_last = (z.chunks - 1) * LANES

    def last_chunk(v):
        zeros = jnp.zeros((z.coef, LANES - z.tail), BF16)
        return jnp.concatenate([v[:, k_last:], zeros], axis=1).astype(F32)

    lane = lax.broadcasted_iota(jnp.int32, (z.coef, LANES), 1)
    on_first = lane < z.face
    on_last = (lane >= z.shift) & (lane < z.shift + z.face)

    def to_last(v):
        return pltpu.roll(jnp.where(on_first, v, 0.0), z.shift, 1)

    def to_first(v):
        return pltpu.roll(jnp.where(on_last, v, 0.0), LANES - z.shift, 1)

    own_first, own_last = on0[:, :LANES].astype(F32), last_chunk(on1)
    far_first, far_last = reach_right[:, :LANES].astype(F32), last_chunk(reach_left)
    own0[:, :LANES] = (own_first + to_first(far_last)).astype(BF16)
    own0[:, LANES:] = on0[:, LANES:]
    own1[:, :k_last] = on1[:, :k_last]
    own1[:, k_last:] = (own_last + to_last(far_first)).astype(BF16)[:, : z.tail]
    for k in range(z.chunks):
        cols = slice(k * LANES, (k + 1) * LANES)
        to_right, to_left = reach_right[:, cols], reach_left[:, cols]
        if k == z.chunks - 1:
            to_right = last_chunk(reach_right).astype(BF16)
            to_left = (far_last + to_last(own_first)).astype(BF16)
        if k == 0:
            to_right = (far_first + to_first(own_last)).astype(BF16)
        put(near, over, (slice(k * z.coef, (k + 1) * z.coef), slice(None)), to_right, to_left)
    row = lax.broadcasted_iota(jnp.int32, (z.nodes, 1), 0)
    x_first, x_last = xs[: z.nodes, :], xs[z.last :, :]
    first = dot(own0[...], x_first.astype(BF16))
    last = dot(own1[...], x_last.astype(BF16))
    inner_first = dot(own0[...], jnp.where(row < z.face, 0.0, x_first).astype(BF16))
    inner_last = dot(own1[...], jnp.where(row >= z.stride, 0.0, x_last).astype(BF16))
    coeffs[...] = inner_first + inner_last
    put(
        near, over, (slice(z.m_coef, z.m_rows), slice(None)),
        (first + inner_last).astype(BF16), (inner_first + last).astype(BF16),
    )


def add_cells(z, term0, term1, out):
    out[: z.nodes, :] += term0
    out[z.last :, :] += term1


def face_scale(z):
    row = lax.broadcasted_iota(jnp.int32, (z.rows, 1), 0)
    return jnp.where((row < z.face) | (row >= z.end), 0.5, 1.0).astype(F32)


CENTRE = (upper_edge + lower_edge) / 2.0

FIRST_ORDER = (7, 8)
ORDER = (3, 2, 5, 4)


def twice(a, b):
    return jnp.concatenate([a, b, a, b], axis=0).astype(BF16)


def send_part(
    z, rows0, rows1, end0, end1, part, coeffs, near, over, far, farther, first, last
):
    c = z.coef
    last[...] = jnp.zeros_like(last)
    first[...] = jnp.zeros_like(first)
    last[: z.face, :] = part[z.end :, :]
    first[z.shift : z.shift + z.face, :] = part[: z.face, :]
    last_rows, first_rows = last[...].astype(BF16), first[...].astype(BF16)
    put(near, over, (slice(z.l_face, z.l_term), slice(None)), last_rows, first_rows)
    on0, on1 = part[: z.nodes, :].astype(BF16), part[z.last :, :].astype(BF16)
    s0, s1 = dot(rows0[...], on0), dot(rows1[...], on1)
    before, own, after = s0[c:], s0[:c] + s1[:c], s1[c:]
    coeffs[:c, :] = before
    coeffs[c : 2 * c, :] = own
    coeffs[2 * c :, :] = after
    before, own, after = before.astype(BF16), own.astype(BF16), after.astype(BF16)
    near[:c, :] = own
    over[:c, :] = own
    put(near, over, (slice(c, 2 * c), slice(None)), after, before)
    even = is_even()
    far[...] = jnp.where(even, before, after)
    farther[...] = jnp.where(even, after, before)
    if end0 is None:
        return
    put(
        near, over, (slice(z.l_term, z.later), slice(None)),
        dot(end1[...], on1).astype(BF16), dot(end0[: z.pad_face, :], on0).astype(BF16),
    )


def whole_coeffs(z, own_ref, near, over, far, farther):
    c = z.coef
    left, right = (v.astype(F32) for v in take(near, over, (slice(0, 2 * c), slice(None))))
    even = is_even()
    a, b = far[...], farther[...]
    far_left, far_right = jnp.where(even, b, a), jnp.where(even, a, b)
    before = own_ref[:c, :] + left[:c] + far_left.astype(F32)
    own = own_ref[c : 2 * c, :] + left[c:] + right[c:]
    after = own_ref[2 * c :, :] + right[:c] + far_right.astype(F32)
    return before, own, after


def face_rows(z, near, over):
    first, last = take(near, over, (slice(z.l_face, z.l_term), slice(None)))
    return (
        first.astype(F32)[: z.face],
        last.astype(F32)[z.shift : z.shift + z.face],
    )


def neighbour_terms(z, s, near, over, cell0, cell1, spread0, spread1):
    before, own, after = s
    first, last = take(near, over, (slice(z.l_face, z.l_term), slice(None)))
    k_last = (z.chunks - 1) * LANES
    term0 = dot(spread0[...], twice(own, before)) + dot(cell0[:, : z.span], first)
    term1 = dot(spread1[...], twice(own, after)) + dot(cell1[:, k_last:], last[: z.tail])
    return term0, term1


def beside_first(
    z, coupling, x0, cell0, cell1, base, mix_high, mix_low, end_rows, xs
):
    xs[...] = x0[...].astype(F32)
    base[...] = (-CENTRE) * (face_scale(z) * xs[...])
    add_cells(
        z, dot(cell0[...], x0[: z.nodes, :]), dot(cell1[...], xs[z.last :, :].astype(BF16)), base
    )
    size = 2 * z.coef
    row = lax.broadcasted_iota(jnp.int32, (size, z.proj), 0)
    col = lax.broadcasted_iota(jnp.int32, (size, z.proj), 1)
    pick = jnp.where(lax.rem(row, z.proj) == col, 1.0, 0.0).astype(F32)
    wide = exact_dot(pick, coupling[...])
    wide = lax.dot_general(
        wide, pick, (((1,), (1,)), ((), ())),
        preferred_element_type=F32, precision=lax.Precision.HIGHEST,
    )
    row = lax.broadcasted_iota(jnp.int32, (size, size), 0)
    col = lax.broadcasted_iota(jnp.int32, (size, size), 1)
    mix = jnp.where(lax.div(row, z.proj) == lax.div(col, z.proj), wide, 0.0)
    mix_high[...], mix_low[...] = halves(mix)
    end_rows[...] = jnp.zeros_like(end_rows)
    end_rows[: z.face, :] = cell1[...].astype(F32)[z.stride :].astype(BF16)


def mixed(a, mix_high, mix_low):
    high, low = halves(dot(a, mix_high[...]) + dot(a, mix_low[...]))
    return jnp.concatenate([high, low], axis=1)


def first_kernel(
    z, gain,
    base, x0, own0, own1, own_coeffs, mine_near, mine_over, from_near, from_over,
    cell0, mix_high, mix_low, end_rows,
    part, coeffs, near, over, far, farther,
    rows0, rows1, spread0, spread1, inner0, inner1,
    xs, ext, terms, first, last,
):
    c, k_last = z.coef, (z.chunks - 1) * LANES
    xs[...] = x0[...].astype(F32)
    rows0[:c, :] = own0[...]
    rows1[:c, :] = own1[...]
    for k in range(z.chunks):
        width = LANES if k < z.chunks - 1 else z.tail
        cols = slice(k * LANES, k * LANES + width)
        rows0[c:, cols], rows1[c:, cols] = take(
            from_near, from_over, (slice(k * c, (k + 1) * c), slice(0, width))
        )
    spread0[...] = mixed(rows0[...].T, mix_high, mix_low)
    spread1[...] = mixed(rows1[...].T, mix_high, mix_low)
    inner0[...] = spread0[...]
    inner1[...] = spread1[...]
    top = inner0[: z.pad_face, :]
    row = lax.broadcasted_iota(jnp.int32, top.shape, 0)
    lane = lax.broadcasted_iota(jnp.int32, top.shape, 1)
    shared = (row < z.face) & (lax.rem(lane, 2 * c) >= c)
    inner0[: z.pad_face, :] = jnp.where(shared, 0.0, top.astype(F32)).astype(BF16)
    start = down16(z.stride)
    top = inner1[start:, :]
    row = lax.broadcasted_iota(jnp.int32, top.shape, 0)
    lane = lax.broadcasted_iota(jnp.int32, top.shape, 1)
    shared = (row >= z.stride - start) & (lax.rem(lane, 2 * c) >= c)
    inner1[start:, :] = jnp.where(shared, 0.0, top.astype(F32)).astype(BF16)
    chunks = [
        take(mine_near, mine_over, (slice(k * c, (k + 1) * c), slice(None)))
        for k in range(z.chunks)
    ]
    ext[:, z.nodes :, :] = jnp.zeros((2, ext.shape[1] - z.nodes, ext.shape[2]), F32)
    halo = take(from_near, from_over, (slice(z.m_rows, z.first), slice(None)))
    skip = z.last - z.right_lo
    ext[0, : z.stride, :] = halo[0].astype(F32)[skip : skip + z.stride]
    ext[0, z.stride : z.nodes, :] = xs[: z.face, :]
    skip = z.face - z.left_lo
    ext[1, : z.face, :] = xs[z.end :, :]
    ext[1, z.face : z.nodes, :] = halo[1].astype(F32)[skip : skip + z.stride]
    own = own_coeffs[...]
    for k in range(z.chunks):
        cols = slice(k * LANES, (k + 1) * LANES)
        own += dot(chunks[k][0], ext[0, cols, :].astype(BF16))
        own += dot(chunks[k][1], ext[1, cols, :].astype(BF16))
    before, after = take(from_near, from_over, (slice(z.m_coef, z.m_rows), slice(None)))
    before = before.astype(F32) + dot(rows0[c:, :], x0[: z.nodes, :])
    after = after.astype(F32) + dot(rows1[c:, :], xs[z.last :, :].astype(BF16))
    terms[...] = base[...]
    add_cells(
        z, dot(inner0[...], twice(own, before)), dot(inner1[...], twice(own, after)), terms
    )
    part[...] = terms[...] * gain
    send_part(
        z, rows0, rows1, None, None,
        part, coeffs, near, over, far, farther, first, last,
    )
    wide = jnp.zeros((z.pad_face, LANES - z.tail), BF16)
    put(
        near, over, (slice(z.l_term, z.later), slice(None)),
        jnp.concatenate([end_rows[:, k_last:], wide], axis=1), cell0[: z.pad_face, :LANES],
    )


def beside_second(z, gain, back, part, x0, cell0, cell1, base):
    scale = face_scale(z)
    base[...] = scale * ((-CENTRE * gain) * part[...] - back * x0[...].astype(F32))
    add_cells(
        z,
        gain * dot(cell0[...], part[: z.nodes, :].astype(BF16)),
        gain * dot(cell1[...], part[z.last :, :].astype(BF16)),
        base,
    )


def second_kernel(
    z, gain,
    base, own_coeffs, from_near, from_over, from_far, from_farther,
    cell0, cell1, end_rows, rows0, rows1, inner0, inner1,
    part, coeffs, near, over, far, farther,
    first_rows, last_rows,
):
    s = whole_coeffs(z, own_coeffs, from_near, from_over, from_far, from_farther)
    term0, term1 = neighbour_terms(z, s, from_near, from_over, cell0, cell1, inner0, inner1)
    part[...] = base[...]
    add_cells(z, gain * term0, gain * term1, part)
    first, last = face_rows(z, from_near, from_over)
    part[: z.face, :] -= (0.5 * CENTRE * gain) * first
    part[z.end :, :] -= (0.5 * CENTRE * gain) * last
    send_part(
        z, rows0, rows1, cell0, end_rows,
        part, coeffs, near, over, far, farther, first_rows, last_rows,
    )


def beside_third(z, gain, back, part, earlier, from_near, from_over, mine_near, mine_over,
                 cell0, cell1, base):
    base[...] = (-CENTRE * gain) * part[...] - back * earlier[...]
    add_cells(
        z,
        gain * dot(cell0[...], part[: z.nodes, :].astype(BF16)),
        gain * dot(cell1[...], part[z.last :, :].astype(BF16)),
        base,
    )
    first, last = face_rows(z, from_near, from_over)
    blocks = take(from_near, from_over, (slice(z.l_term, z.later), slice(0, z.span)))
    mine = take(mine_near, mine_over, (slice(z.l_face, z.l_term), slice(None)))
    base[: z.face, :] += gain * dot(blocks[0], mine[0])[: z.face] - back * first
    base[z.end :, :] += gain * dot(blocks[1], mine[1])[: z.face] - back * last


def third_kernel(
    z, gain, share,
    base, own_coeffs, from_near, from_over, from_far, from_farther,
    cell0, cell1, spread0, spread1, occupation,
    out, density,
):
    s = whole_coeffs(z, own_coeffs, from_near, from_over, from_far, from_farther)
    term0, term1 = neighbour_terms(z, s, from_near, from_over, cell0, cell1, spread0, spread1)
    out[...] = base[...]
    add_cells(z, gain * term0, gain * term1, out)
    first, last = face_rows(z, from_near, from_over)
    terms = take(from_near, from_over, (slice(z.l_term, z.later), slice(None)))
    left, right = (v.astype(F32)[: z.face] for v in terms)
    out[: z.face, :] += gain * (left - CENTRE * first)
    out[z.end :, :] += gain * (right - CENTRE * last)
    result = out[...]
    density[...] = lax.dot_general(
        occupation[...] * share,
        result * result,
        (((1,), (1,)), ((), ())),
        preferred_element_type=F32,
        precision=lax.Precision.HIGHEST,
    )


def call(kernel, outs, scratch, *args, hbm=0, megabytes=32, order=()):
    vmem = pl.BlockSpec(memory_space=pltpu.VMEM)
    far = pl.BlockSpec(memory_space=pltpu.HBM)
    inputs = len(args)
    order = list(order) + [i for i in range(inputs) if i not in order]
    where = [order.index(i) for i in range(inputs)]

    def ordered(*refs):
        kernel(*(refs[i] for i in where), *refs[inputs:])

    return pl.pallas_call(
        ordered,
        out_shape=[pltpu.VMEM(s, t) for s, t in outs],
        in_specs=[far] * hbm + [vmem] * (inputs - hbm),
        out_specs=[vmem] * len(outs),
        scratch_shapes=scratch,
        compiler_params=pltpu.CompilerParams(vmem_limit_bytes=megabytes * 1024 * 1024),
    )(*(args[i] for i in order))


def body(filter_input, cell_table, cell_type, atom_center, proj_values, coupling, occupation):
    cells = cell_type.shape[0]
    atoms, projectors = proj_values.shape[0], proj_values.shape[2]
    rows, states = filter_input.shape
    z = Sizes(rows, cells, cell_table.shape[1], atoms, projectors)
    c, n = z.coef, z.nodes
    devices, groups = lax.axis_size("cells"), lax.axis_size("states")

    def exchanged(array, even_by):
        pairs = [
            (i, (i + (even_by if i % 2 == 0 else -even_by)) % devices) for i in range(devices)
        ]
        return lax.ppermute(array, "cells", pairs)

    def exchange_all(near, over, far, farther):
        far = exchanged(far, -2)
        near = exchanged(near, 1)
        farther = exchanged(farther, 2)
        over = exchanged(over, -1)
        return near, over, far, farther

    half_width = (upper_edge - lower_edge) / 2.0
    scale = half_width / (ground_edge - CENTRE)
    twice_inverse = 2.0 / scale
    gains, backs = [scale / half_width], [0.0]
    for _ in range(STEPS - 1):
        scale_next = 1.0 / (twice_inverse - scale)
        gains.append(2.0 * scale_next / half_width)
        backs.append(scale * scale_next)
        scale = scale_next

    field, share = ((rows, states), F32), ((c, states), F32)
    scratch = pltpu.VMEM(*field)
    x0, near, over, own0, own1, own_share = call(
        functools.partial(pack_kernel, z),
        [((rows, states), BF16)]
        + [((z.first, states), BF16)] * 2
        + [((c, n), BF16)] * 2
        + [share],
        [
            pltpu.SMEM(atom_center.shape, jnp.int32),
            pltpu.VMEM(proj_values.shape, BF16),
            scratch,
            pltpu.SemaphoreType.DMA((3,)),
        ],
        atom_center, filter_input, proj_values,
        hbm=3,
        megabytes=56,
    )
    from_over, from_near = exchanged(over, -1), exchanged(near, 1)

    onehot = (cell_type[:, None] == jnp.arange(cell_table.shape[0])[None, :]).astype(BF16)
    matrices = jnp.einsum("ct,tij->cij", onehot, cell_table, preferred_element_type=F32)
    matrices = matrices.astype(BF16)
    cell0, cell1 = matrices[0], matrices[-1]
    base, mix_high, mix_low, end_rows = call(
        functools.partial(beside_first, z),
        [field] + [((2 * c, 2 * c), BF16)] * 2 + [((z.pad_face, n), BF16)],
        [scratch],
        coupling, x0, cell0, cell1,
    )

    coeffs = ((3 * c, states), F32)
    messages = [((z.later, states), BF16)] * 2 + [((c, states), BF16)] * 2
    faces = [pltpu.VMEM((z.span, states), F32)] * 2
    part1, own_coeffs, near, over, far, farther, rows0, rows1, spread0, spread1, inner0, inner1 = (
        call(
            functools.partial(first_kernel, z, gains[0]),
            [field, coeffs]
            + messages
            + [((2 * c, n), BF16)] * 2
            + [((n, 4 * c), BF16)] * 4,
            [scratch, pltpu.VMEM((2, z.chunks * LANES, states), F32), scratch] + faces,
            base, x0, own0, own1, own_share, near, over, from_near, from_over,
            cell0, mix_high, mix_low, end_rows,
            order=FIRST_ORDER,
        )
    )
    second = exchange_all(near, over, far, farther)
    (base,) = call(
        functools.partial(beside_second, z, gains[1], backs[1]),
        [field],
        [],
        part1, x0, cell0, cell1,
    )
    part2, own_coeffs, near, over, far, farther = call(
        functools.partial(second_kernel, z, gains[1]),
        [field, coeffs] + messages,
        faces,
        base, own_coeffs, *second,
        cell0, cell1, end_rows, rows0, rows1, inner0, inner1,
        order=ORDER,
    )
    third = exchange_all(near, over, far, farther)
    (base,) = call(
        functools.partial(beside_third, z, gains[2], backs[2]),
        [field],
        [],
        part2, part1, second[0], second[1], near, over, cell0, cell1,
    )
    filtered, density = call(
        functools.partial(third_kernel, z, gains[2], 1.0 / (states * groups)),
        [field, ((1, rows), F32)],
        [],
        base, own_coeffs, *third,
        cell0, cell1, spread0, spread1, occupation[None, :],
        order=ORDER,
    )
    return filtered, total(density, groups)[0]


def total(density, groups):
    if groups & (groups - 1):
        return lax.psum(density, "states")

    def partner(array, by):
        return lax.ppermute(array, "states", [(i, i ^ by) for i in range(groups)])

    if groups <= 4:
        return sum((partner(density, by) for by in range(1, groups)), density)
    step = 1
    while step < groups:
        density += partner(density, step)
        step *= 2
    return density


def solution(mesh):
    in_specs = (
        P("cells", "states"),
        P(),
        P("cells"),
        P("cells"),
        P("cells", None, None, None),
        P(),
        P("states"),
    )
    out_specs = (P("cells", "states"), P("cells"))
    return jax.shard_map(body, mesh=mesh, in_specs=in_specs, out_specs=out_specs, check_vma=False)
```

```python
import functools

import jax
import jax.numpy as jnp
from jax import lax
from jax.experimental import pallas as pl
from jax.experimental.pallas import tpu as pltpu
from jax.sharding import PartitionSpec as P

STEPS = 3
LANES = 128
ROWS16 = 16

lower_edge = 4.0
upper_edge = 12.0
ground_edge = -2.0

F32 = jnp.float32
BF16 = jnp.bfloat16


def up16(n):
    return -(-n // ROWS16) * ROWS16


def down16(n):
    return n // ROWS16 * ROWS16


class Sizes:
    def __init__(self, node_rows, cells, cell_nodes, atoms, projectors):
        self.rows = node_rows
        self.nodes = cell_nodes
        self.stride = (node_rows - cell_nodes) // (cells - 1)
        self.face = cell_nodes - self.stride
        self.last = node_rows - cell_nodes
        self.end = node_rows - self.face
        self.atoms = atoms
        self.proj = projectors
        self.coef = atoms * projectors
        self.chunks = -(-cell_nodes // LANES)
        self.tail = cell_nodes - (self.chunks - 1) * LANES
        self.shift = self.stride - (self.chunks - 1) * LANES
        self.m_coef = self.chunks * self.coef
        self.m_rows = self.m_coef + self.coef
        self.right_lo, self.right_hi = down16(self.last), up16(self.end)
        self.left_lo, self.left_hi = down16(self.face), up16(cell_nodes)
        self.halo = max(self.right_hi - self.right_lo, self.left_hi - self.left_lo)
        self.first = self.m_rows + self.halo
        self.pad_face = up16(self.face)
        self.span = up16(self.shift + self.face)
        self.l_face = 2 * self.coef
        self.l_term = self.l_face + self.pad_face
        self.l_block = self.l_term + self.pad_face
        self.later = self.l_block + self.pad_face
        self.second = {
            "near": self.l_term + 2 * ROWS16,
            "over": self.l_term,
            "far": self.coef,
            "farther": self.l_term + ROWS16,
        }


def dot(a, b):
    return jnp.dot(a, b, preferred_element_type=F32)


def exact_dot(a, b):
    return jnp.dot(a, b, preferred_element_type=F32, precision=lax.Precision.HIGHEST)


def halves(v):
    high = v.astype(BF16)
    return high, (v - high.astype(F32)).astype(BF16)


def is_even():
    return lax.rem(lax.axis_index("cells"), 2) == 0


def put(near, over, at, to_right, to_left):
    even = is_even()
    near[at] = jnp.where(even, to_right, to_left)
    over[at] = jnp.where(even, to_left, to_right)


def take(near, over, at):
    even = is_even()
    a, b = near[at], over[at]
    return jnp.where(even, b, a), jnp.where(even, a, b)


def pack_kernel(
    z, center_hbm, x0_hbm, proj_hbm, x0, near, over, own0, own1, coeffs, center, proj, xs, sems
):
    copies = [
        pltpu.make_async_copy(proj_hbm, proj, sems.at[0]),
        pltpu.make_async_copy(center_hbm, center, sems.at[1]),
        pltpu.make_async_copy(x0_hbm, x0, sems.at[2]),
    ]
    for copy in copies:
        copy.start()
    copies[0].wait()
    copies[1].wait()
    on0, on1, reach_left, reach_right = [], [], [], []
    for a in range(z.atoms):
        low = center[a] == 0
        before, here, after = proj[a, 0], proj[a, 1], proj[a, 2]
        none = jnp.zeros_like(before)
        on0.append(jnp.where(low, here, before))
        on1.append(jnp.where(low, after, here))
        reach_left.append(jnp.where(low, before, none))
        reach_right.append(jnp.where(low, none, after))
    on0, on1, reach_left, reach_right = (
        jnp.concatenate(v, axis=0) for v in (on0, on1, reach_left, reach_right)
    )
    k_last = (z.chunks - 1) * LANES

    def last_chunk(v):
        zeros = jnp.zeros((z.coef, LANES - z.tail), BF16)
        return jnp.concatenate([v[:, k_last:], zeros], axis=1).astype(F32)

    lane = lax.broadcasted_iota(jnp.int32, (z.coef, LANES), 1)
    on_first = lane < z.face
    on_last = (lane >= z.shift) & (lane < z.shift + z.face)

    def to_last(v):
        return pltpu.roll(jnp.where(on_first, v, 0.0), z.shift, 1)

    def to_first(v):
        return pltpu.roll(jnp.where(on_last, v, 0.0), LANES - z.shift, 1)

    own_first, own_last = on0[:, :LANES].astype(F32), last_chunk(on1)
    far_first, far_last = reach_right[:, :LANES].astype(F32), last_chunk(reach_left)
    own0[:, :LANES] = (own_first + to_first(far_last)).astype(BF16)
    own0[:, LANES:] = on0[:, LANES:]
    own1[:, :k_last] = on1[:, :k_last]
    own1[:, k_last:] = (own_last + to_last(far_first)).astype(BF16)[:, : z.tail]
    for k in range(z.chunks):
        cols = slice(k * LANES, (k + 1) * LANES)
        to_right, to_left = reach_right[:, cols], reach_left[:, cols]
        if k == z.chunks - 1:
            to_right = last_chunk(reach_right).astype(BF16)
            to_left = (far_last + to_last(own_first)).astype(BF16)
        if k == 0:
            to_right = (far_first + to_first(own_last)).astype(BF16)
        put(near, over, (slice(k * z.coef, (k + 1) * z.coef), slice(None)), to_right, to_left)
    copies[2].wait()
    xs[...] = x0[...].astype(F32)
    put(
        near, over, (slice(z.m_rows, z.first), slice(None)),
        x0[z.right_lo : z.right_lo + z.halo, :], x0[z.left_lo : z.left_lo + z.halo, :],
    )
    row = lax.broadcasted_iota(jnp.int32, (z.nodes, 1), 0)
    x_first, x_last = xs[: z.nodes, :], xs[z.last :, :]
    states = x0.shape[1]
    x_first = jnp.concatenate([x_first, jnp.where(row < z.face, 0.0, x_first)], axis=1)
    x_last = jnp.concatenate([x_last, jnp.where(row >= z.stride, 0.0, x_last)], axis=1)
    on_first = dot(own0[...], x_first.astype(BF16))
    on_last = dot(own1[...], x_last.astype(BF16))
    first, inner_first = on_first[:, :states], on_first[:, states:]
    last, inner_last = on_last[:, :states], on_last[:, states:]
    coeffs[...] = inner_first + inner_last
    put(
        near, over, (slice(z.m_coef, z.m_rows), slice(None)),
        (first + inner_last).astype(BF16), (inner_first + last).astype(BF16),
    )


def add_cells(z, term0, term1, out):
    out[: z.nodes, :] += term0
    out[z.last :, :] += term1


def face_scale(z):
    row = lax.broadcasted_iota(jnp.int32, (z.rows, 1), 0)
    return jnp.where((row < z.face) | (row >= z.end), 0.5, 1.0).astype(F32)


CENTRE = (upper_edge + lower_edge) / 2.0

FIRST_ORDER = (7, 8)
ORDER = (3, 2, 5, 4)


def twice(a, b):
    return jnp.concatenate([a, b, a, b], axis=0).astype(BF16)


def send_part(z, rows0, rows1, part, coeffs, near, over, far, farther, faces):
    c = z.coef
    faces[...] = jnp.zeros_like(faces)
    faces[0, : z.face, :] = part[: z.face, :]
    faces[1, : z.face, :] = part[z.end :, :]
    put(
        near, over, (slice(z.l_face, z.l_term), slice(None)),
        faces[1].astype(BF16), faces[0].astype(BF16),
    )
    on0, on1 = part[: z.nodes, :].astype(BF16), part[z.last :, :].astype(BF16)
    s0, s1 = dot(rows0[...], on0), dot(rows1[...], on1)
    before, own, after = s0[c:], s0[:c] + s1[:c], s1[c:]
    coeffs[:c, :] = before
    coeffs[c : 2 * c, :] = own
    coeffs[2 * c :, :] = after
    before, own, after = before.astype(BF16), own.astype(BF16), after.astype(BF16)
    near[:c, :] = own
    over[:c, :] = own
    put(near, over, (slice(c, 2 * c), slice(None)), after, before)
    even = is_even()
    far[:c, :] = jnp.where(even, before, after)
    farther[:c, :] = jnp.where(even, after, before)
    return on0, on1


def whole_coeffs(z, own_ref, near, over, far, farther):
    c = z.coef
    left, right = (v.astype(F32) for v in take(near, over, (slice(0, 2 * c), slice(None))))
    even = is_even()
    a, b = far[:c, :], farther[:c, :]
    far_left, far_right = jnp.where(even, b, a), jnp.where(even, a, b)
    before = own_ref[:c, :] + left[:c] + far_left.astype(F32)
    own = own_ref[c : 2 * c, :] + left[c:] + right[c:]
    after = own_ref[2 * c :, :] + right[:c] + far_right.astype(F32)
    return before, own, after


def face_rows(z, near, over):
    first, last = take(near, over, (slice(z.l_face, z.l_term), slice(None)))
    return first.astype(F32)[: z.face], last.astype(F32)[: z.face]


def at_last(z, rows, pad):
    pad[...] = jnp.zeros_like(pad)
    pad[z.shift : z.shift + z.face, :] = rows
    return pad[...].astype(BF16)


def neighbour_terms(z, s, faces, cell0, cell1, spread0, spread1, pad):
    before, own, after = s
    first, last = faces
    k_last = (z.chunks - 1) * LANES
    pad[0, : z.face, :] = first
    pad[0, z.face :, :] = jnp.zeros((z.span - z.face, first.shape[1]), F32)
    first = pad[0].astype(BF16)[: z.pad_face]
    last = at_last(z, last, pad.at[1])[: z.tail]
    term0 = dot(spread0[...], twice(own, before)) + dot(cell0[:, : z.pad_face], first)
    term1 = dot(spread1[...], twice(own, after)) + dot(cell1[:, k_last:], last)
    return term0, term1


def beside_first(
    z, coupling, x0, cell0, cell1, base, mix_high, mix_low, end_rows, xs
):
    xs[...] = x0[...].astype(F32)
    base[...] = (-CENTRE) * (face_scale(z) * xs[...])
    add_cells(
        z, dot(cell0[...], x0[: z.nodes, :]), dot(cell1[...], xs[z.last :, :].astype(BF16)), base
    )
    size = 2 * z.coef
    row = lax.broadcasted_iota(jnp.int32, (size, z.proj), 0)
    col = lax.broadcasted_iota(jnp.int32, (size, z.proj), 1)
    pick = jnp.where(lax.rem(row, z.proj) == col, 1.0, 0.0).astype(F32)
    wide = exact_dot(pick, coupling[...])
    wide = lax.dot_general(
        wide, pick, (((1,), (1,)), ((), ())),
        preferred_element_type=F32, precision=lax.Precision.HIGHEST,
    )
    row = lax.broadcasted_iota(jnp.int32, (size, size), 0)
    col = lax.broadcasted_iota(jnp.int32, (size, size), 1)
    mix = jnp.where(lax.div(row, z.proj) == lax.div(col, z.proj), wide, 0.0)
    mix_high[...], mix_low[...] = halves(mix)
    end_rows[...] = jnp.zeros_like(end_rows)
    end_rows[: z.face, :] = cell1[...].astype(F32)[z.stride :].astype(BF16)


def mixed(a, mix_high, mix_low):
    high, low = halves(dot(a, mix_high[...]) + dot(a, mix_low[...]))
    return jnp.concatenate([high, low], axis=1)


def first_kernel(
    z, gain,
    base, x0, own0, own1, own_coeffs, mine_near, mine_over, from_near, from_over,
    mix_high, mix_low,
    part, coeffs, near, over, far, farther,
    rows0, rows1, spread0, spread1, inner0, inner1,
    xs, ext, terms, faces,
):
    c = z.coef
    xs[...] = x0[...].astype(F32)
    rows0[:c, :] = own0[...]
    rows1[:c, :] = own1[...]
    for k in range(z.chunks):
        width = LANES if k < z.chunks - 1 else z.tail
        cols = slice(k * LANES, k * LANES + width)
        rows0[c:, cols], rows1[c:, cols] = take(
            from_near, from_over, (slice(k * c, (k + 1) * c), slice(0, width))
        )
    spread0[...] = mixed(rows0[...].T, mix_high, mix_low)
    spread1[...] = mixed(rows1[...].T, mix_high, mix_low)
    inner0[...] = spread0[...]
    inner1[...] = spread1[...]
    top = inner0[: z.pad_face, :]
    row = lax.broadcasted_iota(jnp.int32, top.shape, 0)
    lane = lax.broadcasted_iota(jnp.int32, top.shape, 1)
    shared = (row < z.face) & (lax.rem(lane, 2 * c) >= c)
    inner0[: z.pad_face, :] = jnp.where(shared, 0.0, top.astype(F32)).astype(BF16)
    start = down16(z.stride)
    top = inner1[start:, :]
    row = lax.broadcasted_iota(jnp.int32, top.shape, 0)
    lane = lax.broadcasted_iota(jnp.int32, top.shape, 1)
    shared = (row >= z.stride - start) & (lax.rem(lane, 2 * c) >= c)
    inner1[start:, :] = jnp.where(shared, 0.0, top.astype(F32)).astype(BF16)
    chunks = [
        take(mine_near, mine_over, (slice(k * c, (k + 1) * c), slice(None)))
        for k in range(z.chunks)
    ]
    ext[:, z.nodes :, :] = jnp.zeros((2, ext.shape[1] - z.nodes, ext.shape[2]), F32)
    halo = take(from_near, from_over, (slice(z.m_rows, z.first), slice(None)))
    skip = z.last - z.right_lo
    ext[0, : z.stride, :] = halo[0].astype(F32)[skip : skip + z.stride]
    ext[0, z.stride : z.nodes, :] = xs[: z.face, :]
    skip = z.face - z.left_lo
    ext[1, : z.face, :] = xs[z.end :, :]
    ext[1, z.face : z.nodes, :] = halo[1].astype(F32)[skip : skip + z.stride]
    own = own_coeffs[...]
    for k in range(z.chunks):
        cols = slice(k * LANES, (k + 1) * LANES)
        own += dot(chunks[k][0], ext[0, cols, :].astype(BF16))
        own += dot(chunks[k][1], ext[1, cols, :].astype(BF16))
    before, after = take(from_near, from_over, (slice(z.m_coef, z.m_rows), slice(None)))
    before = before.astype(F32) + dot(rows0[c:, :], x0[: z.nodes, :])
    after = after.astype(F32) + dot(rows1[c:, :], xs[z.last :, :].astype(BF16))
    terms[...] = base[...]
    add_cells(
        z, dot(inner0[...], twice(own, before)), dot(inner1[...], twice(own, after)), terms
    )
    part[...] = terms[...] * gain
    send_part(z, rows0, rows1, part, coeffs, near, over, far, farther, faces)
    for message, used in ((near, z.l_term), (over, z.l_term), (far, c), (farther, c)):
        if message.shape[0] > used:
            message[used:, :] = jnp.zeros((message.shape[0] - used, message.shape[1]), BF16)


def beside_second(z, gain, back, part, x0, cell0, cell1, base):
    scale = face_scale(z)
    base[...] = scale * ((-CENTRE * gain) * part[...] - back * x0[...].astype(F32))
    add_cells(
        z,
        gain * dot(cell0[...], part[: z.nodes, :].astype(BF16)),
        gain * dot(cell1[...], part[z.last :, :].astype(BF16)),
        base,
    )


def second_kernel(
    z, gain,
    base, own_coeffs, from_near, from_over, from_far, from_farther,
    cell0, cell1, end_rows, rows0, rows1, inner0, inner1,
    part, coeffs, near, over, far, farther,
    edges, pad,
):
    s = whole_coeffs(z, own_coeffs, from_near, from_over, from_far, from_farther)
    first, last = face_rows(z, from_near, from_over)
    term0, term1 = neighbour_terms(z, s, (first, last), cell0, cell1, inner0, inner1, pad)
    part[...] = base[...]
    add_cells(z, gain * term0, gain * term1, part)
    part[: z.face, :] -= (0.5 * CENTRE * gain) * first
    part[z.end :, :] -= (0.5 * CENTRE * gain) * last
    on0, on1 = send_part(z, rows0, rows1, part, coeffs, near, over, far, farther, edges)
    put(
        near, over, (slice(z.l_term, z.l_block), slice(None)),
        dot(end_rows[...], on1).astype(BF16), dot(cell0[: z.pad_face, :], on0).astype(BF16),
    )
    k_last = (z.chunks - 1) * LANES
    wide = jnp.zeros((z.pad_face, LANES - z.tail), BF16)
    put(
        near, over, (slice(z.l_block, z.later), slice(None)),
        jnp.concatenate([end_rows[:, k_last:], wide], axis=1), cell0[: z.pad_face, :LANES],
    )


def beside_third(z, gain, back, part, earlier, from_near, from_over, cell0, cell1, base):
    base[...] = (-CENTRE * gain) * part[...] - back * earlier[...]
    add_cells(
        z,
        gain * dot(cell0[...], part[: z.nodes, :].astype(BF16)),
        gain * dot(cell1[...], part[z.last :, :].astype(BF16)),
        base,
    )
    first, last = face_rows(z, from_near, from_over)
    base[: z.face, :] -= back * first
    base[z.end :, :] -= back * last


def third_kernel(
    z, gain, share,
    base, own_coeffs, from_near, from_over, from_far, from_farther,
    cell0, cell1, spread0, spread1, part, occupation,
    out, density,
    pad, mine,
):
    s = whole_coeffs(z, own_coeffs, from_near, from_over, from_far, from_farther)
    first, last = face_rows(z, from_near, from_over)
    term0, term1 = neighbour_terms(z, s, (first, last), cell0, cell1, spread0, spread1, pad)
    out[...] = base[...]
    add_cells(z, gain * term0, gain * term1, out)
    terms = take(from_near, from_over, (slice(z.l_term, z.l_block), slice(None)))
    blocks = take(from_near, from_over, (slice(z.l_block, z.later), slice(None)))
    own_first = at_last(z, part[: z.face, :], mine.at[0])
    mine[1, : z.face, :] = part[z.end :, :]
    mine[1, z.face :, :] = jnp.zeros((z.span - z.face, part.shape[1]), F32)
    own_last = mine[1].astype(BF16)[: z.pad_face]
    left = (terms[0].astype(F32) + dot(blocks[0][:, : z.span], own_first))[: z.face]
    right = (terms[1].astype(F32) + dot(blocks[1][:, : z.pad_face], own_last))[: z.face]
    out[: z.face, :] += gain * (left - CENTRE * first)
    out[z.end :, :] += gain * (right - CENTRE * last)
    result = out[...]
    weights = jnp.concatenate(halves(occupation[...] * share), axis=0)
    rows = lax.dot_general(
        weights,
        (result * result).astype(BF16),
        (((1,), (1,)), ((), ())),
        preferred_element_type=F32,
    )
    density[...] = rows[:1] + rows[1:]


def call(kernel, outs, scratch, *args, hbm=0, megabytes=32, order=()):
    vmem = pl.BlockSpec(memory_space=pltpu.VMEM)
    far = pl.BlockSpec(memory_space=pltpu.HBM)
    inputs = len(args)
    order = list(order) + [i for i in range(inputs) if i not in order]
    where = [order.index(i) for i in range(inputs)]

    def ordered(*refs):
        kernel(*(refs[i] for i in where), *refs[inputs:])

    return pl.pallas_call(
        ordered,
        out_shape=[pltpu.VMEM(s, t) for s, t in outs],
        in_specs=[far] * hbm + [vmem] * (inputs - hbm),
        out_specs=[vmem] * len(outs),
        scratch_shapes=scratch,
        compiler_params=pltpu.CompilerParams(vmem_limit_bytes=megabytes * 1024 * 1024),
    )(*(args[i] for i in order))


def body(filter_input, cell_table, cell_type, atom_center, proj_values, coupling, occupation):
    cells = cell_type.shape[0]
    atoms, projectors = proj_values.shape[0], proj_values.shape[2]
    rows, states = filter_input.shape
    z = Sizes(rows, cells, cell_table.shape[1], atoms, projectors)
    c, n = z.coef, z.nodes
    devices, groups = lax.axis_size("cells"), lax.axis_size("states")

    def exchanged(array, even_by):
        pairs = [
            (i, (i + (even_by if i % 2 == 0 else -even_by)) % devices) for i in range(devices)
        ]
        return lax.ppermute(array, "cells", pairs)

    def exchange_all(near, over, far, farther):
        far = exchanged(far, -2)
        near = exchanged(near, 1)
        farther = exchanged(farther, 2)
        over = exchanged(over, -1)
        return near, over, far, farther

    half_width = (upper_edge - lower_edge) / 2.0
    scale = half_width / (ground_edge - CENTRE)
    twice_inverse = 2.0 / scale
    gains, backs = [scale / half_width], [0.0]
    for _ in range(STEPS - 1):
        scale_next = 1.0 / (twice_inverse - scale)
        gains.append(2.0 * scale_next / half_width)
        backs.append(scale * scale_next)
        scale = scale_next

    field, share = ((rows, states), F32), ((c, states), F32)
    scratch = pltpu.VMEM(*field)
    x0, near, over, own0, own1, own_share = call(
        functools.partial(pack_kernel, z),
        [((rows, states), BF16)]
        + [((z.first, states), BF16)] * 2
        + [((c, n), BF16)] * 2
        + [share],
        [
            pltpu.SMEM(atom_center.shape, jnp.int32),
            pltpu.VMEM(proj_values.shape, BF16),
            scratch,
            pltpu.SemaphoreType.DMA((3,)),
        ],
        atom_center, filter_input, proj_values,
        hbm=3,
        megabytes=56,
    )
    from_over, from_near = exchanged(over, -1), exchanged(near, 1)

    onehot = (cell_type[:, None] == jnp.arange(cell_table.shape[0])[None, :]).astype(BF16)
    matrices = jnp.einsum("ct,tij->cij", onehot, cell_table, preferred_element_type=F32)
    matrices = matrices.astype(BF16)
    cell0, cell1 = matrices[0], matrices[-1]
    base, mix_high, mix_low, end_rows = call(
        functools.partial(beside_first, z),
        [field] + [((2 * c, 2 * c), BF16)] * 2 + [((z.pad_face, n), BF16)],
        [scratch],
        coupling, x0, cell0, cell1,
    )

    coeffs = ((3 * c, states), F32)
    second_messages = [((n, states), BF16) for n in z.second.values()]
    third_messages = [((z.later, states), BF16)] * 2 + [((c, states), BF16)] * 2
    faces, pad = pltpu.VMEM((2, z.pad_face, states), F32), pltpu.VMEM((2, z.span, states), F32)
    part1, own_coeffs, near, over, far, farther, rows0, rows1, spread0, spread1, inner0, inner1 = (
        call(
            functools.partial(first_kernel, z, gains[0]),
            [field, coeffs]
            + second_messages
            + [((2 * c, n), BF16)] * 2
            + [((n, 4 * c), BF16)] * 4,
            [scratch, pltpu.VMEM((2, z.chunks * LANES, states), F32), scratch, faces],
            base, x0, own0, own1, own_share, near, over, from_near, from_over,
            mix_high, mix_low,
            order=FIRST_ORDER,
        )
    )
    second = exchange_all(near, over, far, farther)
    (base,) = call(
        functools.partial(beside_second, z, gains[1], backs[1]),
        [field],
        [],
        part1, x0, cell0, cell1,
    )
    part2, own_coeffs, near, over, far, farther = call(
        functools.partial(second_kernel, z, gains[1]),
        [field, coeffs] + third_messages,
        [faces, pad],
        base, own_coeffs, *second,
        cell0, cell1, end_rows, rows0, rows1, inner0, inner1,
        order=ORDER,
    )
    third = exchange_all(near, over, far, farther)
    (base,) = call(
        functools.partial(beside_third, z, gains[2], backs[2]),
        [field],
        [],
        part2, part1, second[0], second[1], cell0, cell1,
    )
    filtered, density = call(
        functools.partial(third_kernel, z, gains[2], 1.0 / (states * groups)),
        [field, ((1, rows), F32)],
        [pad, pad],
        base, own_coeffs, *third,
        cell0, cell1, spread0, spread1, part2, occupation[None, :],
        order=ORDER,
    )
    return filtered, total(density, groups)[0]


def total(density, groups):
    if groups & (groups - 1):
        return lax.psum(density, "states")

    def partner(array, by):
        return lax.ppermute(array, "states", [(i, i ^ by) for i in range(groups)])

    if groups <= 4:
        return sum((partner(density, by) for by in range(1, groups)), density)
    step = 1
    while step < groups:
        density += partner(density, step)
        step *= 2
    return density


def solution(mesh):
    in_specs = (
        P("cells", "states"),
        P(),
        P("cells"),
        P("cells"),
        P("cells", None, None, None),
        P(),
        P("states"),
    )
    out_specs = (P("cells", "states"), P("cells"))
    return jax.shard_map(body, mesh=mesh, in_specs=in_specs, out_specs=out_specs, check_vma=False)
```

```python
import functools

import jax
import jax.numpy as jnp
from jax import lax
from jax.experimental import pallas as pl
from jax.experimental.pallas import tpu as pltpu
from jax.sharding import PartitionSpec as P

STEPS = 3
LANES = 128
ROWS16 = 16

lower_edge = 4.0
upper_edge = 12.0
ground_edge = -2.0

F32 = jnp.float32
BF16 = jnp.bfloat16


def up16(n):
    return -(-n // ROWS16) * ROWS16


def down16(n):
    return n // ROWS16 * ROWS16


class Sizes:
    def __init__(self, node_rows, cells, cell_nodes, atoms, projectors):
        self.rows = node_rows
        self.nodes = cell_nodes
        self.stride = (node_rows - cell_nodes) // (cells - 1)
        self.face = cell_nodes - self.stride
        self.last = node_rows - cell_nodes
        self.end = node_rows - self.face
        self.atoms = atoms
        self.proj = projectors
        self.coef = atoms * projectors
        self.chunks = -(-cell_nodes // LANES)
        self.tail = cell_nodes - (self.chunks - 1) * LANES
        self.shift = self.stride - (self.chunks - 1) * LANES
        self.m_coef = self.chunks * self.coef
        self.m_rows = self.m_coef + self.coef
        self.right_lo, self.right_hi = down16(self.last), up16(self.end)
        self.left_lo, self.left_hi = down16(self.face), up16(cell_nodes)
        self.halo = max(self.right_hi - self.right_lo, self.left_hi - self.left_lo)
        self.first = self.m_rows + self.halo
        self.pad_face = up16(self.face)
        self.span = up16(self.shift + self.face)
        self.l_face = 2 * self.coef
        self.l_term = self.l_face + self.pad_face
        self.l_block = self.l_term + self.pad_face
        self.later = self.l_block + self.pad_face
        self.second = {
            "near": self.l_term + 2 * ROWS16,
            "over": self.l_term,
            "far": self.coef,
            "farther": self.l_term + ROWS16,
        }


def dot(a, b):
    return jnp.dot(a, b, preferred_element_type=F32)


def exact_dot(a, b):
    return jnp.dot(a, b, preferred_element_type=F32, precision=lax.Precision.HIGHEST)


def halves(v):
    high = v.astype(BF16)
    return high, (v - high.astype(F32)).astype(BF16)


def is_even():
    return lax.rem(lax.axis_index("cells"), 2) == 0


def put(near, over, at, to_right, to_left):
    even = is_even()
    near[at] = jnp.where(even, to_right, to_left)
    over[at] = jnp.where(even, to_left, to_right)


def take(near, over, at):
    even = is_even()
    a, b = near[at], over[at]
    return jnp.where(even, b, a), jnp.where(even, a, b)


def pack_kernel(
    z, center_hbm, x0_hbm, proj_hbm, x0, near, over, own0, own1, coeffs, center, proj, xs, sems
):
    copies = [
        pltpu.make_async_copy(proj_hbm, proj, sems.at[0]),
        pltpu.make_async_copy(center_hbm, center, sems.at[1]),
        pltpu.make_async_copy(x0_hbm, x0, sems.at[2]),
    ]
    for copy in copies:
        copy.start()
    copies[0].wait()
    copies[1].wait()
    on0, on1, reach_left, reach_right = [], [], [], []
    for a in range(z.atoms):
        low = center[a] == 0
        before, here, after = proj[a, 0], proj[a, 1], proj[a, 2]
        none = jnp.zeros_like(before)
        on0.append(jnp.where(low, here, before))
        on1.append(jnp.where(low, after, here))
        reach_left.append(jnp.where(low, before, none))
        reach_right.append(jnp.where(low, none, after))
    on0, on1, reach_left, reach_right = (
        jnp.concatenate(v, axis=0) for v in (on0, on1, reach_left, reach_right)
    )
    k_last = (z.chunks - 1) * LANES

    def last_chunk(v):
        zeros = jnp.zeros((z.coef, LANES - z.tail), BF16)
        return jnp.concatenate([v[:, k_last:], zeros], axis=1).astype(F32)

    lane = lax.broadcasted_iota(jnp.int32, (z.coef, LANES), 1)
    on_first = lane < z.face
    on_last = (lane >= z.shift) & (lane < z.shift + z.face)

    def to_last(v):
        return pltpu.roll(jnp.where(on_first, v, 0.0), z.shift, 1)

    def to_first(v):
        return pltpu.roll(jnp.where(on_last, v, 0.0), LANES - z.shift, 1)

    own_first, own_last = on0[:, :LANES].astype(F32), last_chunk(on1)
    far_first, far_last = reach_right[:, :LANES].astype(F32), last_chunk(reach_left)
    own0[:, :LANES] = (own_first + to_first(far_last)).astype(BF16)
    own0[:, LANES:] = on0[:, LANES:]
    own1[:, :k_last] = on1[:, :k_last]
    own1[:, k_last:] = (own_last + to_last(far_first)).astype(BF16)[:, : z.tail]
    for k in range(z.chunks):
        cols = slice(k * LANES, (k + 1) * LANES)
        to_right, to_left = reach_right[:, cols], reach_left[:, cols]
        if k == z.chunks - 1:
            to_right = last_chunk(reach_right).astype(BF16)
            to_left = (far_last + to_last(own_first)).astype(BF16)
        if k == 0:
            to_right = (far_first + to_first(own_last)).astype(BF16)
        put(near, over, (slice(k * z.coef, (k + 1) * z.coef), slice(None)), to_right, to_left)
    copies[2].wait()
    xs[...] = x0[...].astype(F32)
    put(
        near, over, (slice(z.m_rows, z.first), slice(None)),
        x0[z.right_lo : z.right_lo + z.halo, :], x0[z.left_lo : z.left_lo + z.halo, :],
    )
    row = lax.broadcasted_iota(jnp.int32, (z.nodes, 1), 0)
    x_first, x_last = xs[: z.nodes, :], xs[z.last :, :]
    states = x0.shape[1]
    x_first = jnp.concatenate([x_first, jnp.where(row < z.face, 0.0, x_first)], axis=1)
    x_last = jnp.concatenate([x_last, jnp.where(row >= z.stride, 0.0, x_last)], axis=1)
    on_first = dot(own0[...], x_first.astype(BF16))
    on_last = dot(own1[...], x_last.astype(BF16))
    first, inner_first = on_first[:, :states], on_first[:, states:]
    last, inner_last = on_last[:, :states], on_last[:, states:]
    coeffs[...] = first + last
    put(
        near, over, (slice(z.m_coef, z.m_rows), slice(None)),
        (first + inner_last).astype(BF16), (inner_first + last).astype(BF16),
    )


def add_cells(z, term0, term1, out):
    out[: z.nodes, :] += term0
    out[z.last :, :] += term1


def face_scale(z):
    row = lax.broadcasted_iota(jnp.int32, (z.rows, 1), 0)
    return jnp.where((row < z.face) | (row >= z.end), 0.5, 1.0).astype(F32)


CENTRE = (upper_edge + lower_edge) / 2.0

FIRST_ORDER = (6, 7)
ORDER = (3, 2, 5, 4)


def twice(a, b):
    return jnp.concatenate([a, b, a, b], axis=0).astype(BF16)


def send_part(z, rows0, rows1, part, coeffs, near, over, far, farther, faces):
    c = z.coef
    faces[...] = jnp.zeros_like(faces)
    faces[0, : z.face, :] = part[: z.face, :]
    faces[1, : z.face, :] = part[z.end :, :]
    put(
        near, over, (slice(z.l_face, z.l_term), slice(None)),
        faces[1].astype(BF16), faces[0].astype(BF16),
    )
    on0, on1 = part[: z.nodes, :].astype(BF16), part[z.last :, :].astype(BF16)
    s0, s1 = dot(rows0[...], on0), dot(rows1[...], on1)
    before, own, after = s0[c:], s0[:c] + s1[:c], s1[c:]
    coeffs[:c, :] = before
    coeffs[c : 2 * c, :] = own
    coeffs[2 * c :, :] = after
    before, own, after = before.astype(BF16), own.astype(BF16), after.astype(BF16)
    near[:c, :] = own
    over[:c, :] = own
    put(near, over, (slice(c, 2 * c), slice(None)), after, before)
    even = is_even()
    far[:c, :] = jnp.where(even, before, after)
    farther[:c, :] = jnp.where(even, after, before)
    return on0, on1


def whole_coeffs(z, own_ref, near, over, far, farther):
    c = z.coef
    left, right = (v.astype(F32) for v in take(near, over, (slice(0, 2 * c), slice(None))))
    even = is_even()
    a, b = far[:c, :], farther[:c, :]
    far_left, far_right = jnp.where(even, b, a), jnp.where(even, a, b)
    before = own_ref[:c, :] + left[:c] + far_left.astype(F32)
    own = own_ref[c : 2 * c, :] + left[c:] + right[c:]
    after = own_ref[2 * c :, :] + right[:c] + far_right.astype(F32)
    return before, own, after


def face_rows(z, near, over):
    first, last = take(near, over, (slice(z.l_face, z.l_term), slice(None)))
    return first.astype(F32)[: z.face], last.astype(F32)[: z.face]


def at_last(z, rows, pad):
    pad[...] = jnp.zeros_like(pad)
    pad[z.shift : z.shift + z.face, :] = rows
    return pad[...].astype(BF16)


def neighbour_terms(z, s, faces, cell0, cell1, spread0, spread1, pad):
    before, own, after = s
    first, last = faces
    k_last = (z.chunks - 1) * LANES
    pad[0, : z.face, :] = first
    pad[0, z.face :, :] = jnp.zeros((z.span - z.face, first.shape[1]), F32)
    first = pad[0].astype(BF16)[: z.pad_face]
    last = at_last(z, last, pad.at[1])[: z.tail]
    term0 = dot(spread0[...], twice(own, before)) + dot(cell0[:, : z.pad_face], first)
    term1 = dot(spread1[...], twice(own, after)) + dot(cell1[:, k_last:], last)
    return term0, term1


def beside_first(
    z, coupling, x0, cell0, cell1, mine_near, mine_over, base, mix, end_rows, outer, xs
):
    xs[...] = x0[...].astype(F32)
    base[...] = (-CENTRE) * (face_scale(z) * xs[...])
    add_cells(
        z, dot(cell0[...], x0[: z.nodes, :]), dot(cell1[...], xs[z.last :, :].astype(BF16)), base
    )
    size = 2 * z.coef
    row = lax.broadcasted_iota(jnp.int32, (size, z.proj), 0)
    col = lax.broadcasted_iota(jnp.int32, (size, z.proj), 1)
    pick = jnp.where(lax.rem(row, z.proj) == col, 1.0, 0.0).astype(F32)
    wide = exact_dot(pick, coupling[...])
    wide = lax.dot_general(
        wide, pick, (((1,), (1,)), ((), ())),
        preferred_element_type=F32, precision=lax.Precision.HIGHEST,
    )
    row = lax.broadcasted_iota(jnp.int32, (size, size), 0)
    col = lax.broadcasted_iota(jnp.int32, (size, size), 1)
    wide = jnp.where(lax.div(row, z.proj) == lax.div(col, z.proj), wide, 0.0)
    mix[...] = jnp.concatenate(halves(wide), axis=1)
    node = lax.broadcasted_iota(jnp.int32, (LANES, z.halo), 0)
    place = lax.broadcasted_iota(jnp.int32, (LANES, z.halo), 1)
    left, right = jnp.zeros((z.coef, z.halo), F32), jnp.zeros((z.coef, z.halo), F32)
    for k in range(z.chunks):
        rows = (slice(k * z.coef, (k + 1) * z.coef), slice(None))
        to_left, to_right = take(mine_near, mine_over, rows)
        at = node + k * LANES
        low = (place == at + (z.last - z.right_lo)) & (at < z.stride)
        high = (place == at - z.left_lo) & (at >= z.face) & (at < z.nodes)
        left += dot(to_left, jnp.where(low, 1.0, 0.0).astype(BF16))
        right += dot(to_right, jnp.where(high, 1.0, 0.0).astype(BF16))
    outer[: z.coef, :] = left.astype(BF16)
    outer[z.coef :, :] = right.astype(BF16)
    end_rows[...] = jnp.zeros_like(end_rows)
    end_rows[: z.face, :] = cell1[...].astype(F32)[z.stride :].astype(BF16)


def mixed(a, mix):
    width = a.shape[1]
    product = dot(a, mix[...])
    return jnp.concatenate(halves(product[:, :width] + product[:, width:]), axis=1)


def leave_out(z, spread0, spread1):
    start = down16(z.stride)
    for ref, rows in ((spread0, slice(0, z.pad_face)), (spread1, slice(start, z.nodes))):
        part = ref[rows, :].astype(F32)
        node = lax.broadcasted_iota(jnp.int32, part.shape, 0) + rows.start
        lane = lax.broadcasted_iota(jnp.int32, part.shape, 1)
        face = (node < z.face) if rows.start == 0 else (node >= z.stride)
        shared = face & (lax.rem(lane, 2 * z.coef) >= z.coef)
        ref[rows, :] = jnp.where(shared, 0.0, part).astype(BF16)


def first_kernel(
    z, gain,
    base, x0, own0, own1, own_coeffs, outer, from_near, from_over, mix,
    part, coeffs, near, over, far, farther,
    rows0, rows1,
    xs, terms, faces, flat0, flat1,
):
    c = z.coef
    xs[...] = x0[...].astype(F32)
    rows0[:c, :] = own0[...]
    rows1[:c, :] = own1[...]
    for k in range(z.chunks):
        width = LANES if k < z.chunks - 1 else z.tail
        cols = slice(k * LANES, k * LANES + width)
        rows0[c:, cols], rows1[c:, cols] = take(
            from_near, from_over, (slice(k * c, (k + 1) * c), slice(0, width))
        )
    flat0[...], flat1[...] = rows0[...].T, rows1[...].T
    leave_out(z, flat0, flat1)
    left, right = take(from_near, from_over, (slice(z.m_rows, z.first), slice(None)))
    own = own_coeffs[...] + dot(outer[:c, :], left) + dot(outer[c:, :], right)
    before, after = take(from_near, from_over, (slice(z.m_coef, z.m_rows), slice(None)))
    before = before.astype(F32) + dot(rows0[c:, :], x0[: z.nodes, :])
    after = after.astype(F32) + dot(rows1[c:, :], xs[z.last :, :].astype(BF16))
    terms[...] = base[...]
    high, low = halves(jnp.concatenate([before, own, after], axis=1))
    mix_high, mix_low = mix[:c, :c], mix[:c, 2 * c : 3 * c]
    weighted = dot(mix_high, high) + dot(mix_high, low) + dot(mix_low, high)
    weighted = weighted.astype(BF16)
    n = before.shape[1]
    before, own, after = (weighted[:, i * n : (i + 1) * n] for i in range(3))
    add_cells(
        z,
        dot(flat0[...], jnp.concatenate([own, before], axis=0)),
        dot(flat1[...], jnp.concatenate([own, after], axis=0)),
        terms,
    )
    part[...] = terms[...] * gain
    send_part(z, rows0, rows1, part, coeffs, near, over, far, farther, faces)
    for message, used in ((near, z.l_term), (over, z.l_term), (far, c), (farther, c)):
        if message.shape[0] > used:
            message[used:, :] = jnp.zeros((message.shape[0] - used, message.shape[1]), BF16)


def beside_second(z, gain, back, part, x0, cell0, cell1, rows0, rows1, mix,
                  base, spread0, spread1, inner0, inner1):
    scale = face_scale(z)
    base[...] = scale * ((-CENTRE * gain) * part[...] - back * x0[...].astype(F32))
    add_cells(
        z,
        gain * dot(cell0[...], part[: z.nodes, :].astype(BF16)),
        gain * dot(cell1[...], part[z.last :, :].astype(BF16)),
        base,
    )
    spread0[...] = mixed(rows0[...].T, mix)
    spread1[...] = mixed(rows1[...].T, mix)
    inner0[...], inner1[...] = spread0[...], spread1[...]
    leave_out(z, inner0, inner1)


def second_kernel(
    z, gain,
    base, own_coeffs, from_near, from_over, from_far, from_farther,
    cell0, cell1, end_rows, rows0, rows1, inner0, inner1,
    part, coeffs, near, over, far, farther,
    edges, pad,
):
    s = whole_coeffs(z, own_coeffs, from_near, from_over, from_far, from_farther)
    first, last = face_rows(z, from_near, from_over)
    term0, term1 = neighbour_terms(z, s, (first, last), cell0, cell1, inner0, inner1, pad)
    part[...] = base[...]
    add_cells(z, gain * term0, gain * term1, part)
    part[: z.face, :] -= (0.5 * CENTRE * gain) * first
    part[z.end :, :] -= (0.5 * CENTRE * gain) * last
    on0, on1 = send_part(z, rows0, rows1, part, coeffs, near, over, far, farther, edges)
    put(
        near, over, (slice(z.l_term, z.l_block), slice(None)),
        dot(end_rows[...], on1).astype(BF16), dot(cell0[: z.pad_face, :], on0).astype(BF16),
    )
    k_last = (z.chunks - 1) * LANES
    wide = jnp.zeros((z.pad_face, LANES - z.tail), BF16)
    put(
        near, over, (slice(z.l_block, z.later), slice(None)),
        jnp.concatenate([end_rows[:, k_last:], wide], axis=1), cell0[: z.pad_face, :LANES],
    )


def beside_third(z, gain, back, part, earlier, from_near, from_over, cell0, cell1, base):
    base[...] = (-CENTRE * gain) * part[...] - back * earlier[...]
    add_cells(
        z,
        gain * dot(cell0[...], part[: z.nodes, :].astype(BF16)),
        gain * dot(cell1[...], part[z.last :, :].astype(BF16)),
        base,
    )
    first, last = face_rows(z, from_near, from_over)
    base[: z.face, :] -= back * first
    base[z.end :, :] -= back * last


def third_kernel(
    z, gain, share,
    base, own_coeffs, from_near, from_over, from_far, from_farther,
    cell0, cell1, spread0, spread1, part, occupation,
    out, density,
    pad, mine,
):
    s = whole_coeffs(z, own_coeffs, from_near, from_over, from_far, from_farther)
    first, last = face_rows(z, from_near, from_over)
    term0, term1 = neighbour_terms(z, s, (first, last), cell0, cell1, spread0, spread1, pad)
    out[...] = base[...]
    add_cells(z, gain * term0, gain * term1, out)
    terms = take(from_near, from_over, (slice(z.l_term, z.l_block), slice(None)))
    blocks = take(from_near, from_over, (slice(z.l_block, z.later), slice(None)))
    own_first = at_last(z, part[: z.face, :], mine.at[0])
    mine[1, : z.face, :] = part[z.end :, :]
    mine[1, z.face :, :] = jnp.zeros((z.span - z.face, part.shape[1]), F32)
    own_last = mine[1].astype(BF16)[: z.pad_face]
    left = (terms[0].astype(F32) + dot(blocks[0][:, : z.span], own_first))[: z.face]
    right = (terms[1].astype(F32) + dot(blocks[1][:, : z.pad_face], own_last))[: z.face]
    out[: z.face, :] += gain * (left - CENTRE * first)
    out[z.end :, :] += gain * (right - CENTRE * last)
    result = out[...]
    weights = jnp.concatenate(halves(occupation[...] * share), axis=0)
    rows = lax.dot_general(
        weights,
        (result * result).astype(BF16),
        (((1,), (1,)), ((), ())),
        preferred_element_type=F32,
    )
    density[...] = rows[:1] + rows[1:]


def call(kernel, outs, scratch, *args, hbm=0, megabytes=32, order=()):
    vmem = pl.BlockSpec(memory_space=pltpu.VMEM)
    far = pl.BlockSpec(memory_space=pltpu.HBM)
    inputs = len(args)
    order = list(order) + [i for i in range(inputs) if i not in order]
    where = [order.index(i) for i in range(inputs)]

    def ordered(*refs):
        kernel(*(refs[i] for i in where), *refs[inputs:])

    return pl.pallas_call(
        ordered,
        out_shape=[pltpu.VMEM(s, t) for s, t in outs],
        in_specs=[far] * hbm + [vmem] * (inputs - hbm),
        out_specs=[vmem] * len(outs),
        scratch_shapes=scratch,
        compiler_params=pltpu.CompilerParams(vmem_limit_bytes=megabytes * 1024 * 1024),
    )(*(args[i] for i in order))


def body(filter_input, cell_table, cell_type, atom_center, proj_values, coupling, occupation):
    cells = cell_type.shape[0]
    atoms, projectors = proj_values.shape[0], proj_values.shape[2]
    rows, states = filter_input.shape
    z = Sizes(rows, cells, cell_table.shape[1], atoms, projectors)
    c, n = z.coef, z.nodes
    devices, groups = lax.axis_size("cells"), lax.axis_size("states")

    def exchanged(array, even_by):
        pairs = [
            (i, (i + (even_by if i % 2 == 0 else -even_by)) % devices) for i in range(devices)
        ]
        return lax.ppermute(array, "cells", pairs)

    def exchange_all(near, over, far, farther):
        far = exchanged(far, -2)
        near = exchanged(near, 1)
        farther = exchanged(farther, 2)
        over = exchanged(over, -1)
        return near, over, far, farther

    half_width = (upper_edge - lower_edge) / 2.0
    scale = half_width / (ground_edge - CENTRE)
    twice_inverse = 2.0 / scale
    gains, backs = [scale / half_width], [0.0]
    for _ in range(STEPS - 1):
        scale_next = 1.0 / (twice_inverse - scale)
        gains.append(2.0 * scale_next / half_width)
        backs.append(scale * scale_next)
        scale = scale_next

    field, share = ((rows, states), F32), ((c, states), F32)
    scratch = pltpu.VMEM(*field)
    x0, near, over, own0, own1, own_share = call(
        functools.partial(pack_kernel, z),
        [((rows, states), BF16)]
        + [((z.first, states), BF16)] * 2
        + [((c, n), BF16)] * 2
        + [share],
        [
            pltpu.SMEM(atom_center.shape, jnp.int32),
            pltpu.VMEM(proj_values.shape, BF16),
            scratch,
            pltpu.SemaphoreType.DMA((3,)),
        ],
        atom_center, filter_input, proj_values,
        hbm=3,
        megabytes=56,
    )
    from_over, from_near = exchanged(over, -1), exchanged(near, 1)

    onehot = (cell_type[:, None] == jnp.arange(cell_table.shape[0])[None, :]).astype(BF16)
    matrices = jnp.einsum("ct,tij->cij", onehot, cell_table, preferred_element_type=F32)
    matrices = matrices.astype(BF16)
    cell0, cell1 = matrices[0], matrices[-1]
    base, mix, end_rows, outer = call(
        functools.partial(beside_first, z),
        [field, ((2 * c, 4 * c), BF16), ((z.pad_face, n), BF16), ((2 * c, z.halo), BF16)],
        [scratch],
        coupling, x0, cell0, cell1, near, over,
    )

    coeffs = ((3 * c, states), F32)
    second_messages = [((n, states), BF16) for n in z.second.values()]
    third_messages = [((z.later, states), BF16)] * 2 + [((c, states), BF16)] * 2
    faces, pad = pltpu.VMEM((2, z.pad_face, states), F32), pltpu.VMEM((2, z.span, states), F32)
    part1, own_coeffs, near, over, far, farther, rows0, rows1 = (
        call(
            functools.partial(first_kernel, z, gains[0]),
            [field, coeffs]
            + second_messages
            + [((2 * c, n), BF16)] * 2,
            [scratch, scratch, faces] + [pltpu.VMEM((n, 2 * c), BF16)] * 2,
            base, x0, own0, own1, own_share, outer, from_near, from_over, mix,
            order=FIRST_ORDER,
        )
    )
    second = exchange_all(near, over, far, farther)
    base, spread0, spread1, inner0, inner1 = call(
        functools.partial(beside_second, z, gains[1], backs[1]),
        [field] + [((n, 4 * c), BF16)] * 4,
        [],
        part1, x0, cell0, cell1, rows0, rows1, mix,
    )
    part2, own_coeffs, near, over, far, farther = call(
        functools.partial(second_kernel, z, gains[1]),
        [field, coeffs] + third_messages,
        [faces, pad],
        base, own_coeffs, *second,
        cell0, cell1, end_rows, rows0, rows1, inner0, inner1,
        order=ORDER,
    )
    third = exchange_all(near, over, far, farther)
    (base,) = call(
        functools.partial(beside_third, z, gains[2], backs[2]),
        [field],
        [],
        part2, part1, second[0], second[1], cell0, cell1,
    )
    filtered, density = call(
        functools.partial(third_kernel, z, gains[2], 1.0 / (states * groups)),
        [field, ((1, rows), F32)],
        [pad, pad],
        base, own_coeffs, *third,
        cell0, cell1, spread0, spread1, part2, occupation[None, :],
        order=ORDER,
    )
    return filtered, total(density, groups)[0]


def total(density, groups):
    if groups & (groups - 1):
        return lax.psum(density, "states")

    def partner(array, by):
        return lax.ppermute(array, "states", [(i, i ^ by) for i in range(groups)])

    if groups <= 4:
        return sum((partner(density, by) for by in range(1, groups)), density)
    step = 1
    while step < groups:
        density += partner(density, step)
        step *= 2
    return density


def solution(mesh):
    in_specs = (
        P("cells", "states"),
        P(),
        P("cells"),
        P("cells"),
        P("cells", None, None, None),
        P(),
        P("states"),
    )
    out_specs = (P("cells", "states"), P("cells"))
    return jax.shard_map(body, mesh=mesh, in_specs=in_specs, out_specs=out_specs, check_vma=False)
```

```python
import functools

import jax
import jax.numpy as jnp
from jax import lax
from jax.experimental import pallas as pl
from jax.experimental.pallas import tpu as pltpu
from jax.sharding import PartitionSpec as P

STEPS = 3
LANES = 128
ROWS16 = 16

lower_edge = 4.0
upper_edge = 12.0
ground_edge = -2.0

F32 = jnp.float32
BF16 = jnp.bfloat16


def up16(n):
    return -(-n // ROWS16) * ROWS16


def down16(n):
    return n // ROWS16 * ROWS16


class Sizes:
    def __init__(self, node_rows, cells, cell_nodes, atoms, projectors):
        self.rows = node_rows
        self.nodes = cell_nodes
        self.stride = (node_rows - cell_nodes) // (cells - 1)
        self.face = cell_nodes - self.stride
        self.last = node_rows - cell_nodes
        self.end = node_rows - self.face
        self.atoms = atoms
        self.proj = projectors
        self.coef = atoms * projectors
        self.chunks = -(-cell_nodes // LANES)
        self.tail = cell_nodes - (self.chunks - 1) * LANES
        self.shift = self.stride - (self.chunks - 1) * LANES
        self.m_coef = self.chunks * self.coef
        self.m_rows = self.m_coef + self.coef
        self.right_lo, self.right_hi = down16(self.last), up16(self.end)
        self.left_lo, self.left_hi = down16(self.face), up16(cell_nodes)
        self.halo = max(self.right_hi - self.right_lo, self.left_hi - self.left_lo)
        self.first = self.m_rows + self.halo
        self.pad_face = up16(self.face)
        self.span = up16(self.shift + self.face)
        self.l_face = 2 * self.coef
        self.l_term = self.l_face + self.pad_face
        self.l_block = self.l_term + self.pad_face
        self.later = self.l_block + self.pad_face
        self.second = {
            "near": self.l_term + 2 * ROWS16,
            "over": self.l_term,
            "far": self.coef,
            "farther": self.l_term + ROWS16,
        }


def dot(a, b):
    return jnp.dot(a, b, preferred_element_type=F32)


def exact_dot(a, b):
    return jnp.dot(a, b, preferred_element_type=F32, precision=lax.Precision.HIGHEST)


def halves(v):
    high = v.astype(BF16)
    return high, (v - high.astype(F32)).astype(BF16)


def is_even():
    return lax.rem(lax.axis_index("cells"), 2) == 0


def put(near, over, at, to_right, to_left):
    even = is_even()
    near[at] = jnp.where(even, to_right, to_left)
    over[at] = jnp.where(even, to_left, to_right)


def take(near, over, at):
    even = is_even()
    a, b = near[at], over[at]
    return jnp.where(even, b, a), jnp.where(even, a, b)


def pack_kernel(
    z, center_hbm, x0_hbm, proj_hbm, x0, near, over, own0, own1, center, proj, xs, sems
):
    copies = [
        pltpu.make_async_copy(proj_hbm, proj, sems.at[0]),
        pltpu.make_async_copy(center_hbm, center, sems.at[1]),
        pltpu.make_async_copy(x0_hbm, x0, sems.at[2]),
    ]
    for copy in copies:
        copy.start()
    copies[0].wait()
    copies[1].wait()
    on0, on1, reach_left, reach_right, is_low = [], [], [], [], []
    for a in range(z.atoms):
        low = center[a] == 0
        before, here, after = proj[a, 0], proj[a, 1], proj[a, 2]
        none = jnp.zeros_like(before)
        on0.append(jnp.where(low, here, before))
        on1.append(jnp.where(low, after, here))
        reach_left.append(jnp.where(low, before, none))
        reach_right.append(jnp.where(low, none, after))
        is_low.append(jnp.full((z.proj, LANES), jnp.where(low, 1.0, 0.0), F32))
    on0, on1, reach_left, reach_right, is_low = (
        jnp.concatenate(v, axis=0) for v in (on0, on1, reach_left, reach_right, is_low)
    )
    k_last = (z.chunks - 1) * LANES

    def last_chunk(v):
        zeros = jnp.zeros((z.coef, LANES - z.tail), BF16)
        return jnp.concatenate([v[:, k_last:], zeros], axis=1).astype(F32)

    lane = lax.broadcasted_iota(jnp.int32, (z.coef, LANES), 1)
    on_first = lane < z.face
    on_last = (lane >= z.shift) & (lane < z.shift + z.face)

    def to_last(v):
        return pltpu.roll(jnp.where(on_first, v, 0.0), z.shift, 1)

    def to_first(v):
        return pltpu.roll(jnp.where(on_last, v, 0.0), LANES - z.shift, 1)

    own_first, own_last = on0[:, :LANES].astype(F32), last_chunk(on1)
    far_first, far_last = reach_right[:, :LANES].astype(F32), last_chunk(reach_left)
    own0[:, :LANES] = (own_first + to_first(far_last)).astype(BF16)
    own0[:, LANES:] = on0[:, LANES:]
    own1[:, :k_last] = on1[:, :k_last]
    own1[:, k_last:] = (own_last + to_last(far_first)).astype(BF16)[:, : z.tail]
    for k in range(z.chunks):
        cols = slice(k * LANES, (k + 1) * LANES)
        to_right, to_left = reach_right[:, cols], reach_left[:, cols]
        if k == z.chunks - 1:
            to_right = last_chunk(reach_right).astype(BF16)
            to_left = (far_last + to_last(own_first)).astype(BF16)
        if k == 0:
            to_right = (far_first + to_first(own_last)).astype(BF16)
        put(near, over, (slice(k * z.coef, (k + 1) * z.coef), slice(None)), to_right, to_left)
    left_out = jnp.where(on_first & (is_low > 0.5), 0.0, own_first).astype(BF16)
    sent0 = jnp.concatenate([left_out, on0[:, LANES:]], axis=1)
    left_out = jnp.where(on_last & (is_low < 0.5), 0.0, own_last).astype(BF16)
    sent1 = jnp.concatenate([on1[:, :k_last], left_out[:, : z.tail]], axis=1)
    copies[2].wait()
    put(
        near, over, (slice(z.m_rows, z.first), slice(None)),
        x0[z.right_lo : z.right_lo + z.halo, :], x0[z.left_lo : z.left_lo + z.halo, :],
    )
    xs[z.right_lo :, :] = x0[z.right_lo :, :].astype(F32)
    sent = dot(sent0, x0[: z.nodes, :]) + dot(sent1, xs[z.last :, :].astype(BF16))
    sent = sent.astype(BF16)
    near[z.m_coef : z.m_rows, :] = sent
    over[z.m_coef : z.m_rows, :] = sent


def add_cells(z, term0, term1, out):
    out[: z.nodes, :] += term0
    out[z.last :, :] += term1


def face_scale(z):
    row = lax.broadcasted_iota(jnp.int32, (z.rows, 1), 0)
    return jnp.where((row < z.face) | (row >= z.end), 0.5, 1.0).astype(F32)


CENTRE = (upper_edge + lower_edge) / 2.0

FIRST_ORDER = (6, 7)
ORDER = (3, 2, 5, 4)


def twice(a, b):
    return jnp.concatenate([a, b, a, b], axis=0).astype(BF16)


def send_part(z, rows0, rows1, part, coeffs, near, over, far, farther, faces):
    c = z.coef
    faces[...] = jnp.zeros_like(faces)
    faces[0, : z.face, :] = part[: z.face, :]
    faces[1, : z.face, :] = part[z.end :, :]
    put(
        near, over, (slice(z.l_face, z.l_term), slice(None)),
        faces[1].astype(BF16), faces[0].astype(BF16),
    )
    on0, on1 = part[: z.nodes, :].astype(BF16), part[z.last :, :].astype(BF16)
    s0, s1 = dot(rows0[...], on0), dot(rows1[...], on1)
    before, own, after = s0[c:], s0[:c] + s1[:c], s1[c:]
    coeffs[:c, :] = before
    coeffs[c : 2 * c, :] = own
    coeffs[2 * c :, :] = after
    before, own, after = before.astype(BF16), own.astype(BF16), after.astype(BF16)
    near[:c, :] = own
    over[:c, :] = own
    put(near, over, (slice(c, 2 * c), slice(None)), after, before)
    even = is_even()
    far[:c, :] = jnp.where(even, before, after)
    farther[:c, :] = jnp.where(even, after, before)
    return on0, on1


def whole_coeffs(z, own_ref, near, over, far, farther):
    c = z.coef
    left, right = (v.astype(F32) for v in take(near, over, (slice(0, 2 * c), slice(None))))
    even = is_even()
    a, b = far[:c, :], farther[:c, :]
    far_left, far_right = jnp.where(even, b, a), jnp.where(even, a, b)
    before = own_ref[:c, :] + left[:c] + far_left.astype(F32)
    own = own_ref[c : 2 * c, :] + left[c:] + right[c:]
    after = own_ref[2 * c :, :] + right[:c] + far_right.astype(F32)
    return before, own, after


def face_rows(z, near, over):
    first, last = take(near, over, (slice(z.l_face, z.l_term), slice(None)))
    return first.astype(F32)[: z.face], last.astype(F32)[: z.face]


def at_last(z, rows, pad):
    pad[...] = jnp.zeros_like(pad)
    pad[z.shift : z.shift + z.face, :] = rows
    return pad[...].astype(BF16)


def neighbour_terms(z, s, faces, cell0, cell1, spread0, spread1, pad):
    before, own, after = s
    first, last = faces
    k_last = (z.chunks - 1) * LANES
    pad[0, : z.face, :] = first
    pad[0, z.face :, :] = jnp.zeros((z.span - z.face, first.shape[1]), F32)
    first = pad[0].astype(BF16)[: z.pad_face]
    last = at_last(z, last, pad.at[1])[: z.tail]
    term0 = dot(spread0[...], twice(own, before)) + dot(cell0[:, : z.pad_face], first)
    term1 = dot(spread1[...], twice(own, after)) + dot(cell1[:, k_last:], last)
    return term0, term1


def beside_first(
    z, coupling, x0, cell0, cell1, mine_near, mine_over, own0, own1,
    base, mix, end_rows, outer, coeffs, xs,
):
    xs[...] = x0[...].astype(F32)
    coeffs[...] = dot(own0[...], x0[: z.nodes, :]) + dot(own1[...], xs[z.last :, :].astype(BF16))
    base[...] = (-CENTRE) * (face_scale(z) * xs[...])
    add_cells(
        z, dot(cell0[...], x0[: z.nodes, :]), dot(cell1[...], xs[z.last :, :].astype(BF16)), base
    )
    size = 2 * z.coef
    row = lax.broadcasted_iota(jnp.int32, (size, z.proj), 0)
    col = lax.broadcasted_iota(jnp.int32, (size, z.proj), 1)
    pick = jnp.where(lax.rem(row, z.proj) == col, 1.0, 0.0).astype(F32)
    wide = exact_dot(pick, coupling[...])
    wide = lax.dot_general(
        wide, pick, (((1,), (1,)), ((), ())),
        preferred_element_type=F32, precision=lax.Precision.HIGHEST,
    )
    row = lax.broadcasted_iota(jnp.int32, (size, size), 0)
    col = lax.broadcasted_iota(jnp.int32, (size, size), 1)
    wide = jnp.where(lax.div(row, z.proj) == lax.div(col, z.proj), wide, 0.0)
    mix[...] = jnp.concatenate(halves(wide), axis=1)
    node = lax.broadcasted_iota(jnp.int32, (LANES, z.halo), 0)
    place = lax.broadcasted_iota(jnp.int32, (LANES, z.halo), 1)
    left, right = jnp.zeros((z.coef, z.halo), F32), jnp.zeros((z.coef, z.halo), F32)
    for k in range(z.chunks):
        rows = (slice(k * z.coef, (k + 1) * z.coef), slice(None))
        to_left, to_right = take(mine_near, mine_over, rows)
        at = node + k * LANES
        low = (place == at + (z.last - z.right_lo)) & (at < z.stride)
        high = (place == at - z.left_lo) & (at >= z.face) & (at < z.nodes)
        left += dot(to_left, jnp.where(low, 1.0, 0.0).astype(BF16))
        right += dot(to_right, jnp.where(high, 1.0, 0.0).astype(BF16))
    outer[: z.coef, :] = left.astype(BF16)
    outer[z.coef :, :] = right.astype(BF16)
    end_rows[...] = jnp.zeros_like(end_rows)
    end_rows[: z.face, :] = cell1[...].astype(F32)[z.stride :].astype(BF16)


def mixed(a, mix):
    width = a.shape[1]
    product = dot(a, mix[...])
    return jnp.concatenate(halves(product[:, :width] + product[:, width:]), axis=1)


def leave_out(z, spread0, spread1):
    start = down16(z.stride)
    for ref, rows in ((spread0, slice(0, z.pad_face)), (spread1, slice(start, z.nodes))):
        part = ref[rows, :].astype(F32)
        node = lax.broadcasted_iota(jnp.int32, part.shape, 0) + rows.start
        lane = lax.broadcasted_iota(jnp.int32, part.shape, 1)
        face = (node < z.face) if rows.start == 0 else (node >= z.stride)
        shared = face & (lax.rem(lane, 2 * z.coef) >= z.coef)
        ref[rows, :] = jnp.where(shared, 0.0, part).astype(BF16)


def first_kernel(
    z, gain,
    base, x0, own0, own1, own_coeffs, outer, from_near, from_over, mix,
    part, coeffs, near, over, far, farther,
    rows0, rows1,
    xs, terms, faces, flat0, flat1,
):
    c = z.coef
    xs[...] = x0[...].astype(F32)
    rows0[:c, :] = own0[...]
    rows1[:c, :] = own1[...]
    for k in range(z.chunks):
        width = LANES if k < z.chunks - 1 else z.tail
        cols = slice(k * LANES, k * LANES + width)
        rows0[c:, cols], rows1[c:, cols] = take(
            from_near, from_over, (slice(k * c, (k + 1) * c), slice(0, width))
        )
    flat0[...], flat1[...] = rows0[...].T, rows1[...].T
    leave_out(z, flat0, flat1)
    left, right = take(from_near, from_over, (slice(z.m_rows, z.first), slice(None)))
    own = own_coeffs[...] + dot(outer[:c, :], left) + dot(outer[c:, :], right)
    before, after = take(from_near, from_over, (slice(z.m_coef, z.m_rows), slice(None)))
    before = before.astype(F32) + dot(rows0[c:, :], x0[: z.nodes, :])
    after = after.astype(F32) + dot(rows1[c:, :], xs[z.last :, :].astype(BF16))
    terms[...] = base[...]
    high, low = halves(jnp.concatenate([before, own, after], axis=1))
    mix_high, mix_low = mix[:c, :c], mix[:c, 2 * c : 3 * c]
    weighted = dot(mix_high, high) + dot(mix_high, low) + dot(mix_low, high)
    weighted = weighted.astype(BF16)
    n = before.shape[1]
    before, own, after = (weighted[:, i * n : (i + 1) * n] for i in range(3))
    add_cells(
        z,
        dot(flat0[...], jnp.concatenate([own, before], axis=0)),
        dot(flat1[...], jnp.concatenate([own, after], axis=0)),
        terms,
    )
    part[...] = terms[...] * gain
    send_part(z, rows0, rows1, part, coeffs, near, over, far, farther, faces)
    for message, used in ((near, z.l_term), (over, z.l_term), (far, c), (farther, c)):
        if message.shape[0] > used:
            message[used:, :] = jnp.zeros((message.shape[0] - used, message.shape[1]), BF16)


def beside_second(z, gain, back, part, x0, cell0, cell1, rows0, rows1, mix,
                  base, spread0, spread1, inner0, inner1):
    scale = face_scale(z)
    base[...] = scale * ((-CENTRE * gain) * part[...] - back * x0[...].astype(F32))
    add_cells(
        z,
        gain * dot(cell0[...], part[: z.nodes, :].astype(BF16)),
        gain * dot(cell1[...], part[z.last :, :].astype(BF16)),
        base,
    )
    spread0[...] = mixed(rows0[...].T, mix)
    spread1[...] = mixed(rows1[...].T, mix)
    inner0[...], inner1[...] = spread0[...], spread1[...]
    leave_out(z, inner0, inner1)


def second_kernel(
    z, gain,
    base, own_coeffs, from_near, from_over, from_far, from_farther,
    cell0, cell1, end_rows, rows0, rows1, inner0, inner1,
    part, coeffs, near, over, far, farther,
    edges, pad,
):
    s = whole_coeffs(z, own_coeffs, from_near, from_over, from_far, from_farther)
    first, last = face_rows(z, from_near, from_over)
    term0, term1 = neighbour_terms(z, s, (first, last), cell0, cell1, inner0, inner1, pad)
    part[...] = base[...]
    add_cells(z, gain * term0, gain * term1, part)
    part[: z.face, :] -= (0.5 * CENTRE * gain) * first
    part[z.end :, :] -= (0.5 * CENTRE * gain) * last
    on0, on1 = send_part(z, rows0, rows1, part, coeffs, near, over, far, farther, edges)
    put(
        near, over, (slice(z.l_term, z.l_block), slice(None)),
        dot(end_rows[...], on1).astype(BF16), dot(cell0[: z.pad_face, :], on0).astype(BF16),
    )
    k_last = (z.chunks - 1) * LANES
    wide = jnp.zeros((z.pad_face, LANES - z.tail), BF16)
    put(
        near, over, (slice(z.l_block, z.later), slice(None)),
        jnp.concatenate([end_rows[:, k_last:], wide], axis=1), cell0[: z.pad_face, :LANES],
    )


def beside_third(z, gain, back, part, earlier, from_near, from_over, cell0, cell1, base):
    base[...] = (-CENTRE * gain) * part[...] - back * earlier[...]
    add_cells(
        z,
        gain * dot(cell0[...], part[: z.nodes, :].astype(BF16)),
        gain * dot(cell1[...], part[z.last :, :].astype(BF16)),
        base,
    )
    first, last = face_rows(z, from_near, from_over)
    base[: z.face, :] -= back * first
    base[z.end :, :] -= back * last


def third_kernel(
    z, gain, share,
    base, own_coeffs, from_near, from_over, from_far, from_farther,
    cell0, cell1, spread0, spread1, part, occupation,
    out, density,
    pad, mine,
):
    s = whole_coeffs(z, own_coeffs, from_near, from_over, from_far, from_farther)
    first, last = face_rows(z, from_near, from_over)
    term0, term1 = neighbour_terms(z, s, (first, last), cell0, cell1, spread0, spread1, pad)
    out[...] = base[...]
    add_cells(z, gain * term0, gain * term1, out)
    terms = take(from_near, from_over, (slice(z.l_term, z.l_block), slice(None)))
    blocks = take(from_near, from_over, (slice(z.l_block, z.later), slice(None)))
    own_first = at_last(z, part[: z.face, :], mine.at[0])
    mine[1, : z.face, :] = part[z.end :, :]
    mine[1, z.face :, :] = jnp.zeros((z.span - z.face, part.shape[1]), F32)
    own_last = mine[1].astype(BF16)[: z.pad_face]
    left = (terms[0].astype(F32) + dot(blocks[0][:, : z.span], own_first))[: z.face]
    right = (terms[1].astype(F32) + dot(blocks[1][:, : z.pad_face], own_last))[: z.face]
    out[: z.face, :] += gain * (left - CENTRE * first)
    out[z.end :, :] += gain * (right - CENTRE * last)
    result = out[...]
    weights = jnp.concatenate(halves(occupation[...] * share), axis=0)
    rows = lax.dot_general(
        weights,
        (result * result).astype(BF16),
        (((1,), (1,)), ((), ())),
        preferred_element_type=F32,
    )
    density[...] = rows[:1] + rows[1:]


def call(kernel, outs, scratch, *args, hbm=0, megabytes=32, order=()):
    vmem = pl.BlockSpec(memory_space=pltpu.VMEM)
    far = pl.BlockSpec(memory_space=pltpu.HBM)
    inputs = len(args)
    order = list(order) + [i for i in range(inputs) if i not in order]
    where = [order.index(i) for i in range(inputs)]

    def ordered(*refs):
        kernel(*(refs[i] for i in where), *refs[inputs:])

    return pl.pallas_call(
        ordered,
        out_shape=[pltpu.VMEM(s, t) for s, t in outs],
        in_specs=[far] * hbm + [vmem] * (inputs - hbm),
        out_specs=[vmem] * len(outs),
        scratch_shapes=scratch,
        compiler_params=pltpu.CompilerParams(vmem_limit_bytes=megabytes * 1024 * 1024),
    )(*(args[i] for i in order))


def body(filter_input, cell_table, cell_type, atom_center, proj_values, coupling, occupation):
    cells = cell_type.shape[0]
    atoms, projectors = proj_values.shape[0], proj_values.shape[2]
    rows, states = filter_input.shape
    z = Sizes(rows, cells, cell_table.shape[1], atoms, projectors)
    c, n = z.coef, z.nodes
    devices, groups = lax.axis_size("cells"), lax.axis_size("states")

    def exchanged(array, even_by):
        pairs = [
            (i, (i + (even_by if i % 2 == 0 else -even_by)) % devices) for i in range(devices)
        ]
        return lax.ppermute(array, "cells", pairs)

    def exchange_all(near, over, far, farther):
        far = exchanged(far, -2)
        near = exchanged(near, 1)
        farther = exchanged(farther, 2)
        over = exchanged(over, -1)
        return near, over, far, farther

    half_width = (upper_edge - lower_edge) / 2.0
    scale = half_width / (ground_edge - CENTRE)
    twice_inverse = 2.0 / scale
    gains, backs = [scale / half_width], [0.0]
    for _ in range(STEPS - 1):
        scale_next = 1.0 / (twice_inverse - scale)
        gains.append(2.0 * scale_next / half_width)
        backs.append(scale * scale_next)
        scale = scale_next

    field, share = ((rows, states), F32), ((c, states), F32)
    scratch = pltpu.VMEM(*field)
    x0, near, over, own0, own1 = call(
        functools.partial(pack_kernel, z),
        [((rows, states), BF16)]
        + [((z.first, states), BF16)] * 2
        + [((c, n), BF16)] * 2,
        [
            pltpu.SMEM(atom_center.shape, jnp.int32),
            pltpu.VMEM(proj_values.shape, BF16),
            scratch,
            pltpu.SemaphoreType.DMA((3,)),
        ],
        atom_center, filter_input, proj_values,
        hbm=3,
        megabytes=56,
    )
    from_over, from_near = exchanged(over, -1), exchanged(near, 1)

    onehot = (cell_type[:, None] == jnp.arange(cell_table.shape[0])[None, :]).astype(BF16)
    matrices = jnp.einsum("ct,tij->cij", onehot, cell_table, preferred_element_type=F32)
    matrices = matrices.astype(BF16)
    cell0, cell1 = matrices[0], matrices[-1]
    base, mix, end_rows, outer, own_share = call(
        functools.partial(beside_first, z),
        [field, ((2 * c, 4 * c), BF16), ((z.pad_face, n), BF16), ((2 * c, z.halo), BF16), share],
        [scratch],
        coupling, x0, cell0, cell1, near, over, own0, own1,
    )

    coeffs = ((3 * c, states), F32)
    second_messages = [((n, states), BF16) for n in z.second.values()]
    third_messages = [((z.later, states), BF16)] * 2 + [((c, states), BF16)] * 2
    faces, pad = pltpu.VMEM((2, z.pad_face, states), F32), pltpu.VMEM((2, z.span, states), F32)
    part1, own_coeffs, near, over, far, farther, rows0, rows1 = (
        call(
            functools.partial(first_kernel, z, gains[0]),
            [field, coeffs]
            + second_messages
            + [((2 * c, n), BF16)] * 2,
            [scratch, scratch, faces] + [pltpu.VMEM((n, 2 * c), BF16)] * 2,
            base, x0, own0, own1, own_share, outer, from_near, from_over, mix,
            order=FIRST_ORDER,
        )
    )
    second = exchange_all(near, over, far, farther)
    base, spread0, spread1, inner0, inner1 = call(
        functools.partial(beside_second, z, gains[1], backs[1]),
        [field] + [((n, 4 * c), BF16)] * 4,
        [],
        part1, x0, cell0, cell1, rows0, rows1, mix,
    )
    part2, own_coeffs, near, over, far, farther = call(
        functools.partial(second_kernel, z, gains[1]),
        [field, coeffs] + third_messages,
        [faces, pad],
        base, own_coeffs, *second,
        cell0, cell1, end_rows, rows0, rows1, inner0, inner1,
        order=ORDER,
    )
    third = exchange_all(near, over, far, farther)
    (base,) = call(
        functools.partial(beside_third, z, gains[2], backs[2]),
        [field],
        [],
        part2, part1, second[0], second[1], cell0, cell1,
    )
    filtered, density = call(
        functools.partial(third_kernel, z, gains[2], 1.0 / (states * groups)),
        [field, ((1, rows), F32)],
        [pad, pad],
        base, own_coeffs, *third,
        cell0, cell1, spread0, spread1, part2, occupation[None, :],
        order=ORDER,
    )
    return filtered, total(density, groups)[0]


def total(density, groups):
    if groups & (groups - 1):
        return lax.psum(density, "states")

    def partner(array, by):
        return lax.ppermute(array, "states", [(i, i ^ by) for i in range(groups)])

    if groups <= 4:
        return sum((partner(density, by) for by in range(1, groups)), density)
    step = 1
    while step < groups:
        density += partner(density, step)
        step *= 2
    return density


def solution(mesh):
    in_specs = (
        P("cells", "states"),
        P(),
        P("cells"),
        P("cells"),
        P("cells", None, None, None),
        P(),
        P("states"),
    )
    out_specs = (P("cells", "states"), P("cells"))
    return jax.shard_map(body, mesh=mesh, in_specs=in_specs, out_specs=out_specs, check_vma=False)
```

```python
import functools

import jax
import jax.numpy as jnp
from jax import lax
from jax.experimental import pallas as pl
from jax.experimental.pallas import tpu as pltpu
from jax.sharding import PartitionSpec as P

STEPS = 3
LANES = 128
ROWS16 = 16

lower_edge = 4.0
upper_edge = 12.0
ground_edge = -2.0

F32 = jnp.float32
BF16 = jnp.bfloat16


def up16(n):
    return -(-n // ROWS16) * ROWS16


def down16(n):
    return n // ROWS16 * ROWS16


class Sizes:
    def __init__(self, node_rows, cells, cell_nodes, atoms, projectors):
        self.rows = node_rows
        self.nodes = cell_nodes
        self.stride = (node_rows - cell_nodes) // (cells - 1)
        self.face = cell_nodes - self.stride
        self.last = node_rows - cell_nodes
        self.end = node_rows - self.face
        self.atoms = atoms
        self.proj = projectors
        self.coef = atoms * projectors
        self.chunks = -(-cell_nodes // LANES)
        self.tail = cell_nodes - (self.chunks - 1) * LANES
        self.shift = self.stride - (self.chunks - 1) * LANES
        self.m_coef = self.chunks * self.coef
        self.m_rows = self.m_coef + self.coef
        self.right_lo, self.right_hi = down16(self.last), up16(self.end)
        self.left_lo, self.left_hi = down16(self.face), up16(cell_nodes)
        self.halo = max(self.right_hi - self.right_lo, self.left_hi - self.left_lo)
        self.first = self.m_rows + self.halo
        self.pad_face = up16(self.face)
        self.span = up16(self.shift + self.face)
        self.l_face = 2 * self.coef
        self.l_term = self.l_face + self.pad_face
        self.l_block = self.l_term + self.pad_face
        self.later = self.l_block + self.pad_face
        self.second = {
            "near": self.l_term + 2 * ROWS16,
            "over": self.l_term,
            "far": self.coef,
            "farther": self.l_term + ROWS16,
        }


def dot(a, b):
    return jnp.dot(a, b, preferred_element_type=F32)


def exact_dot(a, b):
    return jnp.dot(a, b, preferred_element_type=F32, precision=lax.Precision.HIGHEST)


def halves(v):
    high = v.astype(BF16)
    return high, (v - high.astype(F32)).astype(BF16)


def is_even():
    return lax.rem(lax.axis_index("cells"), 2) == 0


def put(near, over, at, to_right, to_left):
    even = is_even()
    near[at] = jnp.where(even, to_right, to_left)
    over[at] = jnp.where(even, to_left, to_right)


def take(near, over, at):
    even = is_even()
    a, b = near[at], over[at]
    return jnp.where(even, b, a), jnp.where(even, a, b)


def pack_kernel(
    z, center_hbm, x0_hbm, proj_hbm, x0, near, over, own0, own1, coeffs, center, proj, xs, sems
):
    copies = [
        pltpu.make_async_copy(proj_hbm, proj, sems.at[0]),
        pltpu.make_async_copy(center_hbm, center, sems.at[1]),
        pltpu.make_async_copy(x0_hbm, x0, sems.at[2]),
    ]
    for copy in copies:
        copy.start()
    copies[0].wait()
    copies[1].wait()
    on0, on1, reach_left, reach_right = [], [], [], []
    for a in range(z.atoms):
        low = center[a] == 0
        before, here, after = proj[a, 0], proj[a, 1], proj[a, 2]
        none = jnp.zeros_like(before)
        on0.append(jnp.where(low, here, before))
        on1.append(jnp.where(low, after, here))
        reach_left.append(jnp.where(low, before, none))
        reach_right.append(jnp.where(low, none, after))
    on0, on1, reach_left, reach_right = (
        jnp.concatenate(v, axis=0) for v in (on0, on1, reach_left, reach_right)
    )
    k_last = (z.chunks - 1) * LANES

    def last_chunk(v):
        zeros = jnp.zeros((z.coef, LANES - z.tail), BF16)
        return jnp.concatenate([v[:, k_last:], zeros], axis=1).astype(F32)

    lane = lax.broadcasted_iota(jnp.int32, (z.coef, LANES), 1)
    on_first = lane < z.face
    on_last = (lane >= z.shift) & (lane < z.shift + z.face)

    def to_last(v):
        return pltpu.roll(jnp.where(on_first, v, 0.0), z.shift, 1)

    def to_first(v):
        return pltpu.roll(jnp.where(on_last, v, 0.0), LANES - z.shift, 1)

    own_first, own_last = on0[:, :LANES].astype(F32), last_chunk(on1)
    far_first, far_last = reach_right[:, :LANES].astype(F32), last_chunk(reach_left)
    own0[:, :LANES] = (own_first + to_first(far_last)).astype(BF16)
    own0[:, LANES:] = on0[:, LANES:]
    own1[:, :k_last] = on1[:, :k_last]
    own1[:, k_last:] = (own_last + to_last(far_first)).astype(BF16)[:, : z.tail]
    for k in range(z.chunks):
        cols = slice(k * LANES, (k + 1) * LANES)
        to_right, to_left = reach_right[:, cols], reach_left[:, cols]
        if k == z.chunks - 1:
            to_right = last_chunk(reach_right).astype(BF16)
            to_left = (far_last + to_last(own_first)).astype(BF16)
        if k == 0:
            to_right = (far_first + to_first(own_last)).astype(BF16)
        put(near, over, (slice(k * z.coef, (k + 1) * z.coef), slice(None)), to_right, to_left)
    copies[2].wait()
    xs[...] = x0[...].astype(F32)
    put(
        near, over, (slice(z.m_rows, z.first), slice(None)),
        x0[z.right_lo : z.right_lo + z.halo, :], x0[z.left_lo : z.left_lo + z.halo, :],
    )
    row = lax.broadcasted_iota(jnp.int32, (z.nodes, 1), 0)
    x_first, x_last = xs[: z.nodes, :], xs[z.last :, :]
    states = x0.shape[1]
    x_first = jnp.concatenate([x_first, jnp.where(row < z.face, 0.0, x_first)], axis=1)
    x_last = jnp.concatenate([x_last, jnp.where(row >= z.stride, 0.0, x_last)], axis=1)
    on_first = dot(own0[...], x_first.astype(BF16))
    on_last = dot(own1[...], x_last.astype(BF16))
    first, inner_first = on_first[:, :states], on_first[:, states:]
    last, inner_last = on_last[:, :states], on_last[:, states:]
    coeffs[...] = first + last
    put(
        near, over, (slice(z.m_coef, z.m_rows), slice(None)),
        (first + inner_last).astype(BF16), (inner_first + last).astype(BF16),
    )


def add_cells(z, term0, term1, out):
    out[: z.nodes, :] += term0
    out[z.last :, :] += term1


def face_scale(z):
    row = lax.broadcasted_iota(jnp.int32, (z.rows, 1), 0)
    return jnp.where((row < z.face) | (row >= z.end), 0.5, 1.0).astype(F32)


CENTRE = (upper_edge + lower_edge) / 2.0

FIRST_ORDER = (6, 7)
ORDER = (3, 2, 5, 4)


def twice(a, b):
    return jnp.concatenate([a, b, a, b], axis=0).astype(BF16)


def send_part(z, rows0, rows1, part, coeffs, near, over, far, farther, faces):
    c = z.coef
    faces[...] = jnp.zeros_like(faces)
    faces[0, : z.face, :] = part[: z.face, :]
    faces[1, : z.face, :] = part[z.end :, :]
    put(
        near, over, (slice(z.l_face, z.l_term), slice(None)),
        faces[1].astype(BF16), faces[0].astype(BF16),
    )
    on0, on1 = part[: z.nodes, :].astype(BF16), part[z.last :, :].astype(BF16)
    s0, s1 = dot(rows0[...], on0), dot(rows1[...], on1)
    before, own, after = s0[c:], s0[:c] + s1[:c], s1[c:]
    coeffs[:c, :] = before
    coeffs[c : 2 * c, :] = own
    coeffs[2 * c :, :] = after
    before, own, after = before.astype(BF16), own.astype(BF16), after.astype(BF16)
    near[:c, :] = own
    over[:c, :] = own
    put(near, over, (slice(c, 2 * c), slice(None)), after, before)
    even = is_even()
    far[:c, :] = jnp.where(even, before, after)
    farther[:c, :] = jnp.where(even, after, before)
    return on0, on1


def whole_coeffs(z, own_ref, near, over, far, farther):
    c = z.coef
    left, right = (v.astype(F32) for v in take(near, over, (slice(0, 2 * c), slice(None))))
    even = is_even()
    a, b = far[:c, :], farther[:c, :]
    far_left, far_right = jnp.where(even, b, a), jnp.where(even, a, b)
    before = own_ref[:c, :] + left[:c] + far_left.astype(F32)
    own = own_ref[c : 2 * c, :] + left[c:] + right[c:]
    after = own_ref[2 * c :, :] + right[:c] + far_right.astype(F32)
    return before, own, after


def face_rows(z, near, over):
    first, last = take(near, over, (slice(z.l_face, z.l_term), slice(None)))
    return first.astype(F32)[: z.face], last.astype(F32)[: z.face]


def at_last(z, rows, pad):
    pad[...] = jnp.zeros_like(pad)
    pad[z.shift : z.shift + z.face, :] = rows
    return pad[...].astype(BF16)


def neighbour_terms(z, s, faces, cell0, cell1, spread0, spread1, pad):
    before, own, after = s
    first, last = faces
    k_last = (z.chunks - 1) * LANES
    pad[0, : z.face, :] = first
    pad[0, z.face :, :] = jnp.zeros((z.span - z.face, first.shape[1]), F32)
    first = pad[0].astype(BF16)[: z.pad_face]
    last = at_last(z, last, pad.at[1])[: z.tail]
    term0 = dot(spread0[...], twice(own, before)) + dot(cell0[:, : z.pad_face], first)
    term1 = dot(spread1[...], twice(own, after)) + dot(cell1[:, k_last:], last)
    return term0, term1


def beside_first(
    z, gain, coupling, x0, cell0, cell1, mine_near, mine_over, base, mix, end_rows, outer, xs
):
    xs[...] = x0[...].astype(F32)
    base[...] = (-CENTRE * gain) * (face_scale(z) * xs[...])
    add_cells(
        z,
        gain * dot(cell0[...], x0[: z.nodes, :]),
        gain * dot(cell1[...], xs[z.last :, :].astype(BF16)),
        base,
    )
    size = 2 * z.coef
    row = lax.broadcasted_iota(jnp.int32, (size, z.proj), 0)
    col = lax.broadcasted_iota(jnp.int32, (size, z.proj), 1)
    pick = jnp.where(lax.rem(row, z.proj) == col, 1.0, 0.0).astype(F32)
    wide = exact_dot(pick, coupling[...])
    wide = lax.dot_general(
        wide, pick, (((1,), (1,)), ((), ())),
        preferred_element_type=F32, precision=lax.Precision.HIGHEST,
    )
    row = lax.broadcasted_iota(jnp.int32, (size, size), 0)
    col = lax.broadcasted_iota(jnp.int32, (size, size), 1)
    wide = jnp.where(lax.div(row, z.proj) == lax.div(col, z.proj), wide, 0.0)
    mix[...] = jnp.concatenate(halves(wide), axis=1)
    node = lax.broadcasted_iota(jnp.int32, (LANES, z.halo), 0)
    place = lax.broadcasted_iota(jnp.int32, (LANES, z.halo), 1)
    left, right = jnp.zeros((z.coef, z.halo), F32), jnp.zeros((z.coef, z.halo), F32)
    for k in range(z.chunks):
        rows = (slice(k * z.coef, (k + 1) * z.coef), slice(None))
        to_left, to_right = take(mine_near, mine_over, rows)
        at = node + k * LANES
        low = (place == at + (z.last - z.right_lo)) & (at < z.stride)
        high = (place == at - z.left_lo) & (at >= z.face) & (at < z.nodes)
        left += dot(to_left, jnp.where(low, 1.0, 0.0).astype(BF16))
        right += dot(to_right, jnp.where(high, 1.0, 0.0).astype(BF16))
    outer[: z.coef, :] = left.astype(BF16)
    outer[z.coef :, :] = right.astype(BF16)
    end_rows[...] = jnp.zeros_like(end_rows)
    end_rows[: z.face, :] = cell1[...].astype(F32)[z.stride :].astype(BF16)


def mixed(a, mix):
    width = a.shape[1]
    product = dot(a, mix[...])
    return jnp.concatenate(halves(product[:, :width] + product[:, width:]), axis=1)


def leave_out(z, spread0, spread1):
    start = down16(z.stride)
    for ref, rows in ((spread0, slice(0, z.pad_face)), (spread1, slice(start, z.nodes))):
        part = ref[rows, :].astype(F32)
        node = lax.broadcasted_iota(jnp.int32, part.shape, 0) + rows.start
        lane = lax.broadcasted_iota(jnp.int32, part.shape, 1)
        face = (node < z.face) if rows.start == 0 else (node >= z.stride)
        shared = face & (lax.rem(lane, 2 * z.coef) >= z.coef)
        ref[rows, :] = jnp.where(shared, 0.0, part).astype(BF16)


def first_kernel(
    z, gain,
    base, x0, own0, own1, own_coeffs, outer, from_near, from_over, mix,
    part, coeffs, near, over, far, farther,
    rows0, rows1,
    xs, faces, flat0, flat1,
):
    c = z.coef
    xs[z.right_lo :, :] = x0[z.right_lo :, :].astype(F32)
    rows0[:c, :] = own0[...]
    rows1[:c, :] = own1[...]
    for k in range(z.chunks):
        width = LANES if k < z.chunks - 1 else z.tail
        cols = slice(k * LANES, k * LANES + width)
        rows0[c:, cols], rows1[c:, cols] = take(
            from_near, from_over, (slice(k * c, (k + 1) * c), slice(0, width))
        )
    flat0[...], flat1[...] = rows0[...].T, rows1[...].T
    leave_out(z, flat0, flat1)
    left, right = take(from_near, from_over, (slice(z.m_rows, z.first), slice(None)))
    own = own_coeffs[...] + dot(outer[:c, :], left) + dot(outer[c:, :], right)
    before, after = take(from_near, from_over, (slice(z.m_coef, z.m_rows), slice(None)))
    before = before.astype(F32) + dot(rows0[c:, :], x0[: z.nodes, :])
    after = after.astype(F32) + dot(rows1[c:, :], xs[z.last :, :].astype(BF16))
    high, low = halves(jnp.concatenate([before, own, after], axis=1))
    mix_high, mix_low = mix[:c, :c], mix[:c, 2 * c : 3 * c]
    weighted = dot(mix_high, high) + dot(mix_high, low) + dot(mix_low, high)
    weighted = weighted.astype(BF16)
    n = before.shape[1]
    before, own, after = (weighted[:, i * n : (i + 1) * n] for i in range(3))
    part[...] = base[...]
    add_cells(
        z,
        gain * dot(flat0[...], jnp.concatenate([own, before], axis=0)),
        gain * dot(flat1[...], jnp.concatenate([own, after], axis=0)),
        part,
    )
    send_part(z, rows0, rows1, part, coeffs, near, over, far, farther, faces)
    for message, used in ((near, z.l_term), (over, z.l_term), (far, c), (farther, c)):
        if message.shape[0] > used:
            message[used:, :] = jnp.zeros((message.shape[0] - used, message.shape[1]), BF16)


def beside_second(z, gain, back, part, x0, cell0, cell1, rows0, rows1, mix,
                  base, spread0, spread1, inner0, inner1):
    scale = face_scale(z)
    base[...] = scale * ((-CENTRE * gain) * part[...] - back * x0[...].astype(F32))
    add_cells(
        z,
        gain * dot(cell0[...], part[: z.nodes, :].astype(BF16)),
        gain * dot(cell1[...], part[z.last :, :].astype(BF16)),
        base,
    )
    spread0[...] = mixed(rows0[...].T, mix)
    spread1[...] = mixed(rows1[...].T, mix)
    inner0[...], inner1[...] = spread0[...], spread1[...]
    leave_out(z, inner0, inner1)


def second_kernel(
    z, gain,
    base, own_coeffs, from_near, from_over, from_far, from_farther,
    cell0, cell1, end_rows, rows0, rows1, inner0, inner1,
    part, coeffs, near, over, far, farther,
    edges, pad,
):
    s = whole_coeffs(z, own_coeffs, from_near, from_over, from_far, from_farther)
    first, last = face_rows(z, from_near, from_over)
    term0, term1 = neighbour_terms(z, s, (first, last), cell0, cell1, inner0, inner1, pad)
    part[...] = base[...]
    add_cells(z, gain * term0, gain * term1, part)
    part[: z.face, :] -= (0.5 * CENTRE * gain) * first
    part[z.end :, :] -= (0.5 * CENTRE * gain) * last
    on0, on1 = send_part(z, rows0, rows1, part, coeffs, near, over, far, farther, edges)
    put(
        near, over, (slice(z.l_term, z.l_block), slice(None)),
        dot(end_rows[...], on1).astype(BF16), dot(cell0[: z.pad_face, :], on0).astype(BF16),
    )
    k_last = (z.chunks - 1) * LANES
    wide = jnp.zeros((z.pad_face, LANES - z.tail), BF16)
    put(
        near, over, (slice(z.l_block, z.later), slice(None)),
        jnp.concatenate([end_rows[:, k_last:], wide], axis=1), cell0[: z.pad_face, :LANES],
    )


def beside_third(z, gain, back, part, earlier, from_near, from_over, cell0, cell1, base):
    base[...] = (-CENTRE * gain) * part[...] - back * earlier[...]
    add_cells(
        z,
        gain * dot(cell0[...], part[: z.nodes, :].astype(BF16)),
        gain * dot(cell1[...], part[z.last :, :].astype(BF16)),
        base,
    )
    first, last = face_rows(z, from_near, from_over)
    base[: z.face, :] -= back * first
    base[z.end :, :] -= back * last


def third_kernel(
    z, gain, share,
    base, own_coeffs, from_near, from_over, from_far, from_farther,
    cell0, cell1, spread0, spread1, part, occupation,
    out, density,
    pad, mine,
):
    s = whole_coeffs(z, own_coeffs, from_near, from_over, from_far, from_farther)
    first, last = face_rows(z, from_near, from_over)
    term0, term1 = neighbour_terms(z, s, (first, last), cell0, cell1, spread0, spread1, pad)
    out[...] = base[...]
    add_cells(z, gain * term0, gain * term1, out)
    terms = take(from_near, from_over, (slice(z.l_term, z.l_block), slice(None)))
    blocks = take(from_near, from_over, (slice(z.l_block, z.later), slice(None)))
    own_first = at_last(z, part[: z.face, :], mine.at[0])
    mine[1, : z.face, :] = part[z.end :, :]
    mine[1, z.face :, :] = jnp.zeros((z.span - z.face, part.shape[1]), F32)
    own_last = mine[1].astype(BF16)[: z.pad_face]
    left = (terms[0].astype(F32) + dot(blocks[0][:, : z.span], own_first))[: z.face]
    right = (terms[1].astype(F32) + dot(blocks[1][:, : z.pad_face], own_last))[: z.face]
    out[: z.face, :] += gain * (left - CENTRE * first)
    out[z.end :, :] += gain * (right - CENTRE * last)
    result = out[...]
    weights = jnp.concatenate(halves(occupation[...] * share), axis=0)
    rows = lax.dot_general(
        weights,
        (result * result).astype(BF16),
        (((1,), (1,)), ((), ())),
        preferred_element_type=F32,
    )
    density[...] = rows[:1] + rows[1:]


def call(kernel, outs, scratch, *args, hbm=0, megabytes=32, order=()):
    vmem = pl.BlockSpec(memory_space=pltpu.VMEM)
    far = pl.BlockSpec(memory_space=pltpu.HBM)
    inputs = len(args)
    order = list(order) + [i for i in range(inputs) if i not in order]
    where = [order.index(i) for i in range(inputs)]

    def ordered(*refs):
        kernel(*(refs[i] for i in where), *refs[inputs:])

    return pl.pallas_call(
        ordered,
        out_shape=[pltpu.VMEM(s, t) for s, t in outs],
        in_specs=[far] * hbm + [vmem] * (inputs - hbm),
        out_specs=[vmem] * len(outs),
        scratch_shapes=scratch,
        compiler_params=pltpu.CompilerParams(vmem_limit_bytes=megabytes * 1024 * 1024),
    )(*(args[i] for i in order))


def body(filter_input, cell_table, cell_type, atom_center, proj_values, coupling, occupation):
    cells = cell_type.shape[0]
    atoms, projectors = proj_values.shape[0], proj_values.shape[2]
    rows, states = filter_input.shape
    z = Sizes(rows, cells, cell_table.shape[1], atoms, projectors)
    c, n = z.coef, z.nodes
    devices, groups = lax.axis_size("cells"), lax.axis_size("states")

    def exchanged(array, even_by):
        pairs = [
            (i, (i + (even_by if i % 2 == 0 else -even_by)) % devices) for i in range(devices)
        ]
        return lax.ppermute(array, "cells", pairs)

    def exchange_all(near, over, far, farther):
        far = exchanged(far, -2)
        near = exchanged(near, 1)
        farther = exchanged(farther, 2)
        over = exchanged(over, -1)
        return near, over, far, farther

    half_width = (upper_edge - lower_edge) / 2.0
    scale = half_width / (ground_edge - CENTRE)
    twice_inverse = 2.0 / scale
    gains, backs = [scale / half_width], [0.0]
    for _ in range(STEPS - 1):
        scale_next = 1.0 / (twice_inverse - scale)
        gains.append(2.0 * scale_next / half_width)
        backs.append(scale * scale_next)
        scale = scale_next

    field, share = ((rows, states), F32), ((c, states), F32)
    scratch = pltpu.VMEM(*field)
    x0, near, over, own0, own1, own_share = call(
        functools.partial(pack_kernel, z),
        [((rows, states), BF16)]
        + [((z.first, states), BF16)] * 2
        + [((c, n), BF16)] * 2
        + [share],
        [
            pltpu.SMEM(atom_center.shape, jnp.int32),
            pltpu.VMEM(proj_values.shape, BF16),
            scratch,
            pltpu.SemaphoreType.DMA((3,)),
        ],
        atom_center, filter_input, proj_values,
        hbm=3,
        megabytes=56,
    )
    from_over, from_near = exchanged(over, -1), exchanged(near, 1)

    onehot = (cell_type[:, None] == jnp.arange(cell_table.shape[0])[None, :]).astype(BF16)
    matrices = jnp.einsum("ct,tij->cij", onehot, cell_table, preferred_element_type=F32)
    matrices = matrices.astype(BF16)
    cell0, cell1 = matrices[0], matrices[-1]
    base, mix, end_rows, outer = call(
        functools.partial(beside_first, z, gains[0]),
        [field, ((2 * c, 4 * c), BF16), ((z.pad_face, n), BF16), ((2 * c, z.halo), BF16)],
        [scratch],
        coupling, x0, cell0, cell1, near, over,
    )

    coeffs = ((3 * c, states), F32)
    second_messages = [((n, states), BF16) for n in z.second.values()]
    third_messages = [((z.later, states), BF16)] * 2 + [((c, states), BF16)] * 2
    faces, pad = pltpu.VMEM((2, z.pad_face, states), F32), pltpu.VMEM((2, z.span, states), F32)
    part1, own_coeffs, near, over, far, farther, rows0, rows1 = (
        call(
            functools.partial(first_kernel, z, gains[0]),
            [field, coeffs]
            + second_messages
            + [((2 * c, n), BF16)] * 2,
            [scratch, faces] + [pltpu.VMEM((n, 2 * c), BF16)] * 2,
            base, x0, own0, own1, own_share, outer, from_near, from_over, mix,
            order=FIRST_ORDER,
        )
    )
    second = exchange_all(near, over, far, farther)
    base, spread0, spread1, inner0, inner1 = call(
        functools.partial(beside_second, z, gains[1], backs[1]),
        [field] + [((n, 4 * c), BF16)] * 4,
        [],
        part1, x0, cell0, cell1, rows0, rows1, mix,
    )
    part2, own_coeffs, near, over, far, farther = call(
        functools.partial(second_kernel, z, gains[1]),
        [field, coeffs] + third_messages,
        [faces, pad],
        base, own_coeffs, *second,
        cell0, cell1, end_rows, rows0, rows1, inner0, inner1,
        order=ORDER,
    )
    third = exchange_all(near, over, far, farther)
    (base,) = call(
        functools.partial(beside_third, z, gains[2], backs[2]),
        [field],
        [],
        part2, part1, second[0], second[1], cell0, cell1,
    )
    filtered, density = call(
        functools.partial(third_kernel, z, gains[2], 1.0 / (states * groups)),
        [field, ((1, rows), F32)],
        [pad, pad],
        base, own_coeffs, *third,
        cell0, cell1, spread0, spread1, part2, occupation[None, :],
        order=ORDER,
    )
    return filtered, total(density, groups)[0]


def total(density, groups):
    if groups & (groups - 1):
        return lax.psum(density, "states")

    def partner(array, by):
        return lax.ppermute(array, "states", [(i, i ^ by) for i in range(groups)])

    if groups <= 4:
        return sum((partner(density, by) for by in range(1, groups)), density)
    step = 1
    while step < groups:
        density += partner(density, step)
        step *= 2
    return density


def solution(mesh):
    in_specs = (
        P("cells", "states"),
        P(),
        P("cells"),
        P("cells"),
        P("cells", None, None, None),
        P(),
        P("states"),
    )
    out_specs = (P("cells", "states"), P("cells"))
    return jax.shard_map(body, mesh=mesh, in_specs=in_specs, out_specs=out_specs, check_vma=False)
```
